256 devices in a mesh: graph: 32 (over z, x), fsdp: 4 (over y), replica: 2 (over core).
Axes of the slice: x: 4, y: 4, z: 8, core: 2. Of those that a mesh axis runs over, the one named last changes fastest.
Arguments:
- states: bfloat16 [16384, 512], P('graph'), may hold values from -6 to 6
- weights: bfloat16 [5, 512, 512], P(None, 'fsdp'), may hold values from -0.25 to 0.25
- edge_tiles: bfloat16 [32, 4, 2, 48, 128, 128], P('graph', 'fsdp', 'replica'), may hold values from 0 to 0.26516504, as said below
- edge_owner: int32 [32, 4, 2, 48], P(None, 'fsdp', 'replica'), may hold values from 0 to 31, as said below
- edge_source: int32 [32, 4, 2, 48], P(None, 'fsdp', 'replica'), may hold values from 0 to 3
- edge_target: int32 [32, 4, 2, 48], P(None, 'fsdp', 'replica'), may hold values from 0 to 3
- edge_relation: int32 [32, 4, 2, 48], P(None, 'fsdp', 'replica'), may hold values from 0 to 3
- edge_count: int32 [32, 4, 2], P(None, 'fsdp', 'replica'), may hold values from 36 to 48, as said below
- cotangent: bfloat16 [16384, 512], P('graph'), may hold values from -6 to 6
Outputs:
- layer_output: float32 [16384, 512], P(('graph', 'fsdp', 'replica'))
- grad_states: float32 [16384, 512], P(('graph', 'fsdp', 'replica'))
- grad_weights: float32 [5, 512, 512], P(None, ('fsdp', 'replica'))
The draws below stay inside these ranges and needn't reach their ends.
Inputs may be any that keep to these rules, and one draw needn't show every extreme that they name: `edge_owner`: among the live slots of one device at most 2 name the same owner group; the device with all 48 slots live names some owner group exactly 2 times. `edge_count`: live slots come first in each device's list; some device has all 48 live. `edge_tiles`: nonnegative edge weights; about a quarter of each tile's entries are nonzero.
All inputs are finite; a program needn't handle non-finite values.
Results may differ from the reference program's by a relative error of at most 0.0085.
Values may be sent and summed in bfloat16 or wider, within the bound.
A program may use at most 128 MiB of HBM per device.

```python
import jax
import jax.numpy as jnp
from jax import lax

D = 512
REL = 4
TILE = 128
ENT_DEV = 512
EB = 48
CAP = 2
ENTITIES = 16384
N_GRAPH = 32
N_FSDP = 4
N_REPLICA = 2


def draw_edge_tiles(key, part):
    key = jax.random.fold_in(key, 11)
    first, second = jax.random.split(key, 2)
    shape = (N_GRAPH, N_FSDP, N_REPLICA, EB, TILE, TILE)
    links = jax.random.bernoulli(first, 0.25, shape).astype(jnp.float32)
    values = jax.random.uniform(second, shape, jnp.float32, 0.5, 1.5)
    return (links * values * (0.4 / TILE ** 0.5)).astype(jnp.bfloat16)


def draw_edge_owner(key, part):
    key = jax.random.fold_in(key, 5)
    devices_all = N_GRAPH * N_FSDP * N_REPLICA
    several = jax.random.split(key, devices_all)

    def one_device(device_key):
        first, second, third = jax.random.split(device_key, 3)
        forced = jax.random.randint(first, (), 0, N_GRAPH)
        slots = jax.random.permutation(second, N_GRAPH * CAP) // CAP
        order = jnp.argsort((slots != forced).astype(jnp.int32), stable=True)
        chosen = slots[order][:EB]
        return jax.random.permutation(third, chosen)
    owners = jax.vmap(one_device)(several)
    return owners.reshape(N_GRAPH, N_FSDP, N_REPLICA, EB).astype(jnp.int32)


def draw_edge_count(key, part):
    key = jax.random.fold_in(key, 7)
    first, second, third = jax.random.split(key, 3)
    devices_all = N_GRAPH * N_FSDP * N_REPLICA
    base = 3 * EB // 4
    span = EB - base
    upper = jax.random.randint(first, (devices_all,), 0, span + 1)
    lower = jax.random.randint(second, (devices_all,), 0, span + 1)
    counts = base + upper * lower // span
    fullest = jax.random.randint(third, (), 0, devices_all)
    counts = jnp.where(jnp.arange(devices_all) == fullest, EB, counts)
    return counts.reshape(N_GRAPH, N_FSDP, N_REPLICA).astype(jnp.int32)


def plant(values, own_key, least, high):
    shape = values.shape
    place = [jax.random.randint(jax.random.fold_in(own_key, axis), (), 0, shape[axis]) for axis in range(len(shape))]
    values = values.at[tuple(place)].set(least)
    longest = shape.index(max(shape))
    place[longest] = (place[longest] + 1) % shape[longest]
    return values.at[tuple(place)].set(high)


def level_of(own_key, dims, shards, least, top_value):
    def one(position, shards_of):
        steps = jax.random.uniform(jax.random.fold_in(jax.random.fold_in(own_key, 6), position), (shards_of,), jnp.float32, least / len(shards), top_value / len(shards))
        return jnp.repeat(jnp.exp(steps), dims[position] // shards_of).reshape((-1,) + (1,) * (len(dims) - position - 1))

    loudness = one(*shards[0])
    for cut in shards[1:]:
        loudness = loudness * one(*cut)
    return loudness


def bell_draw(key, dims, scale, limit, cuts=(), held_as=jnp.bfloat16):
    array = scale * jax.random.normal(key, dims, jnp.float32)
    if cuts:
        array = array * level_of(key, dims, cuts, -0.22, 0.18)
    return jnp.clip(array, -limit, limit).astype(held_as)


def setup_inputs(seed: int = 0) -> dict:
    keys = jax.random.split(jax.random.key(seed), 10)
    return {
        "states": bell_draw(keys[0], (ENTITIES, D), 1.0, 6.0, ((0, 32),)),
        "weights": bell_draw(keys[1], (REL + 1, D, D), D ** -0.5, 0.25, ((1, 4),)),
        "edge_tiles": draw_edge_tiles(jax.random.fold_in(keys[9], 71), 0),
        "edge_owner": draw_edge_owner(jax.random.fold_in(keys[9], 71), 0),
        "edge_source": plant(jax.random.randint(keys[4], (N_GRAPH, N_FSDP, N_REPLICA, EB), 0, ENT_DEV // TILE), jax.random.fold_in(keys[4], 1), 0, (ENT_DEV // TILE) - 1).astype(jnp.int32),
        "edge_target": plant(jax.random.randint(keys[5], (N_GRAPH, N_FSDP, N_REPLICA, EB), 0, ENT_DEV // TILE), jax.random.fold_in(keys[5], 1), 0, (ENT_DEV // TILE) - 1).astype(jnp.int32),
        "edge_relation": plant(jax.random.randint(keys[6], (N_GRAPH, N_FSDP, N_REPLICA, EB), 0, REL), jax.random.fold_in(keys[6], 1), 0, REL - 1).astype(jnp.int32),
        "edge_count": draw_edge_count(jax.random.fold_in(keys[9], 71), 0),
        "cotangent": bell_draw(keys[8], (ENTITIES, D), 1.0, 6.0, ((0, 32),)),
    }


def silu_slope(pre):
    sigma = jax.nn.sigmoid(pre)
    return sigma * (1.0 + pre * (1.0 - sigma))


def reference(states, weights, edge_tiles, edge_owner, edge_source, edge_target, edge_relation, edge_count, cotangent):
    blocks_per = ENT_DEV // TILE
    all_blocks = N_GRAPH * blocks_per
    devices_all = N_GRAPH * N_FSDP * N_REPLICA
    rel_weights = weights[:REL]
    self_weight = weights[REL]
    state_blocks = states.reshape(all_blocks, TILE, D)

    def transform_one(panel):
        return jnp.dot(states, panel, preferred_element_type=jnp.float32).astype(jnp.bfloat16)

    table = lax.map(transform_one, rel_weights).reshape(REL, all_blocks, TILE, D)
    tiles_flat = edge_tiles.reshape(devices_all, EB, TILE, TILE)
    owners = edge_owner.reshape(devices_all, EB).astype(jnp.int32)
    sources = edge_source.reshape(devices_all, EB).astype(jnp.int32)
    targets = edge_target.reshape(devices_all, EB).astype(jnp.int32)
    labels = edge_relation.reshape(devices_all, EB).astype(jnp.int32)
    positions = jnp.arange(EB, dtype=jnp.int32)
    active = positions[None, :] < edge_count.reshape(devices_all)[:, None]
    group_of = jnp.arange(devices_all, dtype=jnp.int32) // (N_FSDP * N_REPLICA)
    source_global = owners * blocks_per + sources
    target_global = group_of[:, None] * blocks_per + targets

    def forward_step(carry, packed):
        tiles_here, source_here, target_here, label_here, active_here = packed
        inputs = table[label_here, source_here]
        terms = jnp.einsum("enm,emd->end", tiles_here.astype(jnp.float32), inputs.astype(jnp.float32))
        terms = jnp.where(active_here[:, None, None], terms, jnp.zeros((), jnp.float32))
        return carry.at[target_here].add(terms), None

    messages, unused = lax.scan(forward_step, jnp.zeros((all_blocks, TILE, D), jnp.float32),
                                (tiles_flat, source_global, target_global, labels, active))
    pre = messages.reshape(N_GRAPH * ENT_DEV, D) + jnp.dot(states, self_weight, preferred_element_type=jnp.float32)
    layer_output = jax.nn.silu(pre)
    slope = (cotangent.astype(jnp.float32) * silu_slope(pre)).astype(jnp.bfloat16)
    slope_blocks = slope.reshape(all_blocks, TILE, D)

    def backward_step(carry, packed):
        tiles_here, source_here, target_here, label_here, active_here = packed
        upstream = slope_blocks[target_here]
        pulled = jnp.einsum("enm,end->emd", tiles_here.astype(jnp.float32), upstream.astype(jnp.float32))
        pulled = lax.optimization_barrier(pulled.astype(jnp.bfloat16)).astype(jnp.float32)
        pulled = jnp.where(active_here[:, None, None], pulled, jnp.zeros((), jnp.float32))
        return carry.at[source_here, label_here].add(pulled), None

    pair_sums, unused = lax.scan(backward_step, jnp.zeros((all_blocks, REL, TILE, D), jnp.float32),
                                 (tiles_flat, source_global, target_global, labels, active))
    pair_sums = pair_sums.astype(jnp.bfloat16)
    weight_grad = jnp.einsum("bnd,brne->rde", state_blocks.astype(jnp.float32), pair_sums.astype(jnp.float32))
    self_grad = jnp.dot(states.T, slope, preferred_element_type=jnp.float32)
    grad_weights = jnp.concatenate([weight_grad, self_grad[None]], axis=0)
    carried = jnp.einsum("brne,rde->bnd", pair_sums.astype(jnp.float32), rel_weights.astype(jnp.float32))
    grad_states = jnp.dot(slope, self_weight.T, preferred_element_type=jnp.float32) + carried.reshape(N_GRAPH * ENT_DEV, D)
    return layer_output, grad_states, grad_weights
```

```python
import jax
import jax.numpy as jnp
from jax import lax
from jax.experimental import pallas as pl
from jax.experimental.pallas import tpu as pltpu
from jax.sharding import PartitionSpec as P

D = 512
REL = 4
TILE = 128
EB = 48
NZ = 8
NX = 4
NY = 4
NC = 8
SLOTS = 8
ROWS = 64
WR = 160
WC = 128
BF = jnp.bfloat16
F32 = jnp.float32
MESH = pl.DeviceIdType.MESH
ANY = pl.BlockSpec(memory_space=pl.ANY)
VM = pl.BlockSpec(memory_space=pltpu.VMEM)
SM = pl.BlockSpec(memory_space=pltpu.SMEM)
DMA = pltpu.SemaphoreType.DMA


def params(collective=None):
    more = {} if collective is None else {"collective_id": collective, "has_side_effects": True}
    return pltpu.CompilerParams(vmem_limit_bytes=56 * 1024 * 1024, **more)


def place():
    g = lax.axis_index("graph")
    return g // NX, g % NX, lax.axis_index("fsdp"), lax.axis_index("replica")


def send(src, dst, ssem, rsem, z, x, y, p):
    return pltpu.make_async_remote_copy(
        src_ref=src,
        dst_ref=dst,
        send_sem=ssem,
        recv_sem=rsem,
        device_id=(z * NX + x, y, p),
        device_id_type=MESH,
    )


def greet(partners, swap=None):
    barrier = pltpu.get_barrier_semaphore()
    for z, x, y, p in partners:
        pl.semaphore_signal(barrier, inc=1, device_id=(z * NX + x, y, p), device_id_type=MESH)
    if swap is not None:
        (z, x, y, p), is_self = swap

        @pl.when(jnp.logical_not(is_self))
        def _():
            pl.semaphore_signal(barrier, inc=1, device_id=(z * NX + x, y, p), device_id_type=MESH)

        pl.semaphore_wait(barrier, len(partners) + jnp.where(is_self, 0, 1))
    else:
        pl.semaphore_wait(barrier, len(partners))


def group_peers(z, x, y, p):
    return [
        (z, x, (y + dy) % NY, (p + dp) % 2)
        for dy, dp in ((0, 1), (1, 0), (3, 0), (1, 1), (3, 1), (2, 0), (2, 1))
    ]


def x_peers(z, x, y, p):
    return [(z, (x + i) % NX, y, p) for i in (1, 2, 3)]


def z_peers(z, x, y, p, steps=(1, 7)):
    return [((z + i) % NZ, x, y, p) for i in steps]


def swap_of(z, x, y, p):
    return (2 * (z // 2) + p, y, x, z % 2), (x == y) & (z % 2 == p)


def pack_kernel(owner, source, target, relation, count, tiles, packed, meta, filled):
    g = lax.axis_index("graph")
    for c in range(NC):
        for s in range(SLOTS):
            meta[c, 0, s] = -1

    def clear(o, carry):
        filled[o] = 0
        return carry

    lax.fori_loop(0, NZ * NX, clear, 0)

    def put(e, carry):
        o = owner[g, e]
        rank = filled[o]
        filled[o] = rank + 1
        c = (o % NX) * 2 + (o // NX) % 2
        s = (o // 8) * 2 + rank
        meta[c, 0, s] = source[g, e] + 4 * target[g, e] + 16 * relation[g, e]
        packed[c, s] = tiles[e]
        return carry

    lax.fori_loop(0, count[g], put, 0)


def pack(owner, source, target, relation, count, tiles):
    return pl.pallas_call(
        pack_kernel,
        out_shape=(
            jax.ShapeDtypeStruct((NC, SLOTS, TILE, TILE), BF),
            jax.ShapeDtypeStruct((NC, 8, 128), jnp.int32),
        ),
        in_specs=[SM] * 5 + [VM],
        out_specs=(VM, SM),
        scratch_shapes=[pltpu.SMEM((NZ * NX,), jnp.int32)],
        compiler_params=params(),
    )(owner, source, target, relation, count, tiles)


def deal_kernel(
    packed, meta, states, tiles_o, meta_o, xp,
    own_sems, t_send, t_recv, m_send, m_recv, v_send, v_recv, x_send, x_recv, z_send, z_recv,
):
    z, x, y, p = place()
    peers = group_peers(z, x, y, p)
    xs = x_peers(z, x, y, p)
    up, down = z_peers(z, x, y, p)
    target, is_self = swap_of(z, x, y, p)
    greet(peers + xs + [up, down], (target, is_self))
    c = y * 2 + p
    piece = states.at[pl.ds(pl.multiple_of((p * NY + y) * ROWS, ROWS), ROWS)]

    @pl.when(jnp.logical_not(is_self))
    def _():
        send(piece, xp.at[target[0], target[1]], v_send, v_recv, *target).start()

    @pl.when(is_self)
    def _():
        pltpu.make_async_copy(piece, xp.at[z, x], own_sems.at[0]).start()

    mine = pltpu.make_async_copy(packed.at[c], tiles_o.at[c], own_sems.at[1])
    mine_meta = pltpu.make_async_copy(meta.at[c], meta_o.at[c], own_sems.at[2])
    mine.start()
    mine_meta.start()
    tile_copies = []
    for i, q in enumerate(peers):
        cq = q[2] * 2 + q[3]
        a = send(packed.at[cq], tiles_o.at[c], t_send.at[i], t_recv.at[i], *q)
        b = send(meta.at[cq], meta_o.at[c], m_send.at[i], m_recv.at[i], *q)
        a.start()
        b.start()
        tile_copies += [a, b]

    @pl.when(jnp.logical_not(is_self))
    def _():
        send(piece, xp.at[z, x], v_send, v_recv, *target).wait()

    @pl.when(is_self)
    def _():
        pltpu.make_async_copy(piece, xp.at[z, x], own_sems.at[0]).wait()

    x_copies = [
        send(xp.at[z, x], xp.at[z, x], x_send.at[i], x_recv.at[i], *q) for i, q in enumerate(xs)
    ]
    for a in x_copies:
        a.start()

    z_copies = {}
    for s in range(4):
        for i in range(NX):
            xi = (x + i) % NX
            if s == 0 and i > 0:
                x_copies[3 - i].wait_recv()
            for d, q in ((0, up), (1, down)):
                if s > 0 and (d, s - 1, i) in z_copies:
                    z_copies[d, s - 1, i].wait_recv()
                if s < 3 or (i < 2) == (d == 0):
                    zs = (z - s + NZ) % NZ if d == 0 else (z + s) % NZ
                    a = send(xp.at[zs, xi], xp.at[zs, xi], z_send.at[d, s, i], z_recv.at[d, s, i], *q)
                    a.start()
                    z_copies[d, s, i] = a
    for (d, s, i), a in z_copies.items():
        if s == 3:
            a.wait_recv()
    for a in x_copies + list(z_copies.values()):
        a.wait_send()
    mine.wait()
    mine_meta.wait()
    for a in tile_copies:
        a.wait()


def deal(packed, meta, states):
    return pl.pallas_call(
        deal_kernel,
        out_shape=(
            jax.ShapeDtypeStruct((NC, SLOTS, TILE, TILE), BF),
            jax.ShapeDtypeStruct((NC, 8, 128), jnp.int32),
            jax.ShapeDtypeStruct((NZ, NX, ROWS, D), BF),
        ),
        in_specs=[ANY] * 3,
        out_specs=(ANY, ANY, ANY),
        scratch_shapes=[
            DMA((3,)), DMA((7,)), DMA((7,)), DMA((7,)), DMA((7,)), DMA(()), DMA(()),
            DMA((3,)), DMA((3,)), DMA((2, 4, 4)), DMA((2, 4, 4)),
        ],
        compiler_params=params(0),
    )(packed, meta, states)


def forward_kernel(meta, tiles, xp, weights, t_out, m_out, acc):
    acc[...] = jnp.zeros_like(acc)

    def slot(i, carry):
        c = i // SLOTS
        s = i % SLOTS
        code = meta[c, 0, s]

        @pl.when(code >= 0)
        def _():
            source = pl.multiple_of(((s // 2) * 4 + code % 4) * TILE, TILE)
            into = pl.multiple_of((code // 4) * TILE, TILE)
            got = jnp.dot(tiles[c, s], xp[pl.ds(source, TILE), :], preferred_element_type=F32)
            acc[pl.ds(into, TILE), :] += got

        return carry

    lax.fori_loop(0, NC * SLOTS, slot, 0)
    total = jnp.zeros((D, D), F32)
    for r in range(REL):
        t = acc[r * D : (r + 1) * D, :].astype(BF)
        t_out[r] = t
        total = total + jnp.dot(t, weights[r], preferred_element_type=F32)
    m_out[...] = total.astype(BF).reshape(m_out.shape)


def forward(meta, tiles, xp, weights):
    return pl.pallas_call(
        forward_kernel,
        out_shape=(
            jax.ShapeDtypeStruct((REL, D, D), BF),
            jax.ShapeDtypeStruct((NC, ROWS, D), BF),
        ),
        in_specs=[SM, VM, VM, VM],
        out_specs=(VM, VM),
        scratch_shapes=[pltpu.VMEM((REL * D, D), F32)],
        compiler_params=params(),
    )(meta, tiles, xp, weights)


def slope_kernel(
    m_in, x_own, cot_own, weights, out_o, slope_o, self_o, m_recv, mine, s1, r1, s2, r2, own_sem
):
    z, x, y, p = place()
    peers = group_peers(z, x, y, p)
    greet(peers)
    c = y * 2 + p
    first = []
    for i, q in enumerate(peers):
        a = send(m_in.at[q[2] * 2 + q[3]], m_recv.at[i], s1.at[i], r1.at[i], *q)
        a.start()
        first.append(a)
    w = weights[REL]
    pre = m_in[c].astype(F32) + jnp.dot(x_own[...], w, preferred_element_type=F32)
    for i, a in enumerate(first):
        a.wait_recv()
        pre = pre + m_recv[i].astype(F32)
    sigma = jax.nn.sigmoid(pre)
    slope = (cot_own[...].astype(F32) * (sigma * (1.0 + pre * (1.0 - sigma)))).astype(BF)
    mine[...] = slope
    second = []
    for i, q in enumerate(peers):
        a = send(mine, slope_o.at[c], s2.at[i], r2.at[i], *q)
        a.start()
        second.append(a)
    slope_o[c] = slope
    out_o[...] = pre * sigma
    self_o[...] = lax.dot_general(
        slope, w, (((1,), (1,)), ((), ())), preferred_element_type=F32
    )
    for a in first:
        a.wait_send()
    for a in second:
        a.wait()


def slopes(m_in, x_own, cot_own, weights):
    return pl.pallas_call(
        slope_kernel,
        out_shape=(
            jax.ShapeDtypeStruct((ROWS, D), F32),
            jax.ShapeDtypeStruct((NC, ROWS, D), BF),
            jax.ShapeDtypeStruct((ROWS, D), F32),
        ),
        in_specs=[VM] * 4,
        out_specs=(VM, VM, VM),
        scratch_shapes=[
            pltpu.VMEM((7, ROWS, D), BF), pltpu.VMEM((ROWS, D), BF),
            DMA((7,)), DMA((7,)), DMA((7,)), DMA((7,)), DMA(()),
        ],
        compiler_params=params(1),
    )(m_in, x_own, cot_own, weights)


def backward_kernel(meta, tiles, slope, weights, t_in, x_own, s_own, g_out, w_out, zs, acc):
    over_rows = (((0,), (0,)), ((), ()))
    over_columns = (((1,), (1,)), ((), ()))
    acc[...] = jnp.zeros_like(acc)
    for r in range(REL):
        zs[r * D : (r + 1) * D, :] = lax.dot_general(
            slope[...], weights[r], over_columns, preferred_element_type=F32
        ).astype(BF)

    def slot(i, carry):
        c = i // SLOTS
        s = i % SLOTS
        code = meta[c, 0, s]

        @pl.when(code >= 0)
        def _():
            into = pl.multiple_of(((s // 2) * 4 + code % 4) * TILE, TILE)
            source = pl.multiple_of((code // 4) * TILE, TILE)
            got = lax.dot_general(
                tiles[c, s], zs[pl.ds(source, TILE), :], over_rows, preferred_element_type=F32
            )
            acc[pl.ds(into, TILE), :] += got

        return carry

    lax.fori_loop(0, NC * SLOTS, slot, 0)
    for k in range(4):
        for b in range(4):
            for h in range(2):
                row = (k * 4 + b) * TILE + h * ROWS
                g_out[2 * k + h, b] = acc[row : row + ROWS, :].astype(BF)
    for m in range(REL + 1):
        if m < REL:
            part = lax.dot_general(t_in[m], slope[...], over_rows, preferred_element_type=F32)
        else:
            part = lax.dot_general(x_own[...], s_own[...], over_rows, preferred_element_type=F32)
        part = part.astype(BF)
        for c in range(NC):
            for q in range(4):
                for low, high in ((0, 32), (32, 64)):
                    row = m * ROWS + low
                    w_out[c, (row // WR) * 4 + q, row % WR : row % WR + 32, :] = part[
                        c * ROWS + low : c * ROWS + high, q * WC : (q + 1) * WC
                    ]


def backward(meta, tiles, slope, weights, t_in, x_own, s_own):
    return pl.pallas_call(
        backward_kernel,
        out_shape=(
            jax.ShapeDtypeStruct((NZ, NX, ROWS, D), BF),
            jax.ShapeDtypeStruct((NC, NZ, WR, WC), BF),
        ),
        in_specs=[SM] + [VM] * 6,
        out_specs=(VM, VM),
        scratch_shapes=[pltpu.VMEM((REL * D, D), BF), pltpu.VMEM((16 * TILE, D), F32)],
        compiler_params=params(),
    )(meta, tiles, slope, weights, t_in, x_own, s_own)


def reduce_kernel(
    g_in, w_in, self_in, g_out, w_out,
    c_buf, y_src, y_buf, y_own, zw_src, zw_buf, xw_src, xw_buf, aw_buf,
    g_src, g_buf, gx_src, gx_buf, v_src, v_buf,
    c_s, c_r, y_s, y_r, zw_s, zw_r, xw_s, xw_r, aw_s, aw_r, g_s, g_r, gx_s, gx_r, v_s, v_r,
):
    z, x, y, p = place()
    core = (z, x, y, 1 - p)
    ys = [(z, x, (y + i) % NY, p) for i in (1, 3, 2)]
    xs = x_peers(z, x, y, p)
    around = z_peers(z, x, y, p, (1, 7, 2, 6, 3, 5, 4))
    up, down = around[0], around[1]
    target, is_self = swap_of(z, x, y, p)
    greet([core] + ys + xs + around, (target, is_self))

    c_copies = []
    for i in range(NY):
        yi = (y + i) % NY
        a = send(w_in.at[yi * 2 + 1 - p], c_buf.at[yi], c_s.at[i], c_r.at[i], *core)
        a.start()
        c_copies.append(a)

    g_copies = {}
    hops = {(d, i): 4 if (i < 2) == (d == 0) else 3 for d in range(2) for i in range(NX)}

    def chain(s):
        for i in range(NX):
            xi = (x + i) % NX
            for d, q in ((0, up), (1, down)):
                left = hops[d, i] - s
                if left <= 0:
                    continue
                zd = (z + left) % NZ if d == 0 else (z - left + NZ) % NZ
                if s == 0:
                    src = g_in.at[zd, xi]
                else:
                    g_copies[d, s - 1, i].wait_recv()
                    g_src[d, s - 1, i] = (
                        g_in[zd, xi].astype(F32) + g_buf[d, s - 1, i].astype(F32)
                    ).astype(BF)
                    src = g_src.at[d, s - 1, i]
                a = send(src, g_buf.at[d, s, i], g_s.at[d, s, i], g_r.at[d, s, i], *q)
                a.start()
                g_copies[d, s, i] = a

    chain(0)
    y_copies = []
    for j, q in enumerate(ys):
        i = (1, 3, 2)[j]
        yi = q[2]
        c_copies[i].wait_recv()
        y_src[j] = (w_in[yi * 2 + p].astype(F32) + c_buf[yi].astype(F32)).astype(BF)
        a = send(y_src.at[j], y_buf.at[j], y_s.at[j], y_r.at[j], *q)
        a.start()
        y_copies.append(a)
    c_copies[0].wait_recv()
    y_own[...] = w_in[y * 2 + p].astype(F32) + c_buf[y].astype(F32)
    chain(1)
    chain(2)

    total = y_own[...]
    for j, a in enumerate(y_copies):
        a.wait_recv()
        total = total + y_buf[j].astype(F32)
    zw_src[...] = total.astype(BF)
    zw_copies = []
    for i, q in enumerate(around):
        a = send(zw_src.at[q[0]], zw_buf.at[i], zw_s.at[i], zw_r.at[i], *q)
        a.start()
        zw_copies.append(a)
    chain(3)

    gx_copies = []
    own = None
    for i in (1, 2, 3, 0):
        xi = (x + i) % NX
        part = g_in[z, xi].astype(F32)
        for d in range(2):
            last = hops[d, i] - 1
            g_copies[d, last, i].wait_recv()
            part = part + g_buf[d, last, i].astype(F32)
        if i:
            gx_src[i - 1] = part.astype(BF)
            a = send(gx_src.at[i - 1], gx_buf.at[i - 1], gx_s.at[i - 1], gx_r.at[i - 1], *xs[i - 1])
            a.start()
            gx_copies.append(a)
        else:
            own = part

    mine = zw_src[z].astype(F32)
    for i, a in enumerate(zw_copies):
        a.wait_recv()
        mine = mine + zw_buf[i].astype(F32)
    xw_src[...] = mine.astype(BF)
    xw_copies = []
    for i, q in enumerate(xs):
        a = send(xw_src, xw_buf.at[x], xw_s.at[i], xw_r.at[i], *q)
        a.start()
        xw_copies.append(a)
    xw_buf[x] = xw_src[...]

    for i, a in enumerate(gx_copies):
        a.wait_recv()
        own = own + gx_buf[i].astype(F32)
    v_src[...] = own.astype(BF)

    @pl.when(jnp.logical_not(is_self))
    def _():
        send(v_src, v_buf, v_s, v_r, *target).start()

    @pl.when(is_self)
    def _():
        v_buf[...] = v_src[...]

    for a in xw_copies:
        a.wait_recv()
    done = xw_buf[0].astype(F32)
    for i in range(1, NX):
        done = done + xw_buf[i].astype(F32)
    aw_buf[z] = done.astype(BF)
    aw_copies = []
    for i, q in enumerate(around):
        a = send(aw_buf.at[z], aw_buf.at[z], aw_s.at[i], aw_r.at[i], *q)
        a.start()
        aw_copies.append(a)

    @pl.when(jnp.logical_not(is_self))
    def _():
        send(v_src, v_buf, v_s, v_r, *target).wait()

    g_out[...] = v_buf[...].astype(F32) + self_in[...]
    for a in aw_copies:
        a.wait_recv()
    for m in range(REL + 1):
        for q in range(4):
            for low in (0, 32):
                row = m * ROWS + low
                w_out[m, low : low + 32, q * WC : (q + 1) * WC] = aw_buf[
                    (row // WR) * 4 + q, row % WR : row % WR + 32, :
                ].astype(F32)
    for a in c_copies + y_copies + zw_copies + xw_copies + aw_copies + gx_copies:
        a.wait_send()
    for a in g_copies.values():
        a.wait_send()


def reduce(g_in, w_in, self_in):
    return pl.pallas_call(
        reduce_kernel,
        out_shape=(
            jax.ShapeDtypeStruct((ROWS, D), F32),
            jax.ShapeDtypeStruct((REL + 1, ROWS, D), F32),
        ),
        in_specs=[VM] * 3,
        out_specs=(VM, VM),
        scratch_shapes=[
            pltpu.VMEM((NY, NZ, WR, WC), BF),
            pltpu.VMEM((3, NZ, WR, WC), BF),
            pltpu.VMEM((3, NZ, WR, WC), BF),
            pltpu.VMEM((NZ, WR, WC), F32),
            pltpu.VMEM((NZ, WR, WC), BF),
            pltpu.VMEM((7, WR, WC), BF),
            pltpu.VMEM((WR, WC), BF),
            pltpu.VMEM((NX, WR, WC), BF),
            pltpu.VMEM((NZ, WR, WC), BF),
            pltpu.VMEM((2, 3, NX, ROWS, D), BF),
            pltpu.VMEM((2, 4, NX, ROWS, D), BF),
            pltpu.VMEM((3, ROWS, D), BF),
            pltpu.VMEM((3, ROWS, D), BF),
            pltpu.VMEM((ROWS, D), BF),
            pltpu.VMEM((ROWS, D), BF),
            DMA((4,)), DMA((4,)), DMA((3,)), DMA((3,)), DMA((7,)), DMA((7,)), DMA((3,)), DMA((3,)),
            DMA((7,)), DMA((7,)), DMA((2, 4, 4)), DMA((2, 4, 4)), DMA((3,)), DMA((3,)), DMA(()), DMA(()),
        ],
        compiler_params=params(2),
    )(g_in, w_in, self_in)


def shards(
    states,
    weights,
    edge_tiles,
    edge_owner,
    edge_source,
    edge_target,
    edge_relation,
    edge_count,
    cotangent,
):
    groups = edge_owner.shape[0]
    share = lax.axis_index(("fsdp", "replica"))
    full = lax.all_gather(weights, "fsdp", axis=1, tiled=True)
    owner = edge_owner.reshape(groups, EB)
    source = edge_source.reshape(groups, EB)
    target = edge_target.reshape(groups, EB)
    relation = edge_relation.reshape(groups, EB)
    count = edge_count.reshape(groups)
    tiles = edge_tiles.reshape(EB, TILE, TILE)
    packed, meta = pack(owner, source, target, relation, count, tiles)
    tiles, meta, xp = deal(packed, meta, states)
    t_all, m_part = forward(meta, tiles, xp.reshape(-1, D), full)
    x_own = lax.dynamic_slice_in_dim(states, share * ROWS, ROWS, 0)
    cot_own = lax.dynamic_slice_in_dim(cotangent, share * ROWS, ROWS, 0)
    layer_output, slope, self_part = slopes(m_part, x_own, cot_own, full)
    s_own = lax.dynamic_slice_in_dim(slope, share, 1, 0).reshape(ROWS, D)
    g_part, w_part = backward(meta, tiles, slope.reshape(-1, D), full, t_all, x_own, s_own)
    grad_states, grad_weights = reduce(g_part, w_part, self_part)
    return layer_output, grad_states, grad_weights


def solution(mesh):
    return jax.shard_map(
        shards,
        mesh=mesh,
        in_specs=(
            P("graph", None),
            P(None, "fsdp", None),
            P("graph", "fsdp", "replica", None, None, None),
            P(None, "fsdp", "replica", None),
            P(None, "fsdp", "replica", None),
            P(None, "fsdp", "replica", None),
            P(None, "fsdp", "replica", None),
            P(None, "fsdp", "replica"),
            P("graph", None),
        ),
        out_specs=(
            P(("graph", "fsdp", "replica"), None),
            P(("graph", "fsdp", "replica"), None),
            P(None, ("fsdp", "replica"), None),
        ),
        check_vma=False,
    )
```

```python
import jax
import jax.numpy as jnp
from jax import lax
from jax.experimental import pallas as pl
from jax.experimental.pallas import tpu as pltpu
from jax.sharding import PartitionSpec as P

D = 512
REL = 4
TILE = 128
EB = 48
NZ = 8
NX = 4
NY = 4
NC = 8
SLOTS = 8
ROWS = 64
WROWS = 320
WC = 128
BF = jnp.bfloat16
F32 = jnp.float32
MESH = pl.DeviceIdType.MESH
ANY = pl.BlockSpec(memory_space=pl.ANY)
VM = pl.BlockSpec(memory_space=pltpu.VMEM)
SM = pl.BlockSpec(memory_space=pltpu.SMEM)
DMA = pltpu.SemaphoreType.DMA


def params(mib, collective=None):
    more = {} if collective is None else {"collective_id": collective, "has_side_effects": True}
    return pltpu.CompilerParams(vmem_limit_bytes=mib * 1024 * 1024, **more)


def place():
    g = lax.axis_index("graph")
    return g // NX, g % NX, lax.axis_index("fsdp"), lax.axis_index("replica")


def send(src, dst, ssem, rsem, z, x, y, p):
    return pltpu.make_async_remote_copy(
        src_ref=src,
        dst_ref=dst,
        send_sem=ssem,
        recv_sem=rsem,
        device_id=(z * NX + x, y, p),
        device_id_type=MESH,
    )


def greet(partners, swap=None):
    barrier = pltpu.get_barrier_semaphore()
    for z, x, y, p in partners:
        pl.semaphore_signal(barrier, inc=1, device_id=(z * NX + x, y, p), device_id_type=MESH)
    if swap is not None:
        (z, x, y, p), is_self = swap

        @pl.when(jnp.logical_not(is_self))
        def _():
            pl.semaphore_signal(barrier, inc=1, device_id=(z * NX + x, y, p), device_id_type=MESH)

        pl.semaphore_wait(barrier, len(partners) + jnp.where(is_self, 0, 1))
    else:
        pl.semaphore_wait(barrier, len(partners))


def group_peers(z, x, y, p):
    return [
        (z, x, (y + dy) % NY, (p + dp) % 2)
        for dy, dp in ((0, 1), (1, 0), (3, 0), (1, 1), (3, 1), (2, 0), (2, 1))
    ]


def y_peers(z, x, y, p):
    return [(z, x, (y + i) % NY, p) for i in (1, 3, 2)]


def x_peers(z, x, y, p):
    return [(z, (x + i) % NX, y, p) for i in (1, 2, 3)]


def z_peers(z, x, y, p, steps=(1, 7)):
    return [((z + i) % NZ, x, y, p) for i in steps]


def swap_of(z, x, y, p):
    return (2 * (z // 2) + p, y, x, z % 2), (x == y) & (z % 2 == p)


def pack_kernel(owner, source, target, relation, count, tiles, packed, meta, filled):
    g = lax.axis_index("graph")
    for c in range(NC):
        for s in range(SLOTS):
            meta[c, 0, s] = -1

    def clear(o, carry):
        filled[o] = 0
        return carry

    lax.fori_loop(0, NZ * NX, clear, 0)

    def put(e, carry):
        o = owner[g, e]
        rank = filled[o]
        filled[o] = rank + 1
        c = (o % NX) * 2 + (o // NX) % 2
        s = (o // 8) * 2 + rank
        meta[c, 0, s] = source[g, e] + 4 * target[g, e] + 16 * relation[g, e]
        packed[c, s] = tiles[e]
        return carry

    lax.fori_loop(0, count[g], put, 0)


def pack(owner, source, target, relation, count, tiles):
    return pl.pallas_call(
        pack_kernel,
        out_shape=(
            jax.ShapeDtypeStruct((NC, SLOTS, TILE, TILE), BF),
            jax.ShapeDtypeStruct((NC, 8, 128), jnp.int32),
        ),
        in_specs=[SM] * 5 + [VM],
        out_specs=(VM, SM),
        scratch_shapes=[pltpu.SMEM((NZ * NX,), jnp.int32)],
        compiler_params=params(8),
    )(owner, source, target, relation, count, tiles)


def deal_kernel(
    packed, meta, states, weights, tiles_o, meta_o, xp, full,
    own_sems, t_send, t_recv, m_send, m_recv, v_send, v_recv, x_send, x_recv, z_send, z_recv,
    wy_send, wy_recv, wx_send, wx_recv, wc_send, wc_recv,
):
    z, x, y, p = place()
    peers = group_peers(z, x, y, p)
    core, ys = peers[0], y_peers(z, x, y, p)
    xs = x_peers(z, x, y, p)
    up, down = z_peers(z, x, y, p)
    target, is_self = swap_of(z, x, y, p)
    greet(peers + xs + [up, down], (target, is_self))
    c = y * 2 + p
    piece = states.at[pl.ds(pl.multiple_of((p * NY + y) * ROWS, ROWS), ROWS)]

    @pl.when(jnp.logical_not(is_self))
    def _():
        send(piece, xp.at[target[0], target[1]], v_send, v_recv, *target).start()

    @pl.when(is_self)
    def _():
        pltpu.make_async_copy(piece, xp.at[z, x], own_sems.at[0]).start()

    def rows(yi, xi):
        return pl.ds(pl.multiple_of(yi * 128 + p * 64 + xi * 16, 16), 16)

    wy_copies = []
    mine_w = weights.at[:, pl.ds(pl.multiple_of(p * 64 + x * 16, 16), 16)]
    for i, q in enumerate(ys):
        a = send(mine_w, full.at[:, rows(y, x)], wy_send.at[i], wy_recv.at[i], *q)
        a.start()
        wy_copies.append(a)

    own_copies = [
        pltpu.make_async_copy(packed.at[c], tiles_o.at[c], own_sems.at[1]),
        pltpu.make_async_copy(meta.at[c], meta_o.at[c], own_sems.at[2]),
        pltpu.make_async_copy(
            weights, full.at[:, pl.ds(pl.multiple_of(y * 128, 128), 128)], own_sems.at[3]
        ),
    ]
    for a in own_copies:
        a.start()
    tile_copies = []
    for i, q in enumerate(peers):
        cq = q[2] * 2 + q[3]
        a = send(packed.at[cq], tiles_o.at[c], t_send.at[i], t_recv.at[i], *q)
        b = send(meta.at[cq], meta_o.at[c], m_send.at[i], m_recv.at[i], *q)
        a.start()
        b.start()
        tile_copies += [a, b]

    @pl.when(jnp.logical_not(is_self))
    def _():
        send(piece, xp.at[z, x], v_send, v_recv, *target).wait()

    @pl.when(is_self)
    def _():
        pltpu.make_async_copy(piece, xp.at[z, x], own_sems.at[0]).wait()

    x_copies = [
        send(xp.at[z, x], xp.at[z, x], x_send.at[i], x_recv.at[i], *q) for i, q in enumerate(xs)
    ]
    for a in x_copies:
        a.start()

    wx_copies = []
    wc_copies = []
    z_copies = {}
    for s in range(4):
        for i in range(NX):
            xi = (x + i) % NX
            if s == 0 and i > 0:
                x_copies[3 - i].wait_recv()
            for d, q in ((0, up), (1, down)):
                if s > 0 and (d, s - 1, i) in z_copies:
                    z_copies[d, s - 1, i].wait_recv()
                if s < 3 or (i < 2) == (d == 0):
                    zs = (z - s + NZ) % NZ if d == 0 else (z + s) % NZ
                    a = send(xp.at[zs, xi], xp.at[zs, xi], z_send.at[d, s, i], z_recv.at[d, s, i], *q)
                    a.start()
                    z_copies[d, s, i] = a
        if s == 0:
            for i, yi in enumerate(((y + 3) % NY, (y + 1) % NY, (y + 2) % NY)):
                wy_copies[i].wait_recv()
                for j, q in enumerate(xs):
                    ref = full.at[:, rows(yi, x)]
                    a = send(ref, ref, wx_send.at[i, j], wx_recv.at[i, j], *q)
                    a.start()
                    wx_copies.append(a)
        if s == 2:
            for i, yi in enumerate(((y + 3) % NY, (y + 1) % NY, (y + 2) % NY)):
                for j in range(3):
                    wx_copies[i * 3 + j].wait_recv()
                ref = full.at[:, pl.ds(pl.multiple_of(yi * 128 + p * 64, 64), 64)]
                a = send(ref, ref, wc_send.at[i], wc_recv.at[i], *core)
                a.start()
                wc_copies.append(a)
    for (d, s, i), a in z_copies.items():
        if s == 3:
            a.wait_recv()
    for a in x_copies + list(z_copies.values()) + wy_copies + wx_copies:
        a.wait_send()
    for a in own_copies + wc_copies + tile_copies:
        a.wait()


def deal(packed, meta, states, weights):
    return pl.pallas_call(
        deal_kernel,
        out_shape=(
            jax.ShapeDtypeStruct((NC, SLOTS, TILE, TILE), BF),
            jax.ShapeDtypeStruct((NC, 8, 128), jnp.int32),
            jax.ShapeDtypeStruct((NZ, NX, ROWS, D), BF),
            jax.ShapeDtypeStruct((REL + 1, D, D), BF),
        ),
        in_specs=[ANY] * 4,
        out_specs=(ANY,) * 4,
        scratch_shapes=[
            DMA((4,)), DMA((7,)), DMA((7,)), DMA((7,)), DMA((7,)), DMA(()), DMA(()),
            DMA((3,)), DMA((3,)), DMA((2, 4, 4)), DMA((2, 4, 4)),
            DMA((3,)), DMA((3,)), DMA((3, 3)), DMA((3, 3)), DMA((3,)), DMA((3,)),
        ],
        compiler_params=params(1, 0),
    )(packed, meta, states, weights)


def forward_kernel(meta, tiles, xp, weights, t_out, m_out, acc):
    acc[...] = jnp.zeros_like(acc)

    def slot(i, carry):
        c = i // SLOTS
        s = i % SLOTS
        code = meta[c, 0, s]

        @pl.when(code >= 0)
        def _():
            source = pl.multiple_of(((s // 2) * 4 + code % 4) * TILE, TILE)
            into = pl.multiple_of((code // 4) * TILE, TILE)
            got = jnp.dot(tiles[c, s], xp[pl.ds(source, TILE), :], preferred_element_type=F32)
            acc[pl.ds(into, TILE), :] += got

        return carry

    lax.fori_loop(0, NC * SLOTS, slot, 0)
    total = jnp.zeros((D, D), F32)
    for r in range(REL):
        t = acc[r * D : (r + 1) * D, :].astype(BF)
        t_out[r] = t
        total = total + jnp.dot(t, weights[r], preferred_element_type=F32)
    total = total.astype(BF)
    for c in range(NC):
        m_out[c % 2, c // 2] = total[c * ROWS : (c + 1) * ROWS]


def forward(meta, tiles, xp, weights):
    return pl.pallas_call(
        forward_kernel,
        out_shape=(
            jax.ShapeDtypeStruct((REL, D, D), BF),
            jax.ShapeDtypeStruct((2, NY, ROWS, D), BF),
        ),
        in_specs=[SM, VM, VM, VM],
        out_specs=(VM, VM),
        scratch_shapes=[pltpu.VMEM((REL * D, D), F32)],
        compiler_params=params(24),
    )(meta, tiles, xp, weights)


def slope_kernel(
    m_in, states, cotangent, weights, out_o, slope_o, self_o,
    x_own, cot_own, w_self, c_buf, y_src, y_buf,
    own_sems, c_s, c_r, y_s, y_r, s_s, s_r, f_s, f_r,
):
    z, x, y, p = place()
    core, ys = (z, x, y, 1 - p), y_peers(z, x, y, p)
    c = y * 2 + p
    share = pl.ds(pl.multiple_of(c * ROWS, ROWS), ROWS)
    loads = [
        pltpu.make_async_copy(states.at[share], x_own, own_sems.at[0]),
        pltpu.make_async_copy(cotangent.at[share], cot_own, own_sems.at[1]),
        pltpu.make_async_copy(weights.at[REL], w_self, own_sems.at[2]),
    ]
    for a in loads:
        a.start()
    greet([core] + ys)
    across = send(m_in.at[1 - p], c_buf, c_s, c_r, *core)
    across.start()
    for a in loads:
        a.wait()
    pre = jnp.dot(x_own[...], w_self[...], preferred_element_type=F32)
    across.wait_recv()
    y_copies = []
    for i, q in enumerate(ys):
        y_src[i] = (m_in[p, q[2]].astype(F32) + c_buf[q[2]].astype(F32)).astype(BF)
        a = send(y_src.at[i], y_buf.at[i], y_s.at[i], y_r.at[i], *q)
        a.start()
        y_copies.append(a)
    pre = pre + m_in[p, y].astype(F32) + c_buf[y].astype(F32)
    for i, a in enumerate(y_copies):
        a.wait_recv()
        pre = pre + y_buf[i].astype(F32)
    sigma = jax.nn.sigmoid(pre)
    slope = (cot_own[...].astype(F32) * (sigma * (1.0 + pre * (1.0 - sigma)))).astype(BF)
    slope_o[c] = slope
    mine = slope_o.at[c]
    s_copies = []
    for i, q in enumerate(ys + [core]):
        a = send(mine, mine, s_s.at[i], s_r.at[i], *q)
        a.start()
        s_copies.append(a)
    out_o[...] = pre * sigma
    self_o[...] = lax.dot_general(
        slope, w_self[...], (((1,), (1,)), ((), ())), preferred_element_type=F32
    )
    f_copies = []
    for i, yi in enumerate(((y + 3) % NY, (y + 1) % NY, (y + 2) % NY)):
        s_copies[i].wait_recv()
        ref = slope_o.at[yi * 2 + p]
        a = send(ref, ref, f_s.at[i], f_r.at[i], *core)
        a.start()
        f_copies.append(a)
    s_copies[3].wait_recv()
    for a in [across] + y_copies + s_copies:
        a.wait_send()
    for a in f_copies:
        a.wait()


def slopes(m_in, states, cotangent, weights):
    return pl.pallas_call(
        slope_kernel,
        out_shape=(
            jax.ShapeDtypeStruct((ROWS, D), F32),
            jax.ShapeDtypeStruct((NC, ROWS, D), BF),
            jax.ShapeDtypeStruct((ROWS, D), F32),
        ),
        in_specs=[VM, ANY, ANY, ANY],
        out_specs=(VM, VM, VM),
        scratch_shapes=[
            pltpu.VMEM((ROWS, D), BF), pltpu.VMEM((ROWS, D), BF), pltpu.VMEM((D, D), BF),
            pltpu.VMEM((NY, ROWS, D), BF), pltpu.VMEM((3, ROWS, D), BF), pltpu.VMEM((3, ROWS, D), BF),
            DMA((3,)), DMA(()), DMA(()), DMA((3,)), DMA((3,)), DMA((4,)), DMA((4,)), DMA((3,)), DMA((3,)),
        ],
        compiler_params=params(8, 1),
    )(m_in, states, cotangent, weights)


def backward_kernel(meta, tiles, slope, weights, t_in, states, g_out, w_out, zs, acc):
    over_rows = (((0,), (0,)), ((), ()))
    over_columns = (((1,), (1,)), ((), ()))
    share = lax.axis_index("fsdp") * 2 + lax.axis_index("replica")
    share = pl.ds(pl.multiple_of(share * ROWS, ROWS), ROWS)
    acc[...] = jnp.zeros_like(acc)
    for r in range(REL):
        zs[r * D : (r + 1) * D, :] = lax.dot_general(
            slope[...], weights[r], over_columns, preferred_element_type=F32
        ).astype(BF)

    def slot(i, carry):
        c = i // SLOTS
        s = i % SLOTS
        code = meta[c, 0, s]

        @pl.when(code >= 0)
        def _():
            into = pl.multiple_of(((s // 2) * 4 + code % 4) * TILE, TILE)
            source = pl.multiple_of((code // 4) * TILE, TILE)
            got = lax.dot_general(
                tiles[c, s], zs[pl.ds(source, TILE), :], over_rows, preferred_element_type=F32
            )
            acc[pl.ds(into, TILE), :] += got

        return carry

    lax.fori_loop(0, NC * SLOTS, slot, 0)
    for k in range(4):
        for b in range(4):
            for h in range(2):
                row = (k * 4 + b) * TILE + h * ROWS
                g_out[2 * k + h, b] = acc[row : row + ROWS, :].astype(BF)
    for m in range(REL + 1):
        if m < REL:
            part = lax.dot_general(t_in[m], slope[...], over_rows, preferred_element_type=F32)
        else:
            part = lax.dot_general(
                states[share, :], slope[share, :], over_rows, preferred_element_type=F32
            )
        part = part.astype(BF)
        for c in range(NC):
            for q in range(NX):
                w_out[c % 2, c // 2, q, m * ROWS : (m + 1) * ROWS, :] = part[
                    c * ROWS : (c + 1) * ROWS, q * WC : (q + 1) * WC
                ]


def backward(meta, tiles, slope, weights, t_in, states):
    return pl.pallas_call(
        backward_kernel,
        out_shape=(
            jax.ShapeDtypeStruct((NZ, NX, ROWS, D), BF),
            jax.ShapeDtypeStruct((2, NY, NX, WROWS, WC), BF),
        ),
        in_specs=[SM] + [VM] * 5,
        out_specs=(VM, VM),
        scratch_shapes=[pltpu.VMEM((REL * D, D), BF), pltpu.VMEM((16 * TILE, D), F32)],
        compiler_params=params(28),
    )(meta, tiles, slope, weights, t_in, states)


def reduce_kernel(
    g_in, w_in, v_buf, w_out,
    c_buf, y_src, y_buf, xw_src, xw_buf, zw_src, zw_buf, aw_buf,
    g_src, g_buf, gx_src, gx_buf, v_src,
    c_s, c_r, y_s, y_r, xw_s, xw_r, zw_s, zw_r, aw_s, aw_r, bw_s, bw_r,
    g_s, g_r, gx_s, gx_r, v_s, v_r,
):
    z, x, y, p = place()
    core = (z, x, y, 1 - p)
    ys = y_peers(z, x, y, p)
    xs = x_peers(z, x, y, p)
    around = z_peers(z, x, y, p, (4, 3, 5, 2, 6, 1, 7))
    up, down = around[5], around[6]
    target, is_self = swap_of(z, x, y, p)
    greet([core] + ys + xs + around, (target, is_self))

    order = (1, 2, 3, 0)
    c_copies = []
    for i in order:
        xi = (x + i) % NX
        a = send(w_in.at[1 - p, :, xi], c_buf.at[:, xi], c_s.at[i], c_r.at[i], *core)
        a.start()
        c_copies.append(a)

    g_copies = {}
    hops = {(d, i): 4 if (i < 2) == (d == 0) else 3 for d in range(2) for i in range(NX)}

    def chain(s):
        for i in range(NX):
            xi = (x + i) % NX
            for d, q in ((0, up), (1, down)):
                left = hops[d, i] - s
                if left <= 0:
                    continue
                zd = (z + left) % NZ if d == 0 else (z - left + NZ) % NZ
                if s == 0:
                    src = g_in.at[zd, xi]
                else:
                    g_copies[d, s - 1, i].wait_recv()
                    g_src[d, s - 1, i] = (
                        g_in[zd, xi].astype(F32) + g_buf[d, s - 1, i].astype(F32)
                    ).astype(BF)
                    src = g_src.at[d, s - 1, i]
                a = send(src, g_buf.at[d, s, i], g_s.at[d, s, i], g_r.at[d, s, i], *q)
                a.start()
                g_copies[d, s, i] = a

    chain(0)
    y_copies = {}
    for n, i in enumerate(order):
        xi = (x + i) % NX
        c_copies[n].wait_recv()
        for j, q in enumerate(ys):
            yi = q[2]
            y_src[i, j] = (w_in[p, yi, xi].astype(F32) + c_buf[yi, xi].astype(F32)).astype(BF)
            a = send(y_src.at[i, j], y_buf.at[i, j], y_s.at[i, j], y_r.at[i, j], *q)
            a.start()
            y_copies[i, j] = a

    def y_total(i):
        xi = (x + i) % NX
        total = w_in[p, y, xi].astype(F32) + c_buf[y, xi].astype(F32)
        for j in range(3):
            y_copies[i, j].wait_recv()
            total = total + y_buf[i, j].astype(F32)
        return total

    chain(1)
    xw_copies = []

    def to_x(i):
        xw_src[i - 1] = y_total(i).astype(BF)
        a = send(xw_src.at[i - 1], xw_buf.at[i - 1], xw_s.at[i - 1], xw_r.at[i - 1], *xs[i - 1])
        a.start()
        xw_copies.append(a)

    to_x(1)
    to_x(2)
    chain(2)
    to_x(3)
    total = y_total(0)
    for i, a in enumerate(xw_copies):
        a.wait_recv()
        total = total + xw_buf[i].astype(F32)
    zw_src[...] = total.reshape(NZ, WROWS // NZ, WC)
    zw_copies = []
    for i, q in enumerate(around):
        a = send(zw_src.at[q[0]], zw_buf.at[i], zw_s.at[i], zw_r.at[i], *q)
        a.start()
        zw_copies.append(a)
    chain(3)

    mine = zw_src[z]
    for i, a in enumerate(zw_copies):
        a.wait_recv()
        mine = mine + zw_buf[i]
    aw_buf[z] = mine
    aw_copies = []
    for i, q in enumerate(around):
        a = send(aw_buf.at[z], aw_buf.at[z], aw_s.at[i], aw_r.at[i], *q)
        a.start()
        aw_copies.append(a)

    gx_copies = []
    own = None
    for i in order:
        xi = (x + i) % NX
        part = g_in[z, xi].astype(F32)
        for d in range(2):
            last = hops[d, i] - 1
            g_copies[d, last, i].wait_recv()
            part = part + g_buf[d, last, i].astype(F32)
        if i:
            gx_src[i - 1] = part.astype(BF)
            a = send(gx_src.at[i - 1], gx_buf.at[i - 1], gx_s.at[i - 1], gx_r.at[i - 1], *xs[i - 1])
            a.start()
            gx_copies.append(a)
        else:
            own = part

    for a in aw_copies:
        a.wait_recv()
    w_out[x] = aw_buf[...].reshape(WROWS, WC).astype(BF)
    bw_copies = []
    for i, q in enumerate(xs):
        a = send(w_out.at[x], w_out.at[x], bw_s.at[i], bw_r.at[i], *q)
        a.start()
        bw_copies.append(a)

    for i, a in enumerate(gx_copies):
        a.wait_recv()
        own = own + gx_buf[i].astype(F32)
    v_src[...] = own.astype(BF)

    @pl.when(jnp.logical_not(is_self))
    def _():
        a = send(v_src, v_buf, v_s, v_r, *target)
        a.start()
        a.wait()

    @pl.when(is_self)
    def _():
        v_buf[...] = v_src[...]

    for a in bw_copies:
        a.wait()
    for a in c_copies + zw_copies + xw_copies + aw_copies + gx_copies:
        a.wait_send()
    for a in list(y_copies.values()) + list(g_copies.values()):
        a.wait_send()


def reduce(g_in, w_in):
    return pl.pallas_call(
        reduce_kernel,
        out_shape=(
            jax.ShapeDtypeStruct((ROWS, D), BF),
            jax.ShapeDtypeStruct((NX, WROWS, WC), BF),
        ),
        in_specs=[VM] * 2,
        out_specs=(VM, VM),
        scratch_shapes=[
            pltpu.VMEM((NY, NX, WROWS, WC), BF),
            pltpu.VMEM((NX, 3, WROWS, WC), BF),
            pltpu.VMEM((NX, 3, WROWS, WC), BF),
            pltpu.VMEM((3, WROWS, WC), BF),
            pltpu.VMEM((3, WROWS, WC), BF),
            pltpu.VMEM((NZ, WROWS // NZ, WC), F32),
            pltpu.VMEM((7, WROWS // NZ, WC), F32),
            pltpu.VMEM((NZ, WROWS // NZ, WC), F32),
            pltpu.VMEM((2, 3, NX, ROWS, D), BF),
            pltpu.VMEM((2, 4, NX, ROWS, D), BF),
            pltpu.VMEM((3, ROWS, D), BF),
            pltpu.VMEM((3, ROWS, D), BF),
            pltpu.VMEM((ROWS, D), BF),
            DMA((4,)), DMA((4,)), DMA((4, 3)), DMA((4, 3)), DMA((3,)), DMA((3,)), DMA((7,)), DMA((7,)),
            DMA((7,)), DMA((7,)), DMA((3,)), DMA((3,)), DMA((2, 4, 4)), DMA((2, 4, 4)),
            DMA((3,)), DMA((3,)), DMA(()), DMA(()),
        ],
        compiler_params=params(28, 2),
    )(g_in, w_in)


def close_kernel(layer, own, v, w, layer_o, g_o, w_o):
    layer_o[...] = layer[...]
    g_o[...] = own[...] + v[...].astype(F32)
    for m in range(REL + 1):
        for q in range(NX):
            w_o[m, :, q * WC : (q + 1) * WC] = w[q, m * ROWS : (m + 1) * ROWS, :].astype(F32)


def close(layer, own, v, w):
    return pl.pallas_call(
        close_kernel,
        out_shape=(
            jax.ShapeDtypeStruct((ROWS, D), F32),
            jax.ShapeDtypeStruct((ROWS, D), F32),
            jax.ShapeDtypeStruct((REL + 1, ROWS, D), F32),
        ),
        in_specs=[VM] * 4,
        out_specs=(VM, VM, VM),
        compiler_params=params(8),
    )(layer, own, v, w)


def shards(
    states,
    weights,
    edge_tiles,
    edge_owner,
    edge_source,
    edge_target,
    edge_relation,
    edge_count,
    cotangent,
):
    groups = edge_owner.shape[0]
    owner = edge_owner.reshape(groups, EB)
    source = edge_source.reshape(groups, EB)
    target = edge_target.reshape(groups, EB)
    relation = edge_relation.reshape(groups, EB)
    count = edge_count.reshape(groups)
    tiles = edge_tiles.reshape(EB, TILE, TILE)
    packed, meta = pack(owner, source, target, relation, count, tiles)
    tiles, meta, xp, full = deal(packed, meta, states, weights)
    t_all, m_part = forward(meta, tiles, xp.reshape(-1, D), full)
    layer, slope, own = slopes(m_part, states, cotangent, full)
    g_part, w_part = backward(meta, tiles, slope.reshape(-1, D), full, t_all, states)
    v, w = reduce(g_part, w_part)
    return close(layer, own, v, w)


def solution(mesh):
    return jax.shard_map(
        shards,
        mesh=mesh,
        in_specs=(
            P("graph", None),
            P(None, "fsdp", None),
            P("graph", "fsdp", "replica", None, None, None),
            P(None, "fsdp", "replica", None),
            P(None, "fsdp", "replica", None),
            P(None, "fsdp", "replica", None),
            P(None, "fsdp", "replica", None),
            P(None, "fsdp", "replica"),
            P("graph", None),
        ),
        out_specs=(
            P(("graph", "fsdp", "replica"), None),
            P(("graph", "fsdp", "replica"), None),
            P(None, ("fsdp", "replica"), None),
        ),
        check_vma=False,
    )
```

```python
import jax
import jax.numpy as jnp
from jax import lax
from jax.experimental import pallas as pl
from jax.experimental.pallas import tpu as pltpu
from jax.sharding import PartitionSpec as P

D = 512
REL = 4
TILE = 128
EB = 48
NZ = 8
NX = 4
NY = 4
NC = 8
SLOTS = 8
ROWS = 64
WROWS = 320
WC = 128
BF = jnp.bfloat16
F32 = jnp.float32
MESH = pl.DeviceIdType.MESH
ANY = pl.BlockSpec(memory_space=pl.ANY)
VM = pl.BlockSpec(memory_space=pltpu.VMEM)
SM = pl.BlockSpec(memory_space=pltpu.SMEM)
HB = pl.BlockSpec(memory_space=pltpu.HBM)
DMA = pltpu.SemaphoreType.DMA


def params(mib, collective=None):
    more = {} if collective is None else {"collective_id": collective, "has_side_effects": True}
    return pltpu.CompilerParams(vmem_limit_bytes=mib * 1024 * 1024, **more)


def place():
    g = lax.axis_index("graph")
    return g // NX, g % NX, lax.axis_index("fsdp"), lax.axis_index("replica")


def send(src, dst, ssem, rsem, z, x, y, p):
    return pltpu.make_async_remote_copy(
        src_ref=src,
        dst_ref=dst,
        send_sem=ssem,
        recv_sem=rsem,
        device_id=(z * NX + x, y, p),
        device_id_type=MESH,
    )


def greet(partners, swap=None):
    barrier = pltpu.get_barrier_semaphore()
    for z, x, y, p in partners:
        pl.semaphore_signal(barrier, inc=1, device_id=(z * NX + x, y, p), device_id_type=MESH)
    count = len(partners)
    if swap is not None:
        (z, x, y, p), is_self = swap

        @pl.when(jnp.logical_not(is_self))
        def _():
            pl.semaphore_signal(barrier, inc=1, device_id=(z * NX + x, y, p), device_id_type=MESH)

        count = count + jnp.where(is_self, 0, 1)
    return lambda: pl.semaphore_wait(barrier, count)


def group_peers(z, x, y, p):
    return [
        (z, x, (y + dy) % NY, (p + dp) % 2)
        for dy, dp in ((0, 1), (1, 0), (3, 0), (1, 1), (3, 1), (2, 0), (2, 1))
    ]


def y_peers(z, x, y, p):
    return [(z, x, (y + i) % NY, p) for i in (1, 3, 2)]


def x_peers(z, x, y, p):
    return [(z, (x + i) % NX, y, p) for i in (1, 2, 3)]


def z_peers(z, x, y, p, steps=(1, 7)):
    return [((z + i) % NZ, x, y, p) for i in steps]


def swap_of(z, x, y, p):
    return (2 * (z // 2) + p, y, x, z % 2), (x == y) & (z % 2 == p)


def deal_kernel(
    owner, source, target_h, relation, count, tiles, states, weights, tiles_o, meta_o, xp, full,
    edges, counts, tiles_v, idx_v, idx, meta, packed,
    e_sems, own_sems, t_send, t_recv, m_send, m_recv, v_send, v_recv, x_send, x_recv, z_send, z_recv,
    wy_send, wy_recv, wx_send, wx_recv, wc_send, wc_recv,
):
    z, x, y, p = place()
    peers = group_peers(z, x, y, p)
    core, ys = peers[0], y_peers(z, x, y, p)
    xs = x_peers(z, x, y, p)
    up, down = z_peers(z, x, y, p)
    target, is_self = swap_of(z, x, y, p)
    arrived = greet(peers + xs + [up, down], (target, is_self))
    loads = [
        pltpu.make_async_copy(h, edges.at[i], e_sems.at[i])
        for i, h in enumerate((owner, source, target_h, relation))
    ]
    loads.append(pltpu.make_async_copy(count, counts, e_sems.at[4]))
    for a in loads:
        a.start()
    load_tiles = pltpu.make_async_copy(tiles, tiles_v, e_sems.at[5])
    load_tiles.start()
    c = y * 2 + p
    piece = states.at[pl.ds(pl.multiple_of((p * NY + y) * ROWS, ROWS), ROWS)]

    arrived()

    @pl.when(jnp.logical_not(is_self))
    def _():
        send(piece, xp.at[target[0], target[1]], v_send, v_recv, *target).start()

    @pl.when(is_self)
    def _():
        pltpu.make_async_copy(piece, xp.at[z, x], own_sems.at[0]).start()

    def rows(yi, xi):
        return pl.ds(pl.multiple_of(yi * 128 + p * 64 + xi * 16, 16), 16)

    wy_copies = []
    mine_w = weights.at[:, pl.ds(pl.multiple_of(p * 64 + x * 16, 16), 16)]
    for i, q in enumerate(ys):
        a = send(mine_w, full.at[:, rows(y, x)], wy_send.at[i], wy_recv.at[i], *q)
        a.start()
        wy_copies.append(a)

    own_w = pltpu.make_async_copy(
        weights, full.at[:, pl.ds(pl.multiple_of(y * 128, 128), 128)], own_sems.at[3]
    )
    own_w.start()

    for a in loads:
        a.wait()
    g = lax.axis_index("graph")
    e = lax.broadcasted_iota(jnp.int32, (NC * 4, EB), 1)
    row = lax.broadcasted_iota(jnp.int32, (NC * 4, EB), 0)
    wanted = (2 * (row & 3) + ((row >> 2) & 1)) * NX + (row >> 3)
    groups = lax.broadcasted_iota(jnp.int32, (1, NZ * NX), 1)
    live = jnp.sum(jnp.where(groups == g, counts[...], 0), axis=1, keepdims=True)
    own, src, dst, rel = (edges[i, pl.ds(g, 1), :] for i in range(4))
    code = src + 4 * (dst * REL + rel)
    hit = (own == wanted) & (e < live)
    first = jnp.min(jnp.where(hit, e, EB), axis=1, keepdims=True)
    last = jnp.max(jnp.where(hit, e, -1), axis=1, keepdims=True)
    code0 = jnp.sum(jnp.where(hit & (e == first), code, 0), axis=1, keepdims=True)
    code1 = jnp.sum(jnp.where(hit & (e == last), code, 0), axis=1, keepdims=True)
    code0 = jnp.where(first < EB, code0, -1)
    code1 = jnp.where(last > first, code1, -1)
    lane = lax.broadcasted_iota(jnp.int32, (NC * 4, 128), 1)
    idx_v[...] = jnp.where(lane == 0, jnp.minimum(first, EB - 1), jnp.maximum(last, 0))
    codes = jnp.where(lane == 0, code0, code1)
    meta[...] = jnp.full(meta.shape, -1, jnp.int32)
    for i in range(NC):
        meta[i, 0:4, :] = codes[i * 4 : i * 4 + 4]
    to_scalars = pltpu.make_async_copy(idx_v, idx, e_sems.at[6])
    to_scalars.start()
    to_scalars.wait()
    load_tiles.wait()

    def put(ci):
        def one(s, carry):
            packed[ci, s] = tiles_v[idx[ci * 4 + s // 2, s % 2]]
            return carry

        lax.fori_loop(0, SLOTS, one, 0)

    tile_copies = []
    for i, q in enumerate(peers):
        cq = q[2] * 2 + q[3]
        put(cq)
        a = send(packed.at[cq], tiles_o.at[c], t_send.at[i], t_recv.at[i], *q)
        b = send(meta.at[cq], meta_o.at[c], m_send.at[i], m_recv.at[i], *q)
        a.start()
        b.start()
        tile_copies += [a, b]
    put(c)
    own_copies = [
        pltpu.make_async_copy(packed.at[c], tiles_o.at[c], own_sems.at[1]),
        pltpu.make_async_copy(meta.at[c], meta_o.at[c], own_sems.at[2]),
    ]
    for a in own_copies:
        a.start()
    own_copies.append(own_w)

    @pl.when(jnp.logical_not(is_self))
    def _():
        send(piece, xp.at[z, x], v_send, v_recv, *target).wait()

    @pl.when(is_self)
    def _():
        pltpu.make_async_copy(piece, xp.at[z, x], own_sems.at[0]).wait()

    x_copies = [
        send(xp.at[z, x], xp.at[z, x], x_send.at[i], x_recv.at[i], *q) for i, q in enumerate(xs)
    ]
    for a in x_copies:
        a.start()

    wx_copies = []
    wc_copies = []
    z_copies = {}
    for s in range(4):
        for i in range(NX):
            xi = (x + i) % NX
            if s == 0 and i > 0:
                x_copies[3 - i].wait_recv()
            for d, q in ((0, up), (1, down)):
                if s > 0 and (d, s - 1, i) in z_copies:
                    z_copies[d, s - 1, i].wait_recv()
                if s < 3 or (i < 2) == (d == 0):
                    zs = (z - s + NZ) % NZ if d == 0 else (z + s) % NZ
                    a = send(xp.at[zs, xi], xp.at[zs, xi], z_send.at[d, s, i], z_recv.at[d, s, i], *q)
                    a.start()
                    z_copies[d, s, i] = a
        if s == 0:
            for i, yi in enumerate(((y + 3) % NY, (y + 1) % NY, (y + 2) % NY)):
                wy_copies[i].wait_recv()
                for j, q in enumerate(xs):
                    ref = full.at[:, rows(yi, x)]
                    a = send(ref, ref, wx_send.at[i, j], wx_recv.at[i, j], *q)
                    a.start()
                    wx_copies.append(a)
        if s == 2:
            for i, yi in enumerate(((y + 3) % NY, (y + 1) % NY, (y + 2) % NY)):
                for j in range(3):
                    wx_copies[i * 3 + j].wait_recv()
                ref = full.at[:, pl.ds(pl.multiple_of(yi * 128 + p * 64, 64), 64)]
                a = send(ref, ref, wc_send.at[i], wc_recv.at[i], *core)
                a.start()
                wc_copies.append(a)
    for (d, s, i), a in z_copies.items():
        if s == 3:
            a.wait_recv()
    for a in x_copies + list(z_copies.values()) + wy_copies + wx_copies:
        a.wait_send()
    for a in own_copies + wc_copies + tile_copies:
        a.wait()


def deal(owner, source, target, relation, count, tiles, states, weights):
    return pl.pallas_call(
        deal_kernel,
        out_shape=(
            jax.ShapeDtypeStruct((NC, SLOTS, TILE, TILE), BF),
            jax.ShapeDtypeStruct((NC, 8, 128), jnp.int32),
            jax.ShapeDtypeStruct((NZ, NX, ROWS, D), BF),
            jax.ShapeDtypeStruct((REL + 1, D, D), BF),
        ),
        in_specs=[HB] * 8,
        out_specs=(ANY,) * 4,
        scratch_shapes=[
            pltpu.VMEM((4, NZ * NX, EB), jnp.int32),
            pltpu.VMEM((1, NZ * NX), jnp.int32),
            pltpu.VMEM((EB, TILE, TILE), BF),
            pltpu.VMEM((NC * 4, 128), jnp.int32),
            pltpu.SMEM((NC * 4, 128), jnp.int32),
            pltpu.VMEM((NC, 8, 128), jnp.int32),
            pltpu.VMEM((NC, SLOTS, TILE, TILE), BF),
            DMA((7,)), DMA((4,)), DMA((7,)), DMA((7,)), DMA((7,)), DMA((7,)), DMA(()), DMA(()),
            DMA((3,)), DMA((3,)), DMA((2, 4, 4)), DMA((2, 4, 4)),
            DMA((3,)), DMA((3,)), DMA((3, 3)), DMA((3, 3)), DMA((3,)), DMA((3,)),
        ],
        compiler_params=params(8, 0),
    )(owner, source, target, relation, count, tiles, states, weights)


def adjacency_kernel(meta, tiles, adj):
    adj[...] = jnp.zeros_like(adj)

    def slots(c, carry):
        for s in range(SLOTS):
            code = meta[c, s // 2, s % 2]

            @pl.when(code >= 0)
            def _():
                row = pl.ds(pl.multiple_of((code >> 2) * TILE, TILE), TILE)
                column = pl.ds(pl.multiple_of(((s // 2) * 4 + (code & 3)) * TILE, TILE), TILE)
                adj[row, column] += tiles[c, s]

        return carry

    lax.fori_loop(0, NC, slots, 0)


def adjacency(meta, tiles):
    return pl.pallas_call(
        adjacency_kernel,
        out_shape=jax.ShapeDtypeStruct((NY * REL * TILE, 16 * TILE), BF),
        in_specs=[SM, VM],
        out_specs=VM,
        compiler_params=params(6),
    )(meta, tiles)


def main_kernel(
    adj, xp, weights, states, cotangent,
    layer_o, own_o, v_buf, wa, wb,
    tq, tc_buf, ty_src, ty_buf, tg, m_own, m_src, m_buf, my_src, my_buf, slope_s, zs, gw,
    xw_src, xw_buf, zw_src, zw_buf, aw_buf, wb_src, g_in, g_src, g_buf, gx_src, gx_buf, v_src,
    tc_s, tc_r, ty_s, ty_r, mc_s, mc_r, my_s, my_r, s_s, s_r, f_s, f_r,
    xw_s, xw_r, zw_s, zw_r, aw_s, aw_r, wa_s, wa_r, wb_s, wb_r, g_s, g_r, gx_s, gx_r, v_s, v_r,
):
    over_rows = (((0,), (0,)), ((), ()))
    over_columns = (((1,), (1,)), ((), ()))
    z, x, y, p = place()
    core = (z, x, y, 1 - p)
    shifts = (2, 1, 3)
    ys = [(z, x, (y + i) % NY, p) for i in shifts]
    senders = [(y + NY - i) % NY for i in shifts]
    xs = x_peers(z, x, y, p)
    xo = [(q[0], q[1], q[2], 1 - p) for q in xs]
    around = z_peers(z, x, y, p, (4, 3, 5, 2, 6, 1, 7))
    up, down = around[5], around[6]
    target, is_self = swap_of(z, x, y, p)
    arrived = greet([core] + ys + xs + xo + around, (target, is_self))
    c = y * 2 + p
    share = pl.ds(pl.multiple_of(c * ROWS, ROWS), ROWS)

    def half(v, mine):
        low, high = v[:ROWS], v[ROWS:]
        return jnp.where(p == (0 if mine else 1), low, high)

    order = [q[2] for q in ys] + [y]
    m_copies, t_copies, my_copies = [], [], []

    def messages_on(n):
        m_copies[n].wait_recv()
        t = order[n]
        my_src[n] = (m_own[t] + m_buf[t].astype(F32)).astype(BF)
        a = send(my_src.at[n], my_buf.at[n], my_s.at[n], my_r.at[n], *ys[n])
        a.start()
        my_copies.append(a)

    for n, t in enumerate(order):
        rows = pl.ds(pl.multiple_of(t * D, D), D)
        tt = jnp.dot(adj[rows, :], xp[...], preferred_element_type=F32).astype(BF)
        m = jnp.zeros((TILE, D), F32)
        for r in range(REL):
            part = tt[r * TILE : (r + 1) * TILE]
            m = m + jnp.dot(part, weights[r], preferred_element_type=F32)
            for q in range(NY):
                tq[r // 2, t, q, r % 2] = part[:, q * TILE : (q + 1) * TILE]
        m_own[t] = half(m, True)
        m_src[t] = half(m, False).astype(BF)
        if n == 0:
            arrived()
        a = send(m_src.at[t], m_buf.at[t], mc_s.at[n], mc_r.at[n], *core)
        a.start()
        m_copies.append(a)
        if n > 0:
            messages_on(n - 1)
        a = send(tq.at[1 - p, t], tc_buf.at[t], tc_s.at[n], tc_r.at[n], *core)
        a.start()
        t_copies.append(a)

    ty_copies = {}

    def transforms_on(n):
        t = order[n]
        t_copies[n].wait_recv()
        for j, q in enumerate(ys):
            yi = q[2]
            ty_src[j, t] = (tq[p, t, yi].astype(F32) + tc_buf[t, yi].astype(F32)).astype(BF)
            a = send(ty_src.at[j, t], ty_buf.at[j, t], ty_s.at[j, n], ty_r.at[j, n], *q)
            a.start()
            ty_copies[j, n] = a

    transforms_on(0)

    w_self = weights[REL]
    pre = jnp.dot(states[share, :], w_self, preferred_element_type=F32)
    m_copies[3].wait_recv()
    pre = pre + m_own[y] + m_buf[y].astype(F32)
    for n, a in enumerate(my_copies):
        a.wait_recv()
        pre = pre + my_buf[n].astype(F32)
    sigma = jax.nn.sigmoid(pre)
    slope = (cotangent[share, :].astype(F32) * (sigma * (1.0 + pre * (1.0 - sigma)))).astype(BF)
    slope_s[c] = slope
    mine = slope_s.at[c]
    s_copies = []
    for i, q in enumerate(ys + [core]):
        a = send(mine, mine, s_s.at[i], s_r.at[i], *q)
        a.start()
        s_copies.append(a)
    for n in (1, 2, 3):
        transforms_on(n)
    layer_o[...] = pre * sigma
    own_o[...] = lax.dot_general(slope, w_self, over_columns, preferred_element_type=F32)
    f_copies = []
    for i in (1, 2, 0):
        s_copies[i].wait_recv()
        ref = slope_s.at[senders[i] * 2 + p]
        a = send(ref, ref, f_s.at[i], f_r.at[i], *core)
        a.start()
        f_copies.append(a)
    s_copies[3].wait_recv()
    for a in f_copies:
        a.wait_recv()

    whole = slope_s[...].reshape(D, D)
    for r in range(REL):
        part = lax.dot_general(whole, weights[r], over_columns, preferred_element_type=F32)
        part = part.astype(BF)
        for t in range(NY):
            zs[t * D + r * TILE : t * D + (r + 1) * TILE, :] = part[t * TILE : (t + 1) * TILE]

    def gradients(k):
        columns = pl.ds(pl.multiple_of(k * D, D), D)
        part = lax.dot_general(adj[:, columns], zs[...], over_rows, preferred_element_type=F32)
        part = part.astype(BF)
        for b in range(4):
            for h in range(2):
                row = b * TILE + h * ROWS
                g_in[2 * k + h, b] = part[row : row + ROWS]

    g_copies = {}
    hops = {(d, i): 4 if (i < 2) == (d == 0) else 3 for d in range(2) for i in range(NX)}

    def chain(s):
        for i in range(NX):
            xi = (x + i) % NX
            for d, q in ((0, up), (1, down)):
                left = hops[d, i] - s
                if left <= 0:
                    continue
                zd = (z + left) % NZ if d == 0 else (z - left + NZ) % NZ
                if s == 0:
                    src = g_in.at[zd, xi]
                else:
                    g_copies[d, s - 1, i].wait_recv()
                    g_src[d, s - 1, i] = (
                        g_in[zd, xi].astype(F32) + g_buf[d, s - 1, i].astype(F32)
                    ).astype(BF)
                    src = g_src.at[d, s - 1, i]
                a = send(src, g_buf.at[d, s, i], g_s.at[d, s, i], g_r.at[d, s, i], *q)
                a.start()
                g_copies[d, s, i] = a

    pair = z // 2
    odd = 2 * (z % 2)
    gradients((pair + 2) % 4)
    gradients((pair + 1 + odd) % 4)
    chain(0)
    gradients((pair + 3 + odd) % 4)
    chain(1)
    gradients(pair)

    for a in ty_copies.values():
        a.wait_recv()
    for t in range(NY):
        total = tq[p, t, y].astype(F32) + tc_buf[t, y].astype(F32)
        for j in range(3):
            total = total + ty_buf[j, t].astype(F32)
        for r in range(2):
            tg[r, t * TILE : (t + 1) * TILE, :] = total[r].astype(BF)
    parts = [
        lax.dot_general(tg[r], whole, over_rows, preferred_element_type=F32) for r in range(2)
    ]
    columns = pl.ds(pl.multiple_of(y * TILE, TILE), TILE)
    self_part = lax.dot_general(states[:, columns], whole, over_rows, preferred_element_type=F32)
    rows_of = [half(v, True) for v in parts] + [half(self_part, True)] + [half(v, False) for v in parts]
    for m, v in enumerate(rows_of):
        for q in range(NX):
            gw[q, m * ROWS : (m + 1) * ROWS, :] = v[:, q * WC : (q + 1) * WC]
    xw_copies = []
    for i in range(3):
        xw_src[i] = gw[xs[i][1]].astype(BF)
        a = send(xw_src.at[i], xw_buf.at[i], xw_s.at[i], xw_r.at[i], *xs[i])
        a.start()
        xw_copies.append(a)
    chain(2)
    total = gw[x]
    for i, a in enumerate(xw_copies):
        a.wait_recv()
        total = total + xw_buf[i].astype(F32)
    zw_src[...] = total.reshape(NZ, WROWS // NZ, WC)
    zw_copies = []
    for i, q in enumerate(around):
        a = send(zw_src.at[q[0]], zw_buf.at[i], zw_s.at[i], zw_r.at[i], *q)
        a.start()
        zw_copies.append(a)
    chain(3)
    total = zw_src[z]
    for i, a in enumerate(zw_copies):
        a.wait_recv()
        total = total + zw_buf[i]
    aw_buf[z] = total
    aw_copies = []
    for i, q in enumerate(around):
        a = send(aw_buf.at[z], aw_buf.at[z], aw_s.at[i], aw_r.at[i], *q)
        a.start()
        aw_copies.append(a)

    gx_copies = []
    own = None
    for i in (1, 2, 3, 0):
        xi = (x + i) % NX
        part = g_in[z, xi].astype(F32)
        for d in range(2):
            last = hops[d, i] - 1
            g_copies[d, last, i].wait_recv()
            part = part + g_buf[d, last, i].astype(F32)
        if i:
            gx_src[i - 1] = part.astype(BF)
            a = send(gx_src.at[i - 1], gx_buf.at[i - 1], gx_s.at[i - 1], gx_r.at[i - 1], *xs[i - 1])
            a.start()
            gx_copies.append(a)
        else:
            own = part

    for a in aw_copies:
        a.wait_recv()
    done = aw_buf[...].reshape(WROWS, WC).astype(BF)
    wa[x] = done[: 3 * ROWS]
    wb_src[...] = done[3 * ROWS :]
    w_copies = []
    for i, q in enumerate(xs):
        w_copies.append(send(wa.at[x], wa.at[x], wa_s.at[i], wa_r.at[i], *q))
    for i, q in enumerate(xo + [core]):
        w_copies.append(send(wb_src, wb.at[x], wb_s.at[i], wb_r.at[i], *q))
    for a in w_copies:
        a.start()

    for i, a in enumerate(gx_copies):
        a.wait_recv()
        own = own + gx_buf[i].astype(F32)
    v_src[...] = own.astype(BF)

    @pl.when(jnp.logical_not(is_self))
    def _():
        a = send(v_src, v_buf, v_s, v_r, *target)
        a.start()
        a.wait()

    @pl.when(is_self)
    def _():
        v_buf[...] = v_src[...]

    for a in w_copies:
        a.wait()
    for a in m_copies + t_copies + my_copies + s_copies + f_copies:
        a.wait_send()
    for a in xw_copies + zw_copies + aw_copies + gx_copies:
        a.wait_send()
    for a in list(ty_copies.values()) + list(g_copies.values()):
        a.wait_send()


def main(adj, xp, weights, states, cotangent):
    return pl.pallas_call(
        main_kernel,
        out_shape=(
            jax.ShapeDtypeStruct((ROWS, D), F32),
            jax.ShapeDtypeStruct((ROWS, D), F32),
            jax.ShapeDtypeStruct((ROWS, D), BF),
            jax.ShapeDtypeStruct((NX, 3 * ROWS, WC), BF),
            jax.ShapeDtypeStruct((NX, 2 * ROWS, WC), BF),
        ),
        in_specs=[VM] * 5,
        out_specs=(VM,) * 5,
        scratch_shapes=[
            pltpu.VMEM((2, NY, NY, 2, TILE, TILE), BF),
            pltpu.VMEM((NY, NY, 2, TILE, TILE), BF),
            pltpu.VMEM((3, NY, 2, TILE, TILE), BF),
            pltpu.VMEM((3, NY, 2, TILE, TILE), BF),
            pltpu.VMEM((2, D, TILE), BF),
            pltpu.VMEM((NY, ROWS, D), F32),
            pltpu.VMEM((NY, ROWS, D), BF),
            pltpu.VMEM((NY, ROWS, D), BF),
            pltpu.VMEM((3, ROWS, D), BF),
            pltpu.VMEM((3, ROWS, D), BF),
            pltpu.VMEM((NC, ROWS, D), BF),
            pltpu.VMEM((NY * D, D), BF),
            pltpu.VMEM((NX, WROWS, WC), F32),
            pltpu.VMEM((3, WROWS, WC), BF),
            pltpu.VMEM((3, WROWS, WC), BF),
            pltpu.VMEM((NZ, WROWS // NZ, WC), F32),
            pltpu.VMEM((7, WROWS // NZ, WC), F32),
            pltpu.VMEM((NZ, WROWS // NZ, WC), F32),
            pltpu.VMEM((2 * ROWS, WC), BF),
            pltpu.VMEM((NZ, NX, ROWS, D), BF),
            pltpu.VMEM((2, 3, NX, ROWS, D), BF),
            pltpu.VMEM((2, 4, NX, ROWS, D), BF),
            pltpu.VMEM((3, ROWS, D), BF),
            pltpu.VMEM((3, ROWS, D), BF),
            pltpu.VMEM((ROWS, D), BF),
            DMA((4,)), DMA((4,)), DMA((3, 4)), DMA((3, 4)), DMA((4,)), DMA((4,)), DMA((3,)), DMA((3,)),
            DMA((4,)), DMA((4,)), DMA((3,)), DMA((3,)),
            DMA((3,)), DMA((3,)), DMA((7,)), DMA((7,)), DMA((7,)), DMA((7,)), DMA((3,)), DMA((3,)),
            DMA((4,)), DMA((4,)), DMA((2, 4, 4)), DMA((2, 4, 4)), DMA((3,)), DMA((3,)), DMA(()), DMA(()),
        ],
        compiler_params=params(32, 1),
    )(adj, xp, weights, states, cotangent)


def close_kernel(layer, own, v, wa, wb, layer_o, g_o, w_o):
    p = lax.axis_index("replica")
    layer_o[...] = layer[...]
    g_o[...] = own[...] + v[...].astype(F32)
    for q in range(NX):
        columns = slice(q * WC, (q + 1) * WC)
        for m in range(2):
            a = wa[q, m * ROWS : (m + 1) * ROWS, :].astype(F32)
            b = wb[q, m * ROWS : (m + 1) * ROWS, :].astype(F32)
            w_o[m, :, columns] = jnp.where(p == 0, a, b)
            w_o[2 + m, :, columns] = jnp.where(p == 0, b, a)
        w_o[REL, :, columns] = wa[q, 2 * ROWS :, :].astype(F32)


def close(layer, own, v, wa, wb):
    return pl.pallas_call(
        close_kernel,
        out_shape=(
            jax.ShapeDtypeStruct((ROWS, D), F32),
            jax.ShapeDtypeStruct((ROWS, D), F32),
            jax.ShapeDtypeStruct((REL + 1, ROWS, D), F32),
        ),
        in_specs=[VM] * 5,
        out_specs=(VM, VM, VM),
        compiler_params=params(8),
    )(layer, own, v, wa, wb)


def shards(
    states,
    weights,
    edge_tiles,
    edge_owner,
    edge_source,
    edge_target,
    edge_relation,
    edge_count,
    cotangent,
):
    groups = edge_owner.shape[0]
    owner = edge_owner.reshape(groups, EB)
    source = edge_source.reshape(groups, EB)
    target = edge_target.reshape(groups, EB)
    relation = edge_relation.reshape(groups, EB)
    count = edge_count.reshape(1, groups)
    tiles = edge_tiles.reshape(EB, TILE, TILE)
    tiles, meta, xp, full = deal(owner, source, target, relation, count, tiles, states, weights)
    adj = adjacency(meta, tiles)
    layer, own, v, wa, wb = main(adj, xp.reshape(-1, D), full, states, cotangent)
    return close(layer, own, v, wa, wb)


def solution(mesh):
    return jax.shard_map(
        shards,
        mesh=mesh,
        in_specs=(
            P("graph", None),
            P(None, "fsdp", None),
            P("graph", "fsdp", "replica", None, None, None),
            P(None, "fsdp", "replica", None),
            P(None, "fsdp", "replica", None),
            P(None, "fsdp", "replica", None),
            P(None, "fsdp", "replica", None),
            P(None, "fsdp", "replica"),
            P("graph", None),
        ),
        out_specs=(
            P(("graph", "fsdp", "replica"), None),
            P(("graph", "fsdp", "replica"), None),
            P(None, ("fsdp", "replica"), None),
        ),
        check_vma=False,
    )
```

```python
import jax
import jax.numpy as jnp
from jax import lax
from jax.experimental import pallas as pl
from jax.experimental.pallas import tpu as pltpu
from jax.sharding import PartitionSpec as P

D = 512
REL = 4
TILE = 128
EB = 48
NZ = 8
NX = 4
NY = 4
NC = 8
SLOTS = 8
ROWS = 64
WROWS = 320
ZROWS = 48
HA = 32
HB = ROWS - HA
WC = 128
BF = jnp.bfloat16
F32 = jnp.float32
MESH = pl.DeviceIdType.MESH
ANY = pl.BlockSpec(memory_space=pl.ANY)
VM = pl.BlockSpec(memory_space=pltpu.VMEM)
SM = pl.BlockSpec(memory_space=pltpu.SMEM)
IN_HBM = pl.BlockSpec(memory_space=pltpu.HBM)
DMA = pltpu.SemaphoreType.DMA


def params(mib, collective=None):
    more = {} if collective is None else {"collective_id": collective, "has_side_effects": True}
    return pltpu.CompilerParams(vmem_limit_bytes=mib * 1024 * 1024, **more)


def place():
    g = lax.axis_index("graph")
    return g // NX, g % NX, lax.axis_index("fsdp"), lax.axis_index("replica")


def send(src, dst, ssem, rsem, z, x, y, p):
    return pltpu.make_async_remote_copy(
        src_ref=src,
        dst_ref=dst,
        send_sem=ssem,
        recv_sem=rsem,
        device_id=(z * NX + x, y, p),
        device_id_type=MESH,
    )


def greet(partners, swap=None):
    barrier = pltpu.get_barrier_semaphore()
    for z, x, y, p in partners:
        pl.semaphore_signal(barrier, inc=1, device_id=(z * NX + x, y, p), device_id_type=MESH)
    count = len(partners)
    if swap is not None:
        (z, x, y, p), is_self = swap

        @pl.when(jnp.logical_not(is_self))
        def _():
            pl.semaphore_signal(barrier, inc=1, device_id=(z * NX + x, y, p), device_id_type=MESH)

        count = count + jnp.where(is_self, 0, 1)
    return lambda: pl.semaphore_wait(barrier, count)


def group_peers(z, x, y, p):
    return [
        (z, x, (y + dy) % NY, (p + dp) % 2)
        for dy, dp in ((0, 1), (1, 0), (3, 0), (1, 1), (3, 1), (2, 0), (2, 1))
    ]


def y_peers(z, x, y, p):
    return [(z, x, (y + i) % NY, p) for i in (1, 3, 2)]


def x_peers(z, x, y, p):
    return [(z, (x + i) % NX, y, p) for i in (1, 2, 3)]


def z_peers(z, x, y, p, steps=(1, 7)):
    return [((z + i) % NZ, x, y, p) for i in steps]


def swap_of(z, x, y, p):
    return (2 * (z // 2) + p, y, x, z % 2), (x == y) & (z % 2 == p)


def deal_kernel(
    owner, source, target_h, relation, count, tiles, states, weights, tiles_o, meta_o, xp, full,
    edges, counts, tiles_v, idx_v, idx, meta, packed,
    e_sems, own_sems, t_send, t_recv, m_send, m_recv, v_send, v_recv, x_send, x_recv, z_send, z_recv,
    wy_send, wy_recv, wx_send, wx_recv, wc_send, wc_recv,
):
    z, x, y, p = place()
    peers = group_peers(z, x, y, p)
    core, ys = peers[0], y_peers(z, x, y, p)
    xs = x_peers(z, x, y, p)
    up, down = z_peers(z, x, y, p)
    target, is_self = swap_of(z, x, y, p)
    loads = [
        pltpu.make_async_copy(h, edges.at[i], e_sems.at[i])
        for i, h in enumerate((owner, source, target_h, relation))
    ]
    loads.append(pltpu.make_async_copy(count, counts, e_sems.at[4]))
    for a in loads:
        a.start()
    load_tiles = pltpu.make_async_copy(tiles, tiles_v, e_sems.at[5])
    load_tiles.start()
    arrived = greet(peers + xs + [up, down], (target, is_self))
    c = y * 2 + p
    piece = states.at[pl.ds(pl.multiple_of((p * NY + y) * ROWS, ROWS), ROWS)]

    arrived()

    @pl.when(jnp.logical_not(is_self))
    def _():
        send(piece, xp.at[target[0], target[1]], v_send, v_recv, *target).start()

    @pl.when(is_self)
    def _():
        pltpu.make_async_copy(piece, xp.at[z, x], own_sems.at[0]).start()

    def rows(yi, xi):
        return pl.ds(pl.multiple_of(yi * 128 + p * 64 + xi * 16, 16), 16)

    wy_copies = []
    mine_w = weights.at[:, pl.ds(pl.multiple_of(p * 64 + x * 16, 16), 16)]
    for i, q in enumerate(ys):
        a = send(mine_w, full.at[:, rows(y, x)], wy_send.at[i], wy_recv.at[i], *q)
        a.start()
        wy_copies.append(a)

    own_w = pltpu.make_async_copy(
        weights, full.at[:, pl.ds(pl.multiple_of(y * 128, 128), 128)], own_sems.at[3]
    )
    own_w.start()

    for a in loads:
        a.wait()
    g = lax.axis_index("graph")
    e = lax.broadcasted_iota(jnp.int32, (NC * 4, EB), 1)
    row = lax.broadcasted_iota(jnp.int32, (NC * 4, EB), 0)
    wanted = (2 * (row & 3) + ((row >> 2) & 1)) * NX + (row >> 3)
    groups = lax.broadcasted_iota(jnp.int32, (1, NZ * NX), 1)
    live = jnp.sum(jnp.where(groups == g, counts[...], 0), axis=1, keepdims=True)
    own, src, dst, rel = (edges[i, pl.ds(g, 1), :] for i in range(4))
    code = src + 4 * (dst * REL + rel)
    hit = (own == wanted) & (e < live)
    first = jnp.min(jnp.where(hit, e, EB), axis=1, keepdims=True)
    last = jnp.max(jnp.where(hit, e, -1), axis=1, keepdims=True)
    code0 = jnp.sum(jnp.where(hit & (e == first), code, 0), axis=1, keepdims=True)
    code1 = jnp.sum(jnp.where(hit & (e == last), code, 0), axis=1, keepdims=True)
    code0 = jnp.where(first < EB, code0, -1)
    code1 = jnp.where(last > first, code1, -1)
    lane = lax.broadcasted_iota(jnp.int32, (NC * 4, 128), 1)
    idx_v[...] = jnp.where(lane == 0, jnp.minimum(first, EB - 1), jnp.maximum(last, 0))
    codes = jnp.where(lane == 0, code0, code1)
    meta[...] = jnp.full(meta.shape, -1, jnp.int32)
    for i in range(NC):
        meta[i, 0:4, :] = codes[i * 4 : i * 4 + 4]
    to_scalars = pltpu.make_async_copy(idx_v, idx, e_sems.at[6])
    to_scalars.start()
    to_scalars.wait()
    load_tiles.wait()

    def put(ci):
        def one(s, carry):
            packed[ci, s] = tiles_v[idx[ci * 4 + s // 2, s % 2]]
            return carry

        lax.fori_loop(0, SLOTS, one, 0)

    x_copies = [
        send(xp.at[z, x], xp.at[z, x], x_send.at[i], x_recv.at[i], *q) for i, q in enumerate(xs)
    ]

    def x_phase():
        @pl.when(jnp.logical_not(is_self))
        def _():
            send(piece, xp.at[z, x], v_send, v_recv, *target).wait()

        @pl.when(is_self)
        def _():
            pltpu.make_async_copy(piece, xp.at[z, x], own_sems.at[0]).wait()

        for a in x_copies:
            a.start()

    tile_copies = []
    for i, q in enumerate(peers):
        if i == 3:
            x_phase()
        cq = q[2] * 2 + q[3]
        put(cq)
        a = send(packed.at[cq], tiles_o.at[c], t_send.at[i], t_recv.at[i], *q)
        b = send(meta.at[cq], meta_o.at[c], m_send.at[i], m_recv.at[i], *q)
        a.start()
        b.start()
        tile_copies += [a, b]
    put(c)
    own_copies = [
        pltpu.make_async_copy(packed.at[c], tiles_o.at[c], own_sems.at[1]),
        pltpu.make_async_copy(meta.at[c], meta_o.at[c], own_sems.at[2]),
    ]
    for a in own_copies:
        a.start()
    own_copies.append(own_w)

    wx_copies = []
    wc_copies = []
    z_copies = {}
    for s in range(4):
        for i in range(NX):
            xi = (x + i) % NX
            if s == 0 and i > 0:
                x_copies[3 - i].wait_recv()
            for d, q in ((0, up), (1, down)):
                if s > 0 and (d, s - 1, i) in z_copies:
                    z_copies[d, s - 1, i].wait_recv()
                if s < 3 or (i < 2) == (d == 0):
                    zs = (z - s + NZ) % NZ if d == 0 else (z + s) % NZ
                    a = send(xp.at[zs, xi], xp.at[zs, xi], z_send.at[d, s, i], z_recv.at[d, s, i], *q)
                    a.start()
                    z_copies[d, s, i] = a
        if s == 0:
            for i, yi in enumerate(((y + 3) % NY, (y + 1) % NY, (y + 2) % NY)):
                wy_copies[i].wait_recv()
                for j, q in enumerate(xs):
                    ref = full.at[:, rows(yi, x)]
                    a = send(ref, ref, wx_send.at[i, j], wx_recv.at[i, j], *q)
                    a.start()
                    wx_copies.append(a)
        if s == 2:
            for i, yi in enumerate(((y + 3) % NY, (y + 1) % NY, (y + 2) % NY)):
                for j in range(3):
                    wx_copies[i * 3 + j].wait_recv()
                ref = full.at[:, pl.ds(pl.multiple_of(yi * 128 + p * 64, 64), 64)]
                a = send(ref, ref, wc_send.at[i], wc_recv.at[i], *core)
                a.start()
                wc_copies.append(a)
    for (d, s, i), a in z_copies.items():
        if s == 3:
            a.wait_recv()
    for a in x_copies + list(z_copies.values()) + wy_copies + wx_copies:
        a.wait_send()
    for a in own_copies + wc_copies + tile_copies:
        a.wait()


def deal(owner, source, target, relation, count, tiles, states, weights):
    return pl.pallas_call(
        deal_kernel,
        out_shape=(
            jax.ShapeDtypeStruct((NC, SLOTS, TILE, TILE), BF),
            jax.ShapeDtypeStruct((NC, 8, 128), jnp.int32),
            jax.ShapeDtypeStruct((NZ, NX, ROWS, D), BF),
            jax.ShapeDtypeStruct((REL + 1, D, D), BF),
        ),
        in_specs=[IN_HBM] * 8,
        out_specs=(ANY,) * 4,
        scratch_shapes=[
            pltpu.VMEM((4, NZ * NX, EB), jnp.int32),
            pltpu.VMEM((1, NZ * NX), jnp.int32),
            pltpu.VMEM((EB, TILE, TILE), BF),
            pltpu.VMEM((NC * 4, 128), jnp.int32),
            pltpu.SMEM((NC * 4, 128), jnp.int32),
            pltpu.VMEM((NC, 8, 128), jnp.int32),
            pltpu.VMEM((NC, SLOTS, TILE, TILE), BF),
            DMA((7,)), DMA((4,)), DMA((7,)), DMA((7,)), DMA((7,)), DMA((7,)), DMA(()), DMA(()),
            DMA((3,)), DMA((3,)), DMA((2, 4, 4)), DMA((2, 4, 4)),
            DMA((3,)), DMA((3,)), DMA((3, 3)), DMA((3, 3)), DMA((3,)), DMA((3,)),
        ],
        compiler_params=params(8, 0),
    )(owner, source, target, relation, count, tiles, states, weights)


def adjacency_kernel(meta, tiles, adj):
    adj[...] = jnp.zeros_like(adj)

    def slots(c, carry):
        for s in range(SLOTS):
            code = meta[c, s // 2, s % 2]

            @pl.when(code >= 0)
            def _():
                row = pl.ds(pl.multiple_of((code >> 2) * TILE, TILE), TILE)
                column = pl.ds(pl.multiple_of(((s // 2) * 4 + (code & 3)) * TILE, TILE), TILE)
                adj[row, column] += tiles[c, s]

        return carry

    lax.fori_loop(0, NC, slots, 0)


def adjacency(meta, tiles):
    return pl.pallas_call(
        adjacency_kernel,
        out_shape=jax.ShapeDtypeStruct((NY * REL * TILE, 16 * TILE), BF),
        in_specs=[SM, VM],
        out_specs=VM,
        compiler_params=params(6),
    )(meta, tiles)


def main_kernel(
    adj, xp, weights, states, cotangent,
    layer_o, own_o, v_buf, wa, wb,
    tq, tc_buf, ty_src, ty_buf, tg, m_own, m_src, m_buf, my_src, my_buf, slope_s, zs, gw,
    xw_src, xw_buf, zw_src, zw_buf, aw_buf, wb_src, g_in, g_src, g_buf, gx_src, gx_buf,
    bx_buf, b_src, b_buf, v_src,
    tc_s, tc_r, ty_s, ty_r, mc_s, mc_r, my_s, my_r, s_s, s_r, f_s, f_r,
    xw_s, xw_r, zw_s, zw_r, aw_s, aw_r, wa_s, wa_r, wb_s, wb_r, g_s, g_r, gx_s, gx_r,
    bx_s, bx_r, b_s, b_r, v_s, v_r,
):
    over_rows = (((0,), (0,)), ((), ()))
    over_columns = (((1,), (1,)), ((), ()))
    z, x, y, p = place()
    core = (z, x, y, 1 - p)
    shifts = (2, 1, 3)
    ys = [(z, x, (y + i) % NY, p) for i in shifts]
    senders = [(y + NY - i) % NY for i in shifts]
    xs = x_peers(z, x, y, p)
    xo = [(q[0], q[1], q[2], 1 - p) for q in xs]
    around = z_peers(z, x, y, p, (4, 3, 5, 2, 6, 1, 7))
    up, down = around[5], around[6]
    target, is_self = swap_of(z, x, y, p)
    arrived = greet([core] + ys + xs + xo + around, (target, is_self))
    c = y * 2 + p
    share = pl.ds(pl.multiple_of(c * ROWS, ROWS), ROWS)

    def half(v, mine):
        low, high = v[:ROWS], v[ROWS:]
        return jnp.where(p == (0 if mine else 1), low, high)

    order = [q[2] for q in ys] + [y]
    m_copies, t_copies, my_copies = [], [], []

    def messages_on(n):
        m_copies[n].wait_recv()
        t = order[n]
        my_src[n] = (m_own[t] + m_buf[t].astype(F32)).astype(BF)
        a = send(my_src.at[n], my_buf.at[n], my_s.at[n], my_r.at[n], *ys[n])
        a.start()
        my_copies.append(a)

    ty_copies = {}

    def transforms_on(n):
        t = order[n]
        t_copies[n].wait_recv()
        for j, q in enumerate(ys):
            yi = q[2]
            ty_src[j, t] = (tq[p, t, yi].astype(F32) + tc_buf[t, yi].astype(F32)).astype(BF)
            a = send(ty_src.at[j, t], ty_buf.at[j, t], ty_s.at[j, n], ty_r.at[j, n], *q)
            a.start()
            ty_copies[j, n] = a

    for n, t in enumerate(order):
        rows = pl.ds(pl.multiple_of(t * D, D), D)
        tt = jnp.dot(adj[rows, :], xp[...], preferred_element_type=F32).astype(BF)
        m = jnp.zeros((TILE, D), F32)
        for r in range(REL):
            part = tt[r * TILE : (r + 1) * TILE]
            m = m + jnp.dot(part, weights[r], preferred_element_type=F32)
            for q in range(NY):
                tq[r // 2, t, q, r % 2] = part[:, q * TILE : (q + 1) * TILE]
        m_own[t] = half(m, True)
        m_src[t] = half(m, False).astype(BF)
        if n == 0:
            arrived()
        a = send(m_src.at[t], m_buf.at[t], mc_s.at[n], mc_r.at[n], *core)
        a.start()
        m_copies.append(a)
        if n > 0:
            messages_on(n - 1)
        if n == 1:
            transforms_on(0)
        a = send(tq.at[1 - p, t], tc_buf.at[t], tc_s.at[n], tc_r.at[n], *core)
        a.start()
        t_copies.append(a)

    transforms_on(1)

    w_self = weights[REL]
    pre = jnp.dot(states[share, :], w_self, preferred_element_type=F32)
    m_copies[3].wait_recv()
    pre = pre + m_own[y] + m_buf[y].astype(F32)
    for n, a in enumerate(my_copies):
        a.wait_recv()
        pre = pre + my_buf[n].astype(F32)
    sigma = jax.nn.sigmoid(pre)
    slope = (cotangent[share, :].astype(F32) * (sigma * (1.0 + pre * (1.0 - sigma)))).astype(BF)
    slope_s[c] = slope
    mine = slope_s.at[c]
    s_copies = []
    for i, q in enumerate(ys + [core]):
        a = send(mine, mine, s_s.at[i], s_r.at[i], *q)
        a.start()
        s_copies.append(a)
    for n in (2, 3):
        transforms_on(n)
    layer_o[...] = pre * sigma
    own_o[...] = lax.dot_general(slope, w_self, over_columns, preferred_element_type=F32)
    f_copies = []
    for i in (1, 2, 0):
        s_copies[i].wait_recv()
        ref = slope_s.at[senders[i] * 2 + p]
        a = send(ref, ref, f_s.at[i], f_r.at[i], *core)
        a.start()
        f_copies.append(a)
    s_copies[3].wait_recv()
    for a in f_copies:
        a.wait_recv()

    whole = slope_s[...].reshape(D, D)
    for r in range(REL):
        part = lax.dot_general(whole, weights[r], over_columns, preferred_element_type=F32)
        part = part.astype(BF)
        for t in range(NY):
            zs[t * D + r * TILE : t * D + (r + 1) * TILE, :] = part[t * TILE : (t + 1) * TILE]

    def gradients(k):
        columns = pl.ds(pl.multiple_of(k * D, D), D)
        part = lax.dot_general(adj[:, columns], zs[...], over_rows, preferred_element_type=F32)
        part = part.astype(BF)
        for b in range(4):
            for h in range(2):
                row = b * TILE + h * ROWS
                g_in[2 * k + h, b] = part[row : row + ROWS]

    g_copies = {}
    hops = {(d, i): 4 if (i < 2) == (d == 0) else 3 for d in range(2) for i in range(NX)}

    def toward(d, left):
        return (z + left) % NZ if d == 0 else (z - left + NZ) % NZ

    def chain(s):
        for i in range(NX):
            xi = (x + i) % NX
            for d, q in ((0, up), (1, down)):
                left = hops[d, i] - s
                if left <= 0:
                    continue
                zd = toward(d, left)
                if s == 0:
                    src = g_in.at[zd, xi, pl.ds(0, HA)]
                else:
                    g_copies[d, s - 1, i].wait_recv()
                    g_src[d, s - 1, i] = (
                        g_in[zd, xi, :HA].astype(F32) + g_buf[d, s - 1, i].astype(F32)
                    ).astype(BF)
                    src = g_src.at[d, s - 1, i]
                a = send(src, g_buf.at[d, s, i], g_s.at[d, s, i], g_r.at[d, s, i], *q)
                a.start()
                g_copies[d, s, i] = a

    bx_copies = {}
    b_copies = {}

    def across(n, k):
        two = pl.ds(2 * k, 2)
        for j, q in enumerate(xs):
            a = send(
                g_in.at[two, q[1], pl.ds(HA, HB)], bx_buf.at[j, two], bx_s.at[j, n], bx_r.at[j, n], *q
            )
            a.start()
            bx_copies[j, n] = a

    def across_wait(n):
        for j in range(3):
            bx_copies[j, n].wait_recv()

    def x_sum(zd, h):
        columns = slice(h * 256, (h + 1) * 256)
        total = g_in[zd, x, HA:, columns].astype(F32)
        for j in range(3):
            total = total + bx_buf[j, zd, :, columns].astype(F32)
        return total

    def second_chain(s):
        for h in range(2):
            for d, q in ((0, up), (1, down)):
                left = (4 if h == d else 3) - s
                if left <= 0:
                    continue
                total = x_sum(toward(d, left), h)
                if s > 0:
                    b_copies[d, s - 1, h].wait_recv()
                    total = total + b_buf[d, s - 1, h].astype(F32)
                b_src[d, s, h] = total.astype(BF)
                a = send(b_src.at[d, s, h], b_buf.at[d, s, h], b_s.at[d, s, h], b_r.at[d, s, h], *q)
                a.start()
                b_copies[d, s, h] = a

    pair = z // 2
    odd = 2 * (z % 2)
    near = ((pair + 2) % 4, (pair + 1 + odd) % 4, (pair + 3 + odd) % 4, pair)
    for n in (0, 1):
        gradients(near[n])
        across(n, near[n])
    chain(0)
    gradients(near[2])
    across(2, near[2])
    chain(1)
    gradients(near[3])
    across(3, near[3])
    across_wait(0)
    across_wait(1)
    second_chain(0)

    for a in ty_copies.values():
        a.wait_recv()
    for t in range(NY):
        total = tq[p, t, y].astype(F32) + tc_buf[t, y].astype(F32)
        for j in range(3):
            total = total + ty_buf[j, t].astype(F32)
        for r in range(2):
            tg[r, t * TILE : (t + 1) * TILE, :] = total[r].astype(BF)
    parts = [
        lax.dot_general(tg[r], whole, over_rows, preferred_element_type=F32) for r in range(2)
    ]
    columns = pl.ds(pl.multiple_of(y * TILE, TILE), TILE)
    self_part = lax.dot_general(states[:, columns], whole, over_rows, preferred_element_type=F32)
    rows_of = [half(v, True) for v in parts] + [half(self_part, True)] + [half(v, False) for v in parts]
    for m, v in enumerate(rows_of):
        for q in range(NX):
            gw[q, m * ROWS : (m + 1) * ROWS, :] = v[:, q * WC : (q + 1) * WC]
    xw_copies = []
    for i in range(3):
        xw_src[i] = gw[xs[i][1]].astype(BF)
        a = send(xw_src.at[i], xw_buf.at[i], xw_s.at[i], xw_r.at[i], *xs[i])
        a.start()
        xw_copies.append(a)
    chain(2)
    across_wait(2)
    second_chain(1)
    total = gw[x]
    for i, a in enumerate(xw_copies):
        a.wait_recv()
        total = total + xw_buf[i].astype(F32)
    padding = jnp.zeros((NZ, ZROWS - WROWS // NZ, WC), F32)
    zw_src[...] = jnp.concatenate(
        [total.reshape(NZ, WROWS // NZ, WC), padding], axis=1
    ).astype(BF)
    zw_copies = []
    for i, q in enumerate(around):
        a = send(zw_src.at[q[0]], zw_buf.at[i], zw_s.at[i], zw_r.at[i], *q)
        a.start()
        zw_copies.append(a)
    chain(3)
    across_wait(3)
    second_chain(2)
    total = zw_src[z].astype(F32)
    for i, a in enumerate(zw_copies):
        a.wait_recv()
        total = total + zw_buf[i].astype(F32)
    aw_buf[z] = total.astype(BF)
    aw_copies = []
    for i, q in enumerate(around):
        a = send(aw_buf.at[z], aw_buf.at[z], aw_s.at[i], aw_r.at[i], *q)
        a.start()
        aw_copies.append(a)

    second_chain(3)
    gx_copies = []
    own = None
    for i in (1, 2, 3, 0):
        xi = (x + i) % NX
        part = g_in[z, xi, :HA].astype(F32)
        for d in range(2):
            last = hops[d, i] - 1
            g_copies[d, last, i].wait_recv()
            part = part + g_buf[d, last, i].astype(F32)
        if i:
            gx_src[i - 1] = part.astype(BF)
            a = send(gx_src.at[i - 1], gx_buf.at[i - 1], gx_s.at[i - 1], gx_r.at[i - 1], *xs[i - 1])
            a.start()
            gx_copies.append(a)
        else:
            own = part

    for a in aw_copies:
        a.wait_recv()
    done = aw_buf[...].astype(F32)[:, : WROWS // NZ].reshape(WROWS, WC).astype(BF)
    wa[x] = done[: 3 * ROWS]
    wb_src[...] = done[3 * ROWS :]
    w_copies = []
    for i, q in enumerate(xs):
        w_copies.append(send(wa.at[x], wa.at[x], wa_s.at[i], wa_r.at[i], *q))
    for i, q in enumerate(xo + [core]):
        w_copies.append(send(wb_src, wb.at[x], wb_s.at[i], wb_r.at[i], *q))
    for a in w_copies:
        a.start()

    for i, a in enumerate(gx_copies):
        a.wait_recv()
        own = own + gx_buf[i].astype(F32)
    v_src[:HA] = own.astype(BF)
    for h in range(2):
        part = x_sum(z, h)
        for d in range(2):
            last = (4 if h == d else 3) - 1
            b_copies[d, last, h].wait_recv()
            part = part + b_buf[d, last, h].astype(F32)
        v_src[HA:, h * 256 : (h + 1) * 256] = part.astype(BF)

    @pl.when(jnp.logical_not(is_self))
    def _():
        a = send(v_src, v_buf, v_s, v_r, *target)
        a.start()
        a.wait()

    @pl.when(is_self)
    def _():
        v_buf[...] = v_src[...]

    for a in w_copies:
        a.wait()
    for a in m_copies + t_copies + my_copies + s_copies + f_copies:
        a.wait_send()
    for a in xw_copies + zw_copies + aw_copies + gx_copies:
        a.wait_send()
    for some in (ty_copies, g_copies, bx_copies, b_copies):
        for a in some.values():
            a.wait_send()


def main(adj, xp, weights, states, cotangent):
    return pl.pallas_call(
        main_kernel,
        out_shape=(
            jax.ShapeDtypeStruct((ROWS, D), F32),
            jax.ShapeDtypeStruct((ROWS, D), F32),
            jax.ShapeDtypeStruct((ROWS, D), BF),
            jax.ShapeDtypeStruct((NX, 3 * ROWS, WC), BF),
            jax.ShapeDtypeStruct((NX, 2 * ROWS, WC), BF),
        ),
        in_specs=[VM] * 5,
        out_specs=(VM,) * 5,
        scratch_shapes=[
            pltpu.VMEM((2, NY, NY, 2, TILE, TILE), BF),
            pltpu.VMEM((NY, NY, 2, TILE, TILE), BF),
            pltpu.VMEM((3, NY, 2, TILE, TILE), BF),
            pltpu.VMEM((3, NY, 2, TILE, TILE), BF),
            pltpu.VMEM((2, D, TILE), BF),
            pltpu.VMEM((NY, ROWS, D), F32),
            pltpu.VMEM((NY, ROWS, D), BF),
            pltpu.VMEM((NY, ROWS, D), BF),
            pltpu.VMEM((3, ROWS, D), BF),
            pltpu.VMEM((3, ROWS, D), BF),
            pltpu.VMEM((NC, ROWS, D), BF),
            pltpu.VMEM((NY * D, D), BF),
            pltpu.VMEM((NX, WROWS, WC), F32),
            pltpu.VMEM((3, WROWS, WC), BF),
            pltpu.VMEM((3, WROWS, WC), BF),
            pltpu.VMEM((NZ, ZROWS, WC), BF),
            pltpu.VMEM((7, ZROWS, WC), BF),
            pltpu.VMEM((NZ, ZROWS, WC), BF),
            pltpu.VMEM((2 * ROWS, WC), BF),
            pltpu.VMEM((NZ, NX, ROWS, D), BF),
            pltpu.VMEM((2, 3, NX, HA, D), BF),
            pltpu.VMEM((2, 4, NX, HA, D), BF),
            pltpu.VMEM((3, HA, D), BF),
            pltpu.VMEM((3, HA, D), BF),
            pltpu.VMEM((3, NZ, HB, D), BF),
            pltpu.VMEM((2, 4, 2, HB, 256), BF),
            pltpu.VMEM((2, 4, 2, HB, 256), BF),
            pltpu.VMEM((ROWS, D), BF),
            DMA((4,)), DMA((4,)), DMA((3, 4)), DMA((3, 4)), DMA((4,)), DMA((4,)), DMA((3,)), DMA((3,)),
            DMA((4,)), DMA((4,)), DMA((3,)), DMA((3,)),
            DMA((3,)), DMA((3,)), DMA((7,)), DMA((7,)), DMA((7,)), DMA((7,)), DMA((3,)), DMA((3,)),
            DMA((4,)), DMA((4,)), DMA((2, 4, 4)), DMA((2, 4, 4)), DMA((3,)), DMA((3,)),
            DMA((3, 4)), DMA((3, 4)), DMA((2, 4, 2)), DMA((2, 4, 2)), DMA(()), DMA(()),
        ],
        compiler_params=params(32, 1),
    )(adj, xp, weights, states, cotangent)


def close_kernel(layer, own, v, wa, wb, layer_o, g_o, w_o):
    p = lax.axis_index("replica")
    layer_o[...] = layer[...]
    g_o[...] = own[...] + v[...].astype(F32)
    for q in range(NX):
        columns = slice(q * WC, (q + 1) * WC)
        for m in range(2):
            a = wa[q, m * ROWS : (m + 1) * ROWS, :].astype(F32)
            b = wb[q, m * ROWS : (m + 1) * ROWS, :].astype(F32)
            w_o[m, :, columns] = jnp.where(p == 0, a, b)
            w_o[2 + m, :, columns] = jnp.where(p == 0, b, a)
        w_o[REL, :, columns] = wa[q, 2 * ROWS :, :].astype(F32)


def close(layer, own, v, wa, wb):
    return pl.pallas_call(
        close_kernel,
        out_shape=(
            jax.ShapeDtypeStruct((ROWS, D), F32),
            jax.ShapeDtypeStruct((ROWS, D), F32),
            jax.ShapeDtypeStruct((REL + 1, ROWS, D), F32),
        ),
        in_specs=[VM] * 5,
        out_specs=(VM, VM, VM),
        compiler_params=params(8),
    )(layer, own, v, wa, wb)


def shards(
    states,
    weights,
    edge_tiles,
    edge_owner,
    edge_source,
    edge_target,
    edge_relation,
    edge_count,
    cotangent,
):
    groups = edge_owner.shape[0]
    owner = edge_owner.reshape(groups, EB)
    source = edge_source.reshape(groups, EB)
    target = edge_target.reshape(groups, EB)
    relation = edge_relation.reshape(groups, EB)
    count = edge_count.reshape(1, groups)
    tiles = edge_tiles.reshape(EB, TILE, TILE)
    given = (owner, source, target, relation, count, tiles, states, weights)
    given = (pltpu.with_memory_space_constraint(v, pltpu.HBM) for v in given)
    tiles, meta, xp, full = deal(*given)
    adj = adjacency(meta, tiles)
    layer, own, v, wa, wb = main(adj, xp.reshape(-1, D), full, states, cotangent)
    return close(layer, own, v, wa, wb)


def solution(mesh):
    return jax.shard_map(
        shards,
        mesh=mesh,
        in_specs=(
            P("graph", None),
            P(None, "fsdp", None),
            P("graph", "fsdp", "replica", None, None, None),
            P(None, "fsdp", "replica", None),
            P(None, "fsdp", "replica", None),
            P(None, "fsdp", "replica", None),
            P(None, "fsdp", "replica", None),
            P(None, "fsdp", "replica"),
            P("graph", None),
        ),
        out_specs=(
            P(("graph", "fsdp", "replica"), None),
            P(("graph", "fsdp", "replica"), None),
            P(None, ("fsdp", "replica"), None),
        ),
        check_vma=False,
    )
```

```python
import jax
import jax.numpy as jnp
from jax import lax
from jax.experimental import pallas as pl
from jax.experimental.pallas import tpu as pltpu
from jax.sharding import PartitionSpec as P

D = 512
REL = 4
TILE = 128
EB = 48
NZ = 8
NX = 4
NY = 4
NC = 8
SLOTS = 8
ROWS = 64
PART = (128, 192)
EIGHTH = (16, 32)
HA = 48
HB = ROWS - HA
WC = 128
BF = jnp.bfloat16
F32 = jnp.float32
MESH = pl.DeviceIdType.MESH
ANY = pl.BlockSpec(memory_space=pl.ANY)
VM = pl.BlockSpec(memory_space=pltpu.VMEM)
SM = pl.BlockSpec(memory_space=pltpu.SMEM)
IN_HBM = pl.BlockSpec(memory_space=pltpu.HBM)
DMA = pltpu.SemaphoreType.DMA


def params(mib, collective=None):
    more = {} if collective is None else {"collective_id": collective, "has_side_effects": True}
    return pltpu.CompilerParams(vmem_limit_bytes=mib * 1024 * 1024, **more)


def place():
    g = lax.axis_index("graph")
    return g // NX, g % NX, lax.axis_index("fsdp"), lax.axis_index("replica")


def send(src, dst, ssem, rsem, z, x, y, p):
    return pltpu.make_async_remote_copy(
        src_ref=src,
        dst_ref=dst,
        send_sem=ssem,
        recv_sem=rsem,
        device_id=(z * NX + x, y, p),
        device_id_type=MESH,
    )


def greet(partners, swap=None):
    barrier = pltpu.get_barrier_semaphore()
    for z, x, y, p in partners:
        pl.semaphore_signal(barrier, inc=1, device_id=(z * NX + x, y, p), device_id_type=MESH)
    count = len(partners)
    if swap is not None:
        (z, x, y, p), is_self = swap

        @pl.when(jnp.logical_not(is_self))
        def _():
            pl.semaphore_signal(barrier, inc=1, device_id=(z * NX + x, y, p), device_id_type=MESH)

        count = count + jnp.where(is_self, 0, 1)
    return lambda: pl.semaphore_wait(barrier, count)


def group_peers(z, x, y, p):
    return [
        (z, x, (y + dy) % NY, (p + dp) % 2)
        for dy, dp in ((0, 1), (1, 0), (3, 0), (1, 1), (3, 1), (2, 0), (2, 1))
    ]


def y_peers(z, x, y, p):
    return [(z, x, (y + i) % NY, p) for i in (1, 3, 2)]


def x_peers(z, x, y, p):
    return [(z, (x + i) % NX, y, p) for i in (1, 2, 3)]


def z_peers(z, x, y, p, steps=(1, 7)):
    return [((z + i) % NZ, x, y, p) for i in steps]


def swap_of(z, x, y, p):
    return (2 * (z // 2) + p, y, x, z % 2), (x == y) & (z % 2 == p)


def deal_kernel(
    owner, source, target_h, relation, count, tiles, states, weights, tiles_o, meta_o, xp, full, zeros,
    edges, counts, tiles_v, idx_v, idx, meta, packed,
    e_sems, own_sems, t_send, t_recv, m_send, m_recv, v_send, v_recv, x_send, x_recv, z_send, z_recv,
    wy_send, wy_recv, wx_send, wx_recv, wc_send, wc_recv,
):
    z, x, y, p = place()
    peers = group_peers(z, x, y, p)
    core, ys = peers[0], y_peers(z, x, y, p)
    xs = x_peers(z, x, y, p)
    up, down = z_peers(z, x, y, p)
    target, is_self = swap_of(z, x, y, p)
    loads = [
        pltpu.make_async_copy(h, edges.at[i], e_sems.at[i])
        for i, h in enumerate((owner, source, target_h, relation))
    ]
    loads.append(pltpu.make_async_copy(count, counts, e_sems.at[4]))
    for a in loads:
        a.start()
    load_tiles = pltpu.make_async_copy(tiles, tiles_v, e_sems.at[5])
    load_tiles.start()
    arrived = greet(peers + xs + [up, down], (target, is_self))
    c = y * 2 + p
    piece = states.at[pl.ds(pl.multiple_of((p * NY + y) * ROWS, ROWS), ROWS)]

    arrived()

    @pl.when(jnp.logical_not(is_self))
    def _():
        send(piece, xp.at[target[0], target[1]], v_send, v_recv, *target).start()

    @pl.when(is_self)
    def _():
        pltpu.make_async_copy(piece, xp.at[z, x], own_sems.at[0]).start()

    def rows(yi, xi):
        return pl.ds(pl.multiple_of(yi * 128 + p * 64 + xi * 16, 16), 16)

    wy_copies = []
    mine_w = weights.at[:, pl.ds(pl.multiple_of(p * 64 + x * 16, 16), 16)]
    for i, q in enumerate(ys):
        a = send(mine_w, full.at[:, rows(y, x)], wy_send.at[i], wy_recv.at[i], *q)
        a.start()
        wy_copies.append(a)

    own_w = pltpu.make_async_copy(
        weights, full.at[:, pl.ds(pl.multiple_of(y * 128, 128), 128)], own_sems.at[3]
    )
    own_w.start()

    for a in loads:
        a.wait()
    g = lax.axis_index("graph")
    e = lax.broadcasted_iota(jnp.int32, (NC * 4, EB), 1)
    row = lax.broadcasted_iota(jnp.int32, (NC * 4, EB), 0)
    wanted = (2 * (row & 3) + ((row >> 2) & 1)) * NX + (row >> 3)
    groups = lax.broadcasted_iota(jnp.int32, (1, NZ * NX), 1)
    live = jnp.sum(jnp.where(groups == g, counts[...], 0), axis=1, keepdims=True)
    own, src, dst, rel = (edges[i, pl.ds(g, 1), :] for i in range(4))
    code = src + 4 * (dst * REL + rel)
    hit = (own == wanted) & (e < live)
    first = jnp.min(jnp.where(hit, e, EB), axis=1, keepdims=True)
    last = jnp.max(jnp.where(hit, e, -1), axis=1, keepdims=True)
    code0 = jnp.sum(jnp.where(hit & (e == first), code, 0), axis=1, keepdims=True)
    code1 = jnp.sum(jnp.where(hit & (e == last), code, 0), axis=1, keepdims=True)
    code0 = jnp.where(first < EB, code0, -1)
    code1 = jnp.where(last > first, code1, -1)
    lane = lax.broadcasted_iota(jnp.int32, (NC * 4, 128), 1)
    idx_v[...] = jnp.where(lane == 0, jnp.minimum(first, EB - 1), jnp.maximum(last, 0))
    codes = jnp.where(lane == 0, code0, code1)
    meta[...] = jnp.full(meta.shape, -1, jnp.int32)
    for i in range(NC):
        meta[i, 0:4, :] = codes[i * 4 : i * 4 + 4]
    to_scalars = pltpu.make_async_copy(idx_v, idx, e_sems.at[6])
    to_scalars.start()
    to_scalars.wait()
    load_tiles.wait()

    def put(ci):
        def one(s, carry):
            packed[ci, s] = tiles_v[idx[ci * 4 + s // 2, s % 2]]
            return carry

        lax.fori_loop(0, SLOTS, one, 0)

    x_copies = [
        send(xp.at[z, x], xp.at[z, x], x_send.at[i], x_recv.at[i], *q) for i, q in enumerate(xs)
    ]

    def x_phase():
        @pl.when(jnp.logical_not(is_self))
        def _():
            send(piece, xp.at[z, x], v_send, v_recv, *target).wait()

        @pl.when(is_self)
        def _():
            pltpu.make_async_copy(piece, xp.at[z, x], own_sems.at[0]).wait()

        for a in x_copies:
            a.start()

    tile_copies = []
    for i, q in enumerate(peers):
        if i == 3:
            x_phase()
        cq = q[2] * 2 + q[3]
        put(cq)
        a = send(packed.at[cq], tiles_o.at[c], t_send.at[i], t_recv.at[i], *q)
        b = send(meta.at[cq], meta_o.at[c], m_send.at[i], m_recv.at[i], *q)
        a.start()
        b.start()
        tile_copies += [a, b]
    put(c)
    own_copies = [
        pltpu.make_async_copy(packed.at[c], tiles_o.at[c], own_sems.at[1]),
        pltpu.make_async_copy(meta.at[c], meta_o.at[c], own_sems.at[2]),
    ]
    for a in own_copies:
        a.start()
    own_copies.append(own_w)

    zeros[...] = jnp.zeros_like(zeros)

    wx_copies = []
    wc_copies = []
    z_copies = {}
    for s in range(4):
        for i in range(NX):
            xi = (x + i) % NX
            if s == 0 and i > 0:
                x_copies[3 - i].wait_recv()
            for d, q in ((0, up), (1, down)):
                if s > 0 and (d, s - 1, i) in z_copies:
                    z_copies[d, s - 1, i].wait_recv()
                if s < 3 or (i < 2) == (d == 0):
                    zs = (z - s + NZ) % NZ if d == 0 else (z + s) % NZ
                    a = send(xp.at[zs, xi], xp.at[zs, xi], z_send.at[d, s, i], z_recv.at[d, s, i], *q)
                    a.start()
                    z_copies[d, s, i] = a
        if s == 0:
            for i, yi in enumerate(((y + 3) % NY, (y + 1) % NY, (y + 2) % NY)):
                wy_copies[i].wait_recv()
                for j, q in enumerate(xs):
                    ref = full.at[:, rows(yi, x)]
                    a = send(ref, ref, wx_send.at[i, j], wx_recv.at[i, j], *q)
                    a.start()
                    wx_copies.append(a)
        if s == 2:
            for i, yi in enumerate(((y + 3) % NY, (y + 1) % NY, (y + 2) % NY)):
                for j in range(3):
                    wx_copies[i * 3 + j].wait_recv()
                ref = full.at[:, pl.ds(pl.multiple_of(yi * 128 + p * 64, 64), 64)]
                a = send(ref, ref, wc_send.at[i], wc_recv.at[i], *core)
                a.start()
                wc_copies.append(a)
    for (d, s, i), a in z_copies.items():
        if s == 3:
            a.wait_recv()
    for a in x_copies + list(z_copies.values()) + wy_copies + wx_copies:
        a.wait_send()
    for a in own_copies + wc_copies + tile_copies:
        a.wait()


def deal(owner, source, target, relation, count, tiles, states, weights):
    return pl.pallas_call(
        deal_kernel,
        out_shape=(
            jax.ShapeDtypeStruct((NC, SLOTS, TILE, TILE), BF),
            jax.ShapeDtypeStruct((NC, 8, 128), jnp.int32),
            jax.ShapeDtypeStruct((NZ, NX, ROWS, D), BF),
            jax.ShapeDtypeStruct((REL + 1, D, D), BF),
            jax.ShapeDtypeStruct((NY * REL * TILE, 16 * TILE), BF),
        ),
        in_specs=[IN_HBM] * 8,
        out_specs=(ANY,) * 4 + (VM,),
        scratch_shapes=[
            pltpu.VMEM((4, NZ * NX, EB), jnp.int32),
            pltpu.VMEM((1, NZ * NX), jnp.int32),
            pltpu.VMEM((EB, TILE, TILE), BF),
            pltpu.VMEM((NC * 4, 128), jnp.int32),
            pltpu.SMEM((NC * 4, 128), jnp.int32),
            pltpu.VMEM((NC, 8, 128), jnp.int32),
            pltpu.VMEM((NC, SLOTS, TILE, TILE), BF),
            DMA((7,)), DMA((4,)), DMA((7,)), DMA((7,)), DMA((7,)), DMA((7,)), DMA(()), DMA(()),
            DMA((3,)), DMA((3,)), DMA((2, 4, 4)), DMA((2, 4, 4)),
            DMA((3,)), DMA((3,)), DMA((3, 3)), DMA((3, 3)), DMA((3,)), DMA((3,)),
        ],
        compiler_params=params(8, 0),
    )(owner, source, target, relation, count, tiles, states, weights)


def adjacency_kernel(meta, tiles, zeros, adj):
    del zeros

    def slots(c, carry):
        for s in range(SLOTS):
            code = meta[c, s // 2, s % 2]

            @pl.when(code >= 0)
            def _():
                row = pl.ds(pl.multiple_of((code >> 2) * TILE, TILE), TILE)
                column = pl.ds(pl.multiple_of(((s // 2) * 4 + (code & 3)) * TILE, TILE), TILE)
                adj[row, column] += tiles[c, s]

        return carry

    lax.fori_loop(0, NC, slots, 0)


def adjacency(meta, tiles, zeros):
    return pl.pallas_call(
        adjacency_kernel,
        out_shape=jax.ShapeDtypeStruct((NY * REL * TILE, 16 * TILE), BF),
        in_specs=[SM, VM, VM],
        out_specs=VM,
        input_output_aliases={2: 0},
        compiler_params=params(6),
    )(meta, tiles, zeros)


def main_kernel(
    adj, xp, weights, states, cotangent,
    layer_o, g_o, wa, wb,
    tq, tc_buf, ty_src, ty_buf, tg, m_own, m_src, m_buf, my_src, my_buf, slope_s, zs,
    gw_a, xw_src_a, xw_buf_a, zw_src_a, zw_buf_a, aw_buf_a,
    gw_b, xw_src_b, xw_buf_b, zw_src_b, zw_buf_b, aw_buf_b, wb_src, g_in, g_src, g_buf, gx_src, gx_buf,
    bx_buf, gb_src, gb_buf, v_src, v_buf,
    tc_s, tc_r, ty_s, ty_r, mc_s, mc_r, my_s, my_r, s_s, s_r, f_s, f_r,
    xw_s, xw_r, zw_s, zw_r, aw_s, aw_r, wa_s, wa_r, wb_s, wb_r, g_s, g_r, gx_s, gx_r, bx_s, bx_r, gb_s, gb_r, v_s, v_r,
):
    over_rows = (((0,), (0,)), ((), ()))
    over_columns = (((1,), (1,)), ((), ()))
    gw, xw_src, xw_buf = (gw_a, gw_b), (xw_src_a, xw_src_b), (xw_buf_a, xw_buf_b)
    zw_src, zw_buf, aw_buf = (zw_src_a, zw_src_b), (zw_buf_a, zw_buf_b), (aw_buf_a, aw_buf_b)
    z, x, y, p = place()
    core = (z, x, y, 1 - p)
    shifts = (2, 1, 3)
    ys = [(z, x, (y + i) % NY, p) for i in shifts]
    senders = [(y + NY - i) % NY for i in shifts]
    xs = x_peers(z, x, y, p)
    xo = [(q[0], q[1], q[2], 1 - p) for q in xs]
    around = z_peers(z, x, y, p, (4, 3, 5, 2, 6, 1, 7))
    up, down = around[5], around[6]
    target, is_self = swap_of(z, x, y, p)
    arrived = greet([core] + ys + xs + xo + around, (target, is_self))
    c = y * 2 + p
    share = pl.ds(pl.multiple_of(c * ROWS, ROWS), ROWS)

    def half(v, mine):
        low, high = v[:ROWS], v[ROWS:]
        return jnp.where(p == (0 if mine else 1), low, high)

    order = [q[2] for q in ys] + [y]
    m_copies, t_copies, my_copies = [], [], []

    def messages_on(n):
        m_copies[n].wait_recv()
        t = order[n]
        my_src[n] = (m_own[t] + m_buf[t].astype(F32)).astype(BF)
        a = send(my_src.at[n], my_buf.at[n], my_s.at[n], my_r.at[n], *ys[n])
        a.start()
        my_copies.append(a)

    ty_copies = {}

    def transforms_on(n, send_now=True):
        t = order[n]
        t_copies[n].wait_recv()
        for j, q in enumerate(ys):
            yi = q[2]
            ty_src[j, t] = (tq[p, t, yi].astype(F32) + tc_buf[t, yi].astype(F32)).astype(BF)
            if send_now:
                a = send(ty_src.at[j, t], ty_buf.at[j, t], ty_s.at[j, n, 0], ty_r.at[j, n, 0], *q)
                a.start()
                ty_copies[j, n, 0] = a

    def transforms_part(n, r):
        t = order[n]
        for j, q in enumerate(ys):
            a = send(
                ty_src.at[j, t, r], ty_buf.at[j, t, r], ty_s.at[j, n, r], ty_r.at[j, n, r], *q
            )
            a.start()
            ty_copies[j, n, r] = a

    for n, t in enumerate(order):
        rows = pl.ds(pl.multiple_of(t * D, D), D)
        tt = jnp.dot(adj[rows, :], xp[...], preferred_element_type=F32).astype(BF)
        m = jnp.zeros((TILE, D), F32)
        for r in range(REL):
            part = tt[r * TILE : (r + 1) * TILE]
            m = m + jnp.dot(part, weights[r], preferred_element_type=F32)
            for q in range(NY):
                tq[r // 2, t, q, r % 2] = part[:, q * TILE : (q + 1) * TILE]
        m_own[t] = half(m, True)
        m_src[t] = half(m, False).astype(BF)
        if n == 0:
            arrived()
        a = send(m_src.at[t], m_buf.at[t], mc_s.at[n], mc_r.at[n], *core)
        a.start()
        m_copies.append(a)
        if n > 0:
            messages_on(n - 1)
        if n == 1:
            transforms_on(0)
        a = send(tq.at[1 - p, t], tc_buf.at[t], tc_s.at[n], tc_r.at[n], *core)
        a.start()
        t_copies.append(a)

    transforms_on(1)

    w_self = weights[REL]
    pre = jnp.dot(states[share, :], w_self, preferred_element_type=F32)
    m_copies[3].wait_recv()
    pre = pre + m_own[y] + m_buf[y].astype(F32)
    for n, a in enumerate(my_copies):
        a.wait_recv()
        pre = pre + my_buf[n].astype(F32)
    sigma = jax.nn.sigmoid(pre)
    slope = (cotangent[share, :].astype(F32) * (sigma * (1.0 + pre * (1.0 - sigma)))).astype(BF)
    slope_s[c] = slope
    mine = slope_s.at[c]
    s_copies = []
    for i, q in enumerate(ys + [core]):
        a = send(mine, mine, s_s.at[i], s_r.at[i], *q)
        a.start()
        s_copies.append(a)
    for n in (2, 3):
        transforms_on(n, False)
        transforms_part(n, 0)
    for n in (2, 3):
        transforms_part(n, 1)
    layer_o[...] = pre * sigma
    g_o[...] = lax.dot_general(slope, w_self, over_columns, preferred_element_type=F32)
    f_copies = []
    for i in (1, 2, 0):
        s_copies[i].wait_recv()
        ref = slope_s.at[senders[i] * 2 + p]
        a = send(ref, ref, f_s.at[i], f_r.at[i], *core)
        a.start()
        f_copies.append(a)
    def transposed(core_of):
        rows = jnp.concatenate([slope_s[t * 2 + core_of] for t in range(NY)], axis=0)
        for r in range(REL):
            part = lax.dot_general(rows, weights[r], over_columns, preferred_element_type=F32)
            part = part.astype(BF)
            for t in range(NY):
                at = pl.multiple_of(t * D + r * TILE + core_of * ROWS, ROWS)
                zs[pl.ds(at, ROWS), :] = part[t * ROWS : (t + 1) * ROWS]

    transposed(p)
    s_copies[3].wait_recv()
    for a in f_copies:
        a.wait_recv()
    transposed(1 - p)
    whole = slope_s[...].reshape(D, D)

    def gradients(k):
        columns = pl.ds(pl.multiple_of(k * D, D), D)
        part = lax.dot_general(adj[:, columns], zs[...], over_rows, preferred_element_type=F32)
        part = part.astype(BF)
        for b in range(4):
            for h in range(2):
                row = b * TILE + h * ROWS
                g_in[2 * k + h, b] = part[row : row + ROWS]

    g_copies = {}
    hops = {(d, i): 4 if (i < 2) == (d == 0) else 3 for d in range(2) for i in range(NX)}

    def chain(s, only=(3, 4)):
        for i in range(NX):
            xi = (x + i) % NX
            for d, q in ((0, up), (1, down)):
                left = hops[d, i] - s
                if left <= 0 or hops[d, i] not in only:
                    continue
                zd = (z + left) % NZ if d == 0 else (z - left + NZ) % NZ
                if s == 0:
                    src = g_in.at[zd, xi, pl.ds(0, HA)]
                else:
                    g_copies[d, s - 1, i].wait_recv()
                    g_src[d, s - 1, i] = (
                        g_in[zd, xi, :HA].astype(F32) + g_buf[d, s - 1, i].astype(F32)
                    ).astype(BF)
                    src = g_src.at[d, s - 1, i]
                a = send(src, g_buf.at[d, s, i], g_s.at[d, s, i], g_r.at[d, s, i], *q)
                a.start()
                g_copies[d, s, i] = a

    bx_copies = {}

    def across(n):
        k = near[n]
        two = pl.ds(2 * k, 2)
        for j, q in enumerate(xs):
            a = send(
                g_in.at[two, q[1], pl.ds(HA, HB)], bx_buf.at[j, two], bx_s.at[j, n], bx_r.at[j, n], *q
            )
            a.start()
            bx_copies[j, n] = a

    def across_wait(n):
        for j in range(3):
            bx_copies[j, n].wait_recv()

    gb_copies = {}

    def x_sum(zd):
        total = g_in[zd, x, HA:].astype(F32)
        for j in range(3):
            total = total + bx_buf[j, zd].astype(F32)
        return total

    def second(i):
        zd = (z + i) % NZ
        gb_src[i] = x_sum(zd).astype(BF)
        a = send(gb_src.at[i], gb_buf.at[i], gb_s.at[i], gb_r.at[i], zd, x, y, p)
        a.start()
        gb_copies[i] = a

    pair = z // 2
    odd = 2 * (z % 2)
    near = ((pair + 2) % 4, (pair + 1 + odd) % 4, (pair + 3 + odd) % 4, pair)
    columns = pl.ds(pl.multiple_of(y * TILE, TILE), TILE)
    xw_copies, zw_copies, aw_copies, w_copies = [[], []], [[], []], [[], []], []

    def weight_part(r):
        for (j, n, q), a in ty_copies.items():
            if q == r:
                a.wait_recv()
        for t in range(NY):
            total = tq[p, t, y, r].astype(F32) + tc_buf[t, y, r].astype(F32)
            for j in range(3):
                total = total + ty_buf[j, t, r].astype(F32)
            tg[r, t * TILE : (t + 1) * TILE, :] = total.astype(BF)
        part = lax.dot_general(tg[r], whole, over_rows, preferred_element_type=F32)
        rows_of = [half(part, True), half(part, False)]
        if r == 1:
            part = lax.dot_general(states[:, columns], whole, over_rows, preferred_element_type=F32)
            rows_of.insert(1, half(part, True))
        for m, v in enumerate(rows_of):
            for q in range(NX):
                gw[r][q, m * ROWS : (m + 1) * ROWS, :] = v[:, q * WC : (q + 1) * WC]
        for i in range(3):
            xw_src[r][i] = gw[r][xs[i][1]].astype(BF)
            a = send(xw_src[r].at[i], xw_buf[r].at[i], xw_s.at[r, i], xw_r.at[r, i], *xs[i])
            a.start()
            xw_copies[r].append(a)

    def weight_x(r):
        total = gw[r][x]
        for i, a in enumerate(xw_copies[r]):
            a.wait_recv()
            total = total + xw_buf[r][i].astype(F32)
        total = total.reshape(NZ, PART[r] // NZ, WC)
        if EIGHTH[r] > PART[r] // NZ:
            padding = jnp.zeros((NZ, EIGHTH[r] - PART[r] // NZ, WC), F32)
            total = jnp.concatenate([total, padding], axis=1)
        zw_src[r][...] = total.astype(BF)
        for i, q in enumerate(around):
            a = send(zw_src[r].at[q[0]], zw_buf[r].at[i], zw_s.at[r, i], zw_r.at[r, i], *q)
            a.start()
            zw_copies[r].append(a)

    def weight_z(r):
        total = zw_src[r][z].astype(F32)
        for i, a in enumerate(zw_copies[r]):
            a.wait_recv()
            total = total + zw_buf[r][i].astype(F32)
        aw_buf[r][z] = total.astype(BF)
        for i, q in enumerate(around):
            a = send(aw_buf[r].at[z], aw_buf[r].at[z], aw_s.at[r, i], aw_r.at[r, i], *q)
            a.start()
            aw_copies[r].append(a)

    def weight_out(r):
        for a in aw_copies[r]:
            a.wait_recv()
        done = aw_buf[r][...].astype(F32)[:, : PART[r] // NZ].reshape(PART[r], WC).astype(BF)
        mine, other = pl.ds(r * ROWS, (r + 1) * ROWS), pl.ds(r * ROWS, ROWS)
        wa[x, mine, :] = done[: (r + 1) * ROWS]
        wb_src[other, :] = done[(r + 1) * ROWS :]
        for i, q in enumerate(xs):
            ref = wa.at[x, mine]
            w_copies.append(send(ref, ref, wa_s.at[r, i], wa_r.at[r, i], *q))
        for i, q in enumerate(xo + [core]):
            w_copies.append(
                send(wb_src.at[other], wb.at[x, other], wb_s.at[r, i], wb_r.at[r, i], *q)
            )
        for a in w_copies[-7:]:
            a.start()

    gradients(near[0])
    across(0)
    chain(0, (4,))
    gradients(near[1])
    across(1)
    chain(0, (3,))
    weight_part(0)
    gradients(near[2])
    across(2)
    chain(1)
    weight_part(1)
    gradients(near[3])
    across(3)
    weight_x(0)
    chain(2)
    across_wait(0)
    across_wait(1)
    for i in (4, 3, 5):
        second(i)
    weight_z(0)
    weight_x(1)
    chain(3)
    across_wait(2)
    for i in (2, 6):
        second(i)
    weight_out(0)
    weight_z(1)
    across_wait(3)
    for i in (1, 7):
        second(i)

    gx_copies = []
    own = None
    for i in (1, 2, 3, 0):
        xi = (x + i) % NX
        part = g_in[z, xi, :HA].astype(F32)
        for d in range(2):
            last = hops[d, i] - 1
            g_copies[d, last, i].wait_recv()
            part = part + g_buf[d, last, i].astype(F32)
        if i:
            gx_src[i - 1] = part.astype(BF)
            a = send(gx_src.at[i - 1], gx_buf.at[i - 1], gx_s.at[i - 1], gx_r.at[i - 1], *xs[i - 1])
            a.start()
            gx_copies.append(a)
        else:
            own = part

    weight_out(1)
    total = x_sum(z)
    for i, a in gb_copies.items():
        a.wait_recv()
        total = total + gb_buf[i].astype(F32)
    v_src[HA:] = total.astype(BF)
    for i, a in enumerate(gx_copies):
        a.wait_recv()
        own = own + gx_buf[i].astype(F32)
    v_src[:HA] = own.astype(BF)

    @pl.when(jnp.logical_not(is_self))
    def _():
        a = send(v_src, v_buf, v_s, v_r, *target)
        a.start()
        a.wait()

    @pl.when(is_self)
    def _():
        v_buf[...] = v_src[...]

    g_o[...] = g_o[...] + v_buf[...].astype(F32)
    for a in w_copies:
        a.wait()
    for a in m_copies + t_copies + my_copies + s_copies + f_copies:
        a.wait_send()
    for copies in xw_copies + zw_copies + aw_copies + [gx_copies]:
        for a in copies:
            a.wait_send()
    for some in (ty_copies, g_copies, bx_copies, gb_copies):
        for a in some.values():
            a.wait_send()


def main(adj, xp, weights, states, cotangent):
    return pl.pallas_call(
        main_kernel,
        out_shape=(
            jax.ShapeDtypeStruct((ROWS, D), F32),
            jax.ShapeDtypeStruct((ROWS, D), F32),
            jax.ShapeDtypeStruct((NX, 3 * ROWS, WC), BF),
            jax.ShapeDtypeStruct((NX, 2 * ROWS, WC), BF),
        ),
        in_specs=[VM] * 5,
        out_specs=(VM,) * 4,
        scratch_shapes=[
            pltpu.VMEM((2, NY, NY, 2, TILE, TILE), BF),
            pltpu.VMEM((NY, NY, 2, TILE, TILE), BF),
            pltpu.VMEM((3, NY, 2, TILE, TILE), BF),
            pltpu.VMEM((3, NY, 2, TILE, TILE), BF),
            pltpu.VMEM((2, D, TILE), BF),
            pltpu.VMEM((NY, ROWS, D), F32),
            pltpu.VMEM((NY, ROWS, D), BF),
            pltpu.VMEM((NY, ROWS, D), BF),
            pltpu.VMEM((3, ROWS, D), BF),
            pltpu.VMEM((3, ROWS, D), BF),
            pltpu.VMEM((NC, ROWS, D), BF),
            pltpu.VMEM((NY * D, D), BF),
            *(
                v
                for r in range(2)
                for v in (
                    pltpu.VMEM((NX, PART[r], WC), F32),
                    pltpu.VMEM((3, PART[r], WC), BF),
                    pltpu.VMEM((3, PART[r], WC), BF),
                    pltpu.VMEM((NZ, EIGHTH[r], WC), BF),
                    pltpu.VMEM((7, EIGHTH[r], WC), BF),
                    pltpu.VMEM((NZ, EIGHTH[r], WC), BF),
                )
            ),
            pltpu.VMEM((2 * ROWS, WC), BF),
            pltpu.VMEM((NZ, NX, ROWS, D), BF),
            pltpu.VMEM((2, 3, NX, HA, D), BF),
            pltpu.VMEM((2, 4, NX, HA, D), BF),
            pltpu.VMEM((3, HA, D), BF),
            pltpu.VMEM((3, HA, D), BF),
            pltpu.VMEM((3, NZ, HB, D), BF),
            pltpu.VMEM((NZ, HB, D), BF),
            pltpu.VMEM((NZ, HB, D), BF),
            pltpu.VMEM((ROWS, D), BF),
            pltpu.VMEM((ROWS, D), BF),
            DMA((4,)), DMA((4,)), DMA((3, 4, 2)), DMA((3, 4, 2)), DMA((4,)), DMA((4,)), DMA((3,)), DMA((3,)),
            DMA((4,)), DMA((4,)), DMA((3,)), DMA((3,)),
            DMA((2, 3)), DMA((2, 3)), DMA((2, 7)), DMA((2, 7)), DMA((2, 7)), DMA((2, 7)),
            DMA((2, 3)), DMA((2, 3)), DMA((2, 4)), DMA((2, 4)), DMA((2, 4, 4)), DMA((2, 4, 4)), DMA((3,)), DMA((3,)),
            DMA((3, 4)), DMA((3, 4)), DMA((8,)), DMA((8,)), DMA(()), DMA(()),
        ],
        compiler_params=params(32, 1),
    )(adj, xp, weights, states, cotangent)


def close_kernel(layer, g, wa, wb, layer_o, g_o, w_o):
    p = lax.axis_index("replica")
    layer_o[...] = layer[...]
    g_o[...] = g[...]
    for q in range(NX):
        columns = slice(q * WC, (q + 1) * WC)
        for m in range(2):
            a = wa[q, m * ROWS : (m + 1) * ROWS, :].astype(F32)
            b = wb[q, m * ROWS : (m + 1) * ROWS, :].astype(F32)
            w_o[m, :, columns] = jnp.where(p == 0, a, b)
            w_o[2 + m, :, columns] = jnp.where(p == 0, b, a)
        w_o[REL, :, columns] = wa[q, 2 * ROWS :, :].astype(F32)


def close(layer, g, wa, wb):
    return pl.pallas_call(
        close_kernel,
        out_shape=(
            jax.ShapeDtypeStruct((ROWS, D), F32),
            jax.ShapeDtypeStruct((ROWS, D), F32),
            jax.ShapeDtypeStruct((REL + 1, ROWS, D), F32),
        ),
        in_specs=[VM] * 4,
        out_specs=(VM, VM, VM),
        compiler_params=params(8),
    )(layer, g, wa, wb)


def shards(
    states,
    weights,
    edge_tiles,
    edge_owner,
    edge_source,
    edge_target,
    edge_relation,
    edge_count,
    cotangent,
):
    groups = edge_owner.shape[0]
    owner = edge_owner.reshape(groups, EB)
    source = edge_source.reshape(groups, EB)
    target = edge_target.reshape(groups, EB)
    relation = edge_relation.reshape(groups, EB)
    count = edge_count.reshape(1, groups)
    tiles = edge_tiles.reshape(EB, TILE, TILE)
    given = (owner, source, target, relation, count, tiles, states, weights)
    given = (pltpu.with_memory_space_constraint(v, pltpu.HBM) for v in given)
    tiles, meta, xp, full, zeros = deal(*given)
    adj = adjacency(meta, tiles, zeros)
    layer, g, wa, wb = main(adj, xp.reshape(-1, D), full, states, cotangent)
    return close(layer, g, wa, wb)


def solution(mesh):
    return jax.shard_map(
        shards,
        mesh=mesh,
        in_specs=(
            P("graph", None),
            P(None, "fsdp", None),
            P("graph", "fsdp", "replica", None, None, None),
            P(None, "fsdp", "replica", None),
            P(None, "fsdp", "replica", None),
            P(None, "fsdp", "replica", None),
            P(None, "fsdp", "replica", None),
            P(None, "fsdp", "replica"),
            P("graph", None),
        ),
        out_specs=(
            P(("graph", "fsdp", "replica"), None),
            P(("graph", "fsdp", "replica"), None),
            P(None, ("fsdp", "replica"), None),
        ),
        check_vma=False,
    )
```

```python
import jax
import jax.numpy as jnp
from jax import lax
from jax.experimental import pallas as pl
from jax.experimental.pallas import tpu as pltpu
from jax.sharding import PartitionSpec as P

D = 512
REL = 4
TILE = 128
EB = 48
NZ = 8
NX = 4
NY = 4
NC = 8
SLOTS = 8
ROWS = 64
PART = (128, 192)
EIGHTH = (16, 32)
HA = 48
HB = ROWS - HA
WC = 128
BF = jnp.bfloat16
F32 = jnp.float32
MESH = pl.DeviceIdType.MESH
ANY = pl.BlockSpec(memory_space=pl.ANY)
VM = pl.BlockSpec(memory_space=pltpu.VMEM)
SM = pl.BlockSpec(memory_space=pltpu.SMEM)
IN_HBM = pl.BlockSpec(memory_space=pltpu.HBM)
DMA = pltpu.SemaphoreType.DMA


def params(mib, collective=None):
    more = {} if collective is None else {"collective_id": collective, "has_side_effects": True}
    return pltpu.CompilerParams(vmem_limit_bytes=mib * 1024 * 1024, **more)


def place():
    g = lax.axis_index("graph")
    return g // NX, g % NX, lax.axis_index("fsdp"), lax.axis_index("replica")


def send(src, dst, ssem, rsem, z, x, y, p):
    return pltpu.make_async_remote_copy(
        src_ref=src,
        dst_ref=dst,
        send_sem=ssem,
        recv_sem=rsem,
        device_id=(z * NX + x, y, p),
        device_id_type=MESH,
    )


def greet(partners, swap=None):
    barrier = pltpu.get_barrier_semaphore()
    for z, x, y, p in partners:
        pl.semaphore_signal(barrier, inc=1, device_id=(z * NX + x, y, p), device_id_type=MESH)
    count = len(partners)
    if swap is not None:
        (z, x, y, p), is_self = swap

        @pl.when(jnp.logical_not(is_self))
        def _():
            pl.semaphore_signal(barrier, inc=1, device_id=(z * NX + x, y, p), device_id_type=MESH)

        count = count + jnp.where(is_self, 0, 1)
    return lambda: pl.semaphore_wait(barrier, count)


def group_peers(z, x, y, p):
    return [
        (z, x, (y + dy) % NY, (p + dp) % 2)
        for dy, dp in ((0, 1), (1, 0), (3, 0), (1, 1), (3, 1), (2, 0), (2, 1))
    ]


def y_peers(z, x, y, p):
    return [(z, x, (y + i) % NY, p) for i in (1, 3, 2)]


def x_peers(z, x, y, p):
    return [(z, (x + i) % NX, y, p) for i in (1, 2, 3)]


def z_peers(z, x, y, p, steps=(1, 7)):
    return [((z + i) % NZ, x, y, p) for i in steps]


def swap_of(z, x, y, p):
    return (2 * (z // 2) + p, y, x, z % 2), (x == y) & (z % 2 == p)


def deal_kernel(
    owner, source, target_h, relation, count, tiles, states, weights, tiles_o, meta_o, xp, full, zeros,
    edges, counts, tiles_v, idx_v, idx, meta, packed,
    e_sems, own_sems, t_send, t_recv, m_send, m_recv, v_send, v_recv, x_send, x_recv, z_send, z_recv,
    wy_send, wy_recv, wx_send, wx_recv, wc_send, wc_recv,
):
    z, x, y, p = place()
    peers = group_peers(z, x, y, p)
    core, ys = peers[0], y_peers(z, x, y, p)
    xs = x_peers(z, x, y, p)
    up, down = z_peers(z, x, y, p)
    target, is_self = swap_of(z, x, y, p)
    loads = [
        pltpu.make_async_copy(h, edges.at[i], e_sems.at[i])
        for i, h in enumerate((owner, source, target_h, relation))
    ]
    loads.append(pltpu.make_async_copy(count, counts, e_sems.at[4]))
    for a in loads:
        a.start()
    load_tiles = pltpu.make_async_copy(tiles, tiles_v, e_sems.at[5])
    load_tiles.start()
    arrived = greet(peers + xs + [up, down], (target, is_self))
    c = y * 2 + p
    piece = states.at[pl.ds(pl.multiple_of((p * NY + y) * ROWS, ROWS), ROWS)]

    arrived()

    @pl.when(jnp.logical_not(is_self))
    def _():
        send(piece, xp.at[target[0], target[1]], v_send, v_recv, *target).start()

    @pl.when(is_self)
    def _():
        pltpu.make_async_copy(piece, xp.at[z, x], own_sems.at[0]).start()

    def rows(yi, xi):
        return pl.ds(pl.multiple_of(yi * 128 + p * 64 + xi * 16, 16), 16)

    wy_copies = []
    mine_w = weights.at[:, pl.ds(pl.multiple_of(p * 64 + x * 16, 16), 16)]
    for i, q in enumerate(ys):
        a = send(mine_w, full.at[:, rows(y, x)], wy_send.at[i], wy_recv.at[i], *q)
        a.start()
        wy_copies.append(a)

    own_w = pltpu.make_async_copy(
        weights, full.at[:, pl.ds(pl.multiple_of(y * 128, 128), 128)], own_sems.at[3]
    )
    own_w.start()

    for a in loads:
        a.wait()
    g = lax.axis_index("graph")
    e = lax.broadcasted_iota(jnp.int32, (NC * 4, EB), 1)
    row = lax.broadcasted_iota(jnp.int32, (NC * 4, EB), 0)
    wanted = (2 * (row & 3) + ((row >> 2) & 1)) * NX + (row >> 3)
    groups = lax.broadcasted_iota(jnp.int32, (1, NZ * NX), 1)
    live = jnp.sum(jnp.where(groups == g, counts[...], 0), axis=1, keepdims=True)
    own, src, dst, rel = (edges[i, pl.ds(g, 1), :] for i in range(4))
    code = src + 4 * (dst * REL + rel)
    hit = (own == wanted) & (e < live)
    first = jnp.min(jnp.where(hit, e, EB), axis=1, keepdims=True)
    last = jnp.max(jnp.where(hit, e, -1), axis=1, keepdims=True)
    code0 = jnp.sum(jnp.where(hit & (e == first), code, 0), axis=1, keepdims=True)
    code1 = jnp.sum(jnp.where(hit & (e == last), code, 0), axis=1, keepdims=True)
    code0 = jnp.where(first < EB, code0, -1)
    code1 = jnp.where(last > first, code1, -1)
    lane = lax.broadcasted_iota(jnp.int32, (NC * 4, 128), 1)
    idx_v[...] = jnp.where(lane == 0, jnp.minimum(first, EB - 1), jnp.maximum(last, 0))
    codes = jnp.where(lane == 0, code0, code1)
    meta[...] = jnp.full(meta.shape, -1, jnp.int32)
    for i in range(NC):
        meta[i, 0:4, :] = codes[i * 4 : i * 4 + 4]
    to_scalars = pltpu.make_async_copy(idx_v, idx, e_sems.at[6])
    to_scalars.start()
    to_scalars.wait()
    load_tiles.wait()

    def put(ci):
        def one(s, carry):
            packed[ci, s] = tiles_v[idx[ci * 4 + s // 2, s % 2]]
            return carry

        lax.fori_loop(0, SLOTS, one, 0)

    x_copies = [
        send(xp.at[z, x], xp.at[z, x], x_send.at[i], x_recv.at[i], *q) for i, q in enumerate(xs)
    ]

    def x_phase():
        @pl.when(jnp.logical_not(is_self))
        def _():
            send(piece, xp.at[z, x], v_send, v_recv, *target).wait()

        @pl.when(is_self)
        def _():
            pltpu.make_async_copy(piece, xp.at[z, x], own_sems.at[0]).wait()

        for a in x_copies:
            a.start()

    tile_copies = []
    for i, q in enumerate(peers):
        if i == 3:
            x_phase()
        cq = q[2] * 2 + q[3]
        put(cq)
        a = send(packed.at[cq], tiles_o.at[c], t_send.at[i], t_recv.at[i], *q)
        b = send(meta.at[cq], meta_o.at[c], m_send.at[i], m_recv.at[i], *q)
        a.start()
        b.start()
        tile_copies += [a, b]
    put(c)
    own_copies = [
        pltpu.make_async_copy(packed.at[c], tiles_o.at[c], own_sems.at[1]),
        pltpu.make_async_copy(meta.at[c], meta_o.at[c], own_sems.at[2]),
    ]
    for a in own_copies:
        a.start()
    own_copies.append(own_w)

    zeros[...] = jnp.zeros_like(zeros)

    wx_copies = []
    wc_copies = []
    z_copies = {}
    for s in range(4):
        for i in range(NX):
            xi = (x + i) % NX
            if s == 0 and i > 0:
                x_copies[3 - i].wait_recv()
            for d, q in ((0, up), (1, down)):
                if s > 0 and (d, s - 1, i) in z_copies:
                    z_copies[d, s - 1, i].wait_recv()
                if s < 3 or (i < 2) == (d == 0):
                    zs = (z - s + NZ) % NZ if d == 0 else (z + s) % NZ
                    a = send(xp.at[zs, xi], xp.at[zs, xi], z_send.at[d, s, i], z_recv.at[d, s, i], *q)
                    a.start()
                    z_copies[d, s, i] = a
        if s == 0:
            for i, yi in enumerate(((y + 3) % NY, (y + 1) % NY, (y + 2) % NY)):
                wy_copies[i].wait_recv()
                for j, q in enumerate(xs):
                    ref = full.at[:, rows(yi, x)]
                    a = send(ref, ref, wx_send.at[i, j], wx_recv.at[i, j], *q)
                    a.start()
                    wx_copies.append(a)
        if s == 2:
            for i, yi in enumerate(((y + 3) % NY, (y + 1) % NY, (y + 2) % NY)):
                for j in range(3):
                    wx_copies[i * 3 + j].wait_recv()
                ref = full.at[:, pl.ds(pl.multiple_of(yi * 128 + p * 64, 64), 64)]
                a = send(ref, ref, wc_send.at[i], wc_recv.at[i], *core)
                a.start()
                wc_copies.append(a)
    for (d, s, i), a in z_copies.items():
        if s == 3:
            a.wait_recv()
    for a in x_copies + list(z_copies.values()) + wy_copies + wx_copies:
        a.wait_send()
    for a in own_copies + wc_copies + tile_copies:
        a.wait()


def deal(owner, source, target, relation, count, tiles, states, weights):
    return pl.pallas_call(
        deal_kernel,
        out_shape=(
            jax.ShapeDtypeStruct((NC, SLOTS, TILE, TILE), BF),
            jax.ShapeDtypeStruct((NC, 8, 128), jnp.int32),
            jax.ShapeDtypeStruct((NZ, NX, ROWS, D), BF),
            jax.ShapeDtypeStruct((REL + 1, D, D), BF),
            jax.ShapeDtypeStruct((NY * REL * TILE, 16 * TILE), BF),
        ),
        in_specs=[IN_HBM] * 8,
        out_specs=(ANY,) * 4 + (VM,),
        scratch_shapes=[
            pltpu.VMEM((4, NZ * NX, EB), jnp.int32),
            pltpu.VMEM((1, NZ * NX), jnp.int32),
            pltpu.VMEM((EB, TILE, TILE), BF),
            pltpu.VMEM((NC * 4, 128), jnp.int32),
            pltpu.SMEM((NC * 4, 128), jnp.int32),
            pltpu.VMEM((NC, 8, 128), jnp.int32),
            pltpu.VMEM((NC, SLOTS, TILE, TILE), BF),
            DMA((7,)), DMA((4,)), DMA((7,)), DMA((7,)), DMA((7,)), DMA((7,)), DMA(()), DMA(()),
            DMA((3,)), DMA((3,)), DMA((2, 4, 4)), DMA((2, 4, 4)),
            DMA((3,)), DMA((3,)), DMA((3, 3)), DMA((3, 3)), DMA((3,)), DMA((3,)),
        ],
        compiler_params=params(8, 0),
    )(owner, source, target, relation, count, tiles, states, weights)


def adjacency_kernel(meta, tiles, zeros, adj):
    del zeros

    def slots(c, carry):
        for s in range(SLOTS):
            code = meta[c, s // 2, s % 2]

            @pl.when(code >= 0)
            def _():
                row = pl.ds(pl.multiple_of((code >> 2) * TILE, TILE), TILE)
                column = pl.ds(pl.multiple_of(((s // 2) * 4 + (code & 3)) * TILE, TILE), TILE)
                adj[row, column] += tiles[c, s]

        return carry

    lax.fori_loop(0, NC, slots, 0)


def adjacency(meta, tiles, zeros):
    return pl.pallas_call(
        adjacency_kernel,
        out_shape=jax.ShapeDtypeStruct((NY * REL * TILE, 16 * TILE), BF),
        in_specs=[SM, VM, VM],
        out_specs=VM,
        input_output_aliases={2: 0},
        compiler_params=params(6),
    )(meta, tiles, zeros)


def main_kernel(
    adj, xp, weights, states, cotangent,
    layer_o, g_o, wa, wb,
    tq, tc_buf, ty_src, ty_buf, tg, m_own, m_src, m_buf, my_src, my_buf, slope_s, zs,
    gw_a, xw_src_a, xw_buf_a, zw_src_a, zw_buf_a, aw_buf_a,
    gw_b, xw_src_b, xw_buf_b, zw_src_b, zw_buf_b, aw_buf_b, wb_src, g_in, g_src, g_buf, gx_src, gx_buf,
    bx_buf, gb_src, gb_buf, v_src, v_buf,
    tc_s, tc_r, ty_s, ty_r, mc_s, mc_r, my_s, my_r, s_s, s_r, f_s, f_r,
    xw_s, xw_r, zw_s, zw_r, aw_s, aw_r, wa_s, wa_r, wb_s, wb_r, g_s, g_r, gx_s, gx_r, bx_s, bx_r, gb_s, gb_r, v_s, v_r,
):
    over_rows = (((0,), (0,)), ((), ()))
    over_columns = (((1,), (1,)), ((), ()))
    gw, xw_src, xw_buf = (gw_a, gw_b), (xw_src_a, xw_src_b), (xw_buf_a, xw_buf_b)
    zw_src, zw_buf, aw_buf = (zw_src_a, zw_src_b), (zw_buf_a, zw_buf_b), (aw_buf_a, aw_buf_b)
    z, x, y, p = place()
    core = (z, x, y, 1 - p)
    shifts = (2, 1, 3)
    ys = [(z, x, (y + i) % NY, p) for i in shifts]
    senders = [(y + NY - i) % NY for i in shifts]
    xs = x_peers(z, x, y, p)
    xo = [(q[0], q[1], q[2], 1 - p) for q in xs]
    around = z_peers(z, x, y, p, (4, 3, 5, 2, 6, 1, 7))
    up, down = around[5], around[6]
    target, is_self = swap_of(z, x, y, p)
    arrived = greet([core] + ys + xs + xo + around, (target, is_self))
    c = y * 2 + p
    share = pl.ds(pl.multiple_of(c * ROWS, ROWS), ROWS)

    def half(v, mine):
        low, high = v[:ROWS], v[ROWS:]
        return jnp.where(p == (0 if mine else 1), low, high)

    order = [q[2] for q in ys] + [y]
    m_copies, t_copies, my_copies = [], [], []

    def messages_on(n):
        m_copies[n].wait_recv()
        t = order[n]
        my_src[n] = (m_own[t] + m_buf[t].astype(F32)).astype(BF)
        a = send(my_src.at[n], my_buf.at[n], my_s.at[n], my_r.at[n], *ys[n])
        a.start()
        my_copies.append(a)

    ty_copies = {}

    def transforms_on(n, send_now=True):
        t = order[n]
        t_copies[n].wait_recv()
        for j, q in enumerate(ys):
            yi = q[2]
            ty_src[j, t] = (tq[p, t, yi].astype(F32) + tc_buf[t, yi].astype(F32)).astype(BF)
            if send_now:
                a = send(ty_src.at[j, t], ty_buf.at[j, t], ty_s.at[j, n, 0], ty_r.at[j, n, 0], *q)
                a.start()
                ty_copies[j, n, 0] = a

    def transforms_part(n, r):
        t = order[n]
        for j, q in enumerate(ys):
            a = send(
                ty_src.at[j, t, r], ty_buf.at[j, t, r], ty_s.at[j, n, r], ty_r.at[j, n, r], *q
            )
            a.start()
            ty_copies[j, n, r] = a

    for n, t in enumerate(order):
        rows = pl.ds(pl.multiple_of(t * D, D), D)
        tt = jnp.dot(adj[rows, :], xp[...], preferred_element_type=F32).astype(BF)
        m = jnp.zeros((TILE, D), F32)
        for r in range(REL):
            part = tt[r * TILE : (r + 1) * TILE]
            m = m + jnp.dot(part, weights[r], preferred_element_type=F32)
            for q in range(NY):
                tq[r // 2, t, q, r % 2] = part[:, q * TILE : (q + 1) * TILE]
        m_own[t] = half(m, True)
        m_src[t] = half(m, False).astype(BF)
        if n == 0:
            arrived()
        a = send(m_src.at[t], m_buf.at[t], mc_s.at[n], mc_r.at[n], *core)
        a.start()
        m_copies.append(a)
        if n > 0:
            messages_on(n - 1)
        a = send(tq.at[1 - p, t], tc_buf.at[t], tc_s.at[n], tc_r.at[n], *core)
        a.start()
        t_copies.append(a)


    w_self = weights[REL]
    pre = jnp.dot(states[share, :], w_self, preferred_element_type=F32)
    m_copies[3].wait_recv()
    pre = pre + m_own[y] + m_buf[y].astype(F32)
    for n, a in enumerate(my_copies):
        a.wait_recv()
        pre = pre + my_buf[n].astype(F32)
    sigma = jax.nn.sigmoid(pre)
    slope = (cotangent[share, :].astype(F32) * (sigma * (1.0 + pre * (1.0 - sigma)))).astype(BF)
    slope_s[c] = slope
    mine = slope_s.at[c]
    s_copies = []
    for i, q in enumerate(ys + [core]):
        a = send(mine, mine, s_s.at[i], s_r.at[i], *q)
        a.start()
        s_copies.append(a)
    for n in (0, 1, 2, 3):
        transforms_on(n, False)
        transforms_part(n, 0)
    for n in (0, 1, 2, 3):
        transforms_part(n, 1)
    layer_o[...] = pre * sigma
    g_o[...] = lax.dot_general(slope, w_self, over_columns, preferred_element_type=F32)
    f_copies = []
    for i in (1, 2, 0):
        s_copies[i].wait_recv()
        ref = slope_s.at[senders[i] * 2 + p]
        a = send(ref, ref, f_s.at[i], f_r.at[i], *core)
        a.start()
        f_copies.append(a)
    def transposed(core_of):
        rows = jnp.concatenate([slope_s[t * 2 + core_of] for t in range(NY)], axis=0)
        for r in range(REL):
            part = lax.dot_general(rows, weights[r], over_columns, preferred_element_type=F32)
            part = part.astype(BF)
            for t in range(NY):
                at = pl.multiple_of(t * D + r * TILE + core_of * ROWS, ROWS)
                zs[pl.ds(at, ROWS), :] = part[t * ROWS : (t + 1) * ROWS]

    transposed(p)
    s_copies[3].wait_recv()
    for a in f_copies:
        a.wait_recv()
    transposed(1 - p)
    whole = slope_s[...].reshape(D, D)

    def gradients(k):
        columns = pl.ds(pl.multiple_of(k * D, D), D)
        part = lax.dot_general(adj[:, columns], zs[...], over_rows, preferred_element_type=F32)
        part = part.astype(BF)
        for b in range(4):
            for h in range(2):
                row = b * TILE + h * ROWS
                g_in[2 * k + h, b] = part[row : row + ROWS]

    g_copies = {}
    hops = {(d, i): 4 if (i < 2) == (d == 0) else 3 for d in range(2) for i in range(NX)}

    def chain(s, only=(3, 4)):
        for i in range(NX):
            xi = (x + i) % NX
            for d, q in ((0, up), (1, down)):
                left = hops[d, i] - s
                if left <= 0 or hops[d, i] not in only:
                    continue
                zd = (z + left) % NZ if d == 0 else (z - left + NZ) % NZ
                if s == 0:
                    src = g_in.at[zd, xi, pl.ds(0, HA)]
                else:
                    g_copies[d, s - 1, i].wait_recv()
                    g_src[d, s - 1, i] = (
                        g_in[zd, xi, :HA].astype(F32) + g_buf[d, s - 1, i].astype(F32)
                    ).astype(BF)
                    src = g_src.at[d, s - 1, i]
                a = send(src, g_buf.at[d, s, i], g_s.at[d, s, i], g_r.at[d, s, i], *q)
                a.start()
                g_copies[d, s, i] = a

    bx_copies = {}

    def across(n):
        k = near[n]
        two = pl.ds(2 * k, 2)
        for j, q in enumerate(xs):
            a = send(
                g_in.at[two, q[1], pl.ds(HA, HB)], bx_buf.at[j, two], bx_s.at[j, n], bx_r.at[j, n], *q
            )
            a.start()
            bx_copies[j, n] = a

    def across_wait(n):
        for j in range(3):
            bx_copies[j, n].wait_recv()

    gb_copies = {}

    def x_sum(zd):
        total = g_in[zd, x, HA:].astype(F32)
        for j in range(3):
            total = total + bx_buf[j, zd].astype(F32)
        return total

    def second(i):
        zd = (z + i) % NZ
        gb_src[i] = x_sum(zd).astype(BF)
        a = send(gb_src.at[i], gb_buf.at[i], gb_s.at[i], gb_r.at[i], zd, x, y, p)
        a.start()
        gb_copies[i] = a

    pair = z // 2
    odd = 2 * (z % 2)
    near = ((pair + 2) % 4, (pair + 1 + odd) % 4, (pair + 3 + odd) % 4, pair)
    columns = pl.ds(pl.multiple_of(y * TILE, TILE), TILE)
    xw_copies, zw_copies, aw_copies, w_copies = [[], []], [[], []], [[], []], []

    def weight_part(r):
        for (j, n, q), a in ty_copies.items():
            if q == r:
                a.wait_recv()
        for t in range(NY):
            total = tq[p, t, y, r].astype(F32) + tc_buf[t, y, r].astype(F32)
            for j in range(3):
                total = total + ty_buf[j, t, r].astype(F32)
            tg[r, t * TILE : (t + 1) * TILE, :] = total.astype(BF)
        part = lax.dot_general(tg[r], whole, over_rows, preferred_element_type=F32)
        rows_of = [half(part, True), half(part, False)]
        if r == 1:
            part = lax.dot_general(states[:, columns], whole, over_rows, preferred_element_type=F32)
            rows_of.insert(1, half(part, True))
        for m, v in enumerate(rows_of):
            for q in range(NX):
                gw[r][q, m * ROWS : (m + 1) * ROWS, :] = v[:, q * WC : (q + 1) * WC]
        for i in range(3):
            xw_src[r][i] = gw[r][xs[i][1]].astype(BF)
            a = send(xw_src[r].at[i], xw_buf[r].at[i], xw_s.at[r, i], xw_r.at[r, i], *xs[i])
            a.start()
            xw_copies[r].append(a)

    def weight_x(r):
        total = gw[r][x]
        for i, a in enumerate(xw_copies[r]):
            a.wait_recv()
            total = total + xw_buf[r][i].astype(F32)
        total = total.reshape(NZ, PART[r] // NZ, WC)
        if EIGHTH[r] > PART[r] // NZ:
            padding = jnp.zeros((NZ, EIGHTH[r] - PART[r] // NZ, WC), F32)
            total = jnp.concatenate([total, padding], axis=1)
        zw_src[r][...] = total.astype(BF)
        for i, q in enumerate(around):
            a = send(zw_src[r].at[q[0]], zw_buf[r].at[i], zw_s.at[r, i], zw_r.at[r, i], *q)
            a.start()
            zw_copies[r].append(a)

    def weight_z(r):
        total = zw_src[r][z].astype(F32)
        for i, a in enumerate(zw_copies[r]):
            a.wait_recv()
            total = total + zw_buf[r][i].astype(F32)
        aw_buf[r][z] = total.astype(BF)
        for i, q in enumerate(around):
            a = send(aw_buf[r].at[z], aw_buf[r].at[z], aw_s.at[r, i], aw_r.at[r, i], *q)
            a.start()
            aw_copies[r].append(a)

    def weight_out(r):
        for a in aw_copies[r]:
            a.wait_recv()
        done = aw_buf[r][...].astype(F32)[:, : PART[r] // NZ].reshape(PART[r], WC).astype(BF)
        mine, other = pl.ds(r * ROWS, (r + 1) * ROWS), pl.ds(r * ROWS, ROWS)
        wa[x, mine, :] = done[: (r + 1) * ROWS]
        wb_src[other, :] = done[(r + 1) * ROWS :]
        for i, q in enumerate(xs):
            ref = wa.at[x, mine]
            w_copies.append(send(ref, ref, wa_s.at[r, i], wa_r.at[r, i], *q))
        for i, q in enumerate(xo + [core]):
            w_copies.append(
                send(wb_src.at[other], wb.at[x, other], wb_s.at[r, i], wb_r.at[r, i], *q)
            )
        for a in w_copies[-7:]:
            a.start()

    gradients(near[0])
    across(0)
    chain(0, (4,))
    gradients(near[1])
    across(1)
    chain(0, (3,))
    weight_part(0)
    gradients(near[2])
    across(2)
    chain(1)
    weight_part(1)
    gradients(near[3])
    across(3)
    weight_x(0)
    chain(2)
    across_wait(0)
    across_wait(1)
    for i in (4, 3, 5):
        second(i)
    weight_z(0)
    weight_x(1)
    chain(3)
    across_wait(2)
    for i in (2, 6):
        second(i)
    weight_out(0)
    weight_z(1)
    across_wait(3)
    for i in (1, 7):
        second(i)

    gx_copies = []
    own = None
    for i in (1, 2, 3, 0):
        xi = (x + i) % NX
        part = g_in[z, xi, :HA].astype(F32)
        for d in range(2):
            last = hops[d, i] - 1
            g_copies[d, last, i].wait_recv()
            part = part + g_buf[d, last, i].astype(F32)
        if i:
            gx_src[i - 1] = part.astype(BF)
            a = send(gx_src.at[i - 1], gx_buf.at[i - 1], gx_s.at[i - 1], gx_r.at[i - 1], *xs[i - 1])
            a.start()
            gx_copies.append(a)
        else:
            own = part

    weight_out(1)
    total = x_sum(z)
    for i, a in gb_copies.items():
        a.wait_recv()
        total = total + gb_buf[i].astype(F32)
    v_src[HA:] = total.astype(BF)
    for i, a in enumerate(gx_copies):
        a.wait_recv()
        own = own + gx_buf[i].astype(F32)
    v_src[:HA] = own.astype(BF)

    @pl.when(jnp.logical_not(is_self))
    def _():
        a = send(v_src, v_buf, v_s, v_r, *target)
        a.start()
        a.wait()

    @pl.when(is_self)
    def _():
        v_buf[...] = v_src[...]

    g_o[...] = g_o[...] + v_buf[...].astype(F32)
    for a in w_copies:
        a.wait()
    for a in m_copies + t_copies + my_copies + s_copies + f_copies:
        a.wait_send()
    for copies in xw_copies + zw_copies + aw_copies + [gx_copies]:
        for a in copies:
            a.wait_send()
    for some in (ty_copies, g_copies, bx_copies, gb_copies):
        for a in some.values():
            a.wait_send()


def main(adj, xp, weights, states, cotangent):
    return pl.pallas_call(
        main_kernel,
        out_shape=(
            jax.ShapeDtypeStruct((ROWS, D), F32),
            jax.ShapeDtypeStruct((ROWS, D), F32),
            jax.ShapeDtypeStruct((NX, 3 * ROWS, WC), BF),
            jax.ShapeDtypeStruct((NX, 2 * ROWS, WC), BF),
        ),
        in_specs=[VM] * 5,
        out_specs=(VM,) * 4,
        scratch_shapes=[
            pltpu.VMEM((2, NY, NY, 2, TILE, TILE), BF),
            pltpu.VMEM((NY, NY, 2, TILE, TILE), BF),
            pltpu.VMEM((3, NY, 2, TILE, TILE), BF),
            pltpu.VMEM((3, NY, 2, TILE, TILE), BF),
            pltpu.VMEM((2, D, TILE), BF),
            pltpu.VMEM((NY, ROWS, D), F32),
            pltpu.VMEM((NY, ROWS, D), BF),
            pltpu.VMEM((NY, ROWS, D), BF),
            pltpu.VMEM((3, ROWS, D), BF),
            pltpu.VMEM((3, ROWS, D), BF),
            pltpu.VMEM((NC, ROWS, D), BF),
            pltpu.VMEM((NY * D, D), BF),
            *(
                v
                for r in range(2)
                for v in (
                    pltpu.VMEM((NX, PART[r], WC), F32),
                    pltpu.VMEM((3, PART[r], WC), BF),
                    pltpu.VMEM((3, PART[r], WC), BF),
                    pltpu.VMEM((NZ, EIGHTH[r], WC), BF),
                    pltpu.VMEM((7, EIGHTH[r], WC), BF),
                    pltpu.VMEM((NZ, EIGHTH[r], WC), BF),
                )
            ),
            pltpu.VMEM((2 * ROWS, WC), BF),
            pltpu.VMEM((NZ, NX, ROWS, D), BF),
            pltpu.VMEM((2, 3, NX, HA, D), BF),
            pltpu.VMEM((2, 4, NX, HA, D), BF),
            pltpu.VMEM((3, HA, D), BF),
            pltpu.VMEM((3, HA, D), BF),
            pltpu.VMEM((3, NZ, HB, D), BF),
            pltpu.VMEM((NZ, HB, D), BF),
            pltpu.VMEM((NZ, HB, D), BF),
            pltpu.VMEM((ROWS, D), BF),
            pltpu.VMEM((ROWS, D), BF),
            DMA((4,)), DMA((4,)), DMA((3, 4, 2)), DMA((3, 4, 2)), DMA((4,)), DMA((4,)), DMA((3,)), DMA((3,)),
            DMA((4,)), DMA((4,)), DMA((3,)), DMA((3,)),
            DMA((2, 3)), DMA((2, 3)), DMA((2, 7)), DMA((2, 7)), DMA((2, 7)), DMA((2, 7)),
            DMA((2, 3)), DMA((2, 3)), DMA((2, 4)), DMA((2, 4)), DMA((2, 4, 4)), DMA((2, 4, 4)), DMA((3,)), DMA((3,)),
            DMA((3, 4)), DMA((3, 4)), DMA((8,)), DMA((8,)), DMA(()), DMA(()),
        ],
        compiler_params=params(32, 1),
    )(adj, xp, weights, states, cotangent)


def close_kernel(layer, g, wa, wb, layer_o, g_o, w_o):
    p = lax.axis_index("replica")
    layer_o[...] = layer[...]
    g_o[...] = g[...]
    for q in range(NX):
        columns = slice(q * WC, (q + 1) * WC)
        for m in range(2):
            a = wa[q, m * ROWS : (m + 1) * ROWS, :].astype(F32)
            b = wb[q, m * ROWS : (m + 1) * ROWS, :].astype(F32)
            w_o[m, :, columns] = jnp.where(p == 0, a, b)
            w_o[2 + m, :, columns] = jnp.where(p == 0, b, a)
        w_o[REL, :, columns] = wa[q, 2 * ROWS :, :].astype(F32)


def close(layer, g, wa, wb):
    return pl.pallas_call(
        close_kernel,
        out_shape=(
            jax.ShapeDtypeStruct((ROWS, D), F32),
            jax.ShapeDtypeStruct((ROWS, D), F32),
            jax.ShapeDtypeStruct((REL + 1, ROWS, D), F32),
        ),
        in_specs=[VM] * 4,
        out_specs=(VM, VM, VM),
        compiler_params=params(8),
    )(layer, g, wa, wb)


def shards(
    states,
    weights,
    edge_tiles,
    edge_owner,
    edge_source,
    edge_target,
    edge_relation,
    edge_count,
    cotangent,
):
    groups = edge_owner.shape[0]
    owner = edge_owner.reshape(groups, EB)
    source = edge_source.reshape(groups, EB)
    target = edge_target.reshape(groups, EB)
    relation = edge_relation.reshape(groups, EB)
    count = edge_count.reshape(1, groups)
    tiles = edge_tiles.reshape(EB, TILE, TILE)
    given = (owner, source, target, relation, count, tiles, states, weights)
    given = (pltpu.with_memory_space_constraint(v, pltpu.HBM) for v in given)
    tiles, meta, xp, full, zeros = deal(*given)
    adj = adjacency(meta, tiles, zeros)
    layer, g, wa, wb = main(adj, xp.reshape(-1, D), full, states, cotangent)
    return close(layer, g, wa, wb)


def solution(mesh):
    return jax.shard_map(
        shards,
        mesh=mesh,
        in_specs=(
            P("graph", None),
            P(None, "fsdp", None),
            P("graph", "fsdp", "replica", None, None, None),
            P(None, "fsdp", "replica", None),
            P(None, "fsdp", "replica", None),
            P(None, "fsdp", "replica", None),
            P(None, "fsdp", "replica", None),
            P(None, "fsdp", "replica"),
            P("graph", None),
        ),
        out_specs=(
            P(("graph", "fsdp", "replica"), None),
            P(("graph", "fsdp", "replica"), None),
            P(None, ("fsdp", "replica"), None),
        ),
        check_vma=False,
    )
```

```python
import jax
import jax.numpy as jnp
from jax import lax
from jax.experimental import pallas as pl
from jax.experimental.pallas import tpu as pltpu
from jax.sharding import PartitionSpec as P

D = 512
REL = 4
TILE = 128
EB = 48
NZ = 8
NX = 4
NY = 4
NC = 8
SLOTS = 8
ROWS = 64
PART = (128, 192)
EIGHTH = (16, 32)
HA = 48
HB = ROWS - HA
WC = 128
BF = jnp.bfloat16
F32 = jnp.float32
MESH = pl.DeviceIdType.MESH
ANY = pl.BlockSpec(memory_space=pl.ANY)
VM = pl.BlockSpec(memory_space=pltpu.VMEM)
SM = pl.BlockSpec(memory_space=pltpu.SMEM)
IN_HBM = pl.BlockSpec(memory_space=pltpu.HBM)
DMA = pltpu.SemaphoreType.DMA


def params(mib, collective=None):
    more = {} if collective is None else {"collective_id": collective, "has_side_effects": True}
    return pltpu.CompilerParams(vmem_limit_bytes=mib * 1024 * 1024, **more)


def place():
    g = lax.axis_index("graph")
    return g // NX, g % NX, lax.axis_index("fsdp"), lax.axis_index("replica")


def send(src, dst, ssem, rsem, z, x, y, p):
    return pltpu.make_async_remote_copy(
        src_ref=src,
        dst_ref=dst,
        send_sem=ssem,
        recv_sem=rsem,
        device_id=(z * NX + x, y, p),
        device_id_type=MESH,
    )


def greet(partners, swap=None):
    barrier = pltpu.get_barrier_semaphore()
    for z, x, y, p in partners:
        pl.semaphore_signal(barrier, inc=1, device_id=(z * NX + x, y, p), device_id_type=MESH)
    count = len(partners)
    if swap is not None:
        (z, x, y, p), is_self = swap

        @pl.when(jnp.logical_not(is_self))
        def _():
            pl.semaphore_signal(barrier, inc=1, device_id=(z * NX + x, y, p), device_id_type=MESH)

        count = count + jnp.where(is_self, 0, 1)
    return lambda: pl.semaphore_wait(barrier, count)


def group_peers(z, x, y, p):
    return [
        (z, x, (y + dy) % NY, (p + dp) % 2)
        for dy, dp in ((0, 1), (1, 0), (3, 0), (1, 1), (3, 1), (2, 0), (2, 1))
    ]


def y_peers(z, x, y, p):
    return [(z, x, (y + i) % NY, p) for i in (1, 3, 2)]


def x_peers(z, x, y, p):
    return [(z, (x + i) % NX, y, p) for i in (1, 2, 3)]


def z_peers(z, x, y, p, steps=(1, 7)):
    return [((z + i) % NZ, x, y, p) for i in steps]


def swap_of(z, x, y, p):
    return (2 * (z // 2) + p, y, x, z % 2), (x == y) & (z % 2 == p)


def deal_kernel(
    owner, source, target_h, relation, count, tiles, states, weights, tiles_o, meta_o, xp, full, zeros,
    edges, counts, tiles_v, idx_v, idx, meta, packed,
    e_sems, own_sems, t_send, t_recv, m_send, m_recv, v_send, v_recv, x_send, x_recv, z_send, z_recv,
    wy_send, wy_recv, wx_send, wx_recv, wc_send, wc_recv,
):
    z, x, y, p = place()
    peers = group_peers(z, x, y, p)
    core, ys = peers[0], y_peers(z, x, y, p)
    xs = x_peers(z, x, y, p)
    up, down = z_peers(z, x, y, p)
    target, is_self = swap_of(z, x, y, p)
    loads = [
        pltpu.make_async_copy(h, edges.at[i], e_sems.at[i])
        for i, h in enumerate((owner, source, target_h, relation))
    ]
    loads.append(pltpu.make_async_copy(count, counts, e_sems.at[4]))
    for a in loads:
        a.start()
    load_tiles = pltpu.make_async_copy(tiles, tiles_v, e_sems.at[5])
    load_tiles.start()
    arrived = greet(peers + xs + [up, down], (target, is_self))
    c = y * 2 + p
    at = pl.multiple_of((p * NY + y) * ROWS, ROWS)
    piece = states.at[pl.ds(at, ROWS)]
    pieces = [states.at[pl.ds(pl.multiple_of(at + h * 32, 32), 32)] for h in range(2)]

    arrived()

    @pl.when(jnp.logical_not(is_self))
    def _():
        for h in range(2):
            dst = xp.at[target[0], target[1], pl.ds(h * 32, 32)]
            send(pieces[h], dst, v_send.at[h], v_recv.at[h], *target).start()

    @pl.when(is_self)
    def _():
        pltpu.make_async_copy(piece, xp.at[z, x], own_sems.at[0]).start()

    def rows(yi, xi):
        return pl.ds(pl.multiple_of(yi * 128 + p * 64 + xi * 16, 16), 16)

    wy_copies = []
    mine_w = weights.at[:, pl.ds(pl.multiple_of(p * 64 + x * 16, 16), 16)]
    for i, q in enumerate(ys):
        a = send(mine_w, full.at[:, rows(y, x)], wy_send.at[i], wy_recv.at[i], *q)
        a.start()
        wy_copies.append(a)

    own_w = pltpu.make_async_copy(
        weights, full.at[:, pl.ds(pl.multiple_of(y * 128, 128), 128)], own_sems.at[3]
    )
    own_w.start()

    for a in loads:
        a.wait()
    g = lax.axis_index("graph")
    e = lax.broadcasted_iota(jnp.int32, (NC * 4, EB), 1)
    row = lax.broadcasted_iota(jnp.int32, (NC * 4, EB), 0)
    wanted = (2 * (row & 3) + ((row >> 2) & 1)) * NX + (row >> 3)
    groups = lax.broadcasted_iota(jnp.int32, (1, NZ * NX), 1)
    live = jnp.sum(jnp.where(groups == g, counts[...], 0), axis=1, keepdims=True)
    own, src, dst, rel = (edges[i, pl.ds(g, 1), :] for i in range(4))
    code = src + 4 * (dst * REL + rel)
    hit = (own == wanted) & (e < live)
    first = jnp.min(jnp.where(hit, e, EB), axis=1, keepdims=True)
    last = jnp.max(jnp.where(hit, e, -1), axis=1, keepdims=True)
    code0 = jnp.sum(jnp.where(hit & (e == first), code, 0), axis=1, keepdims=True)
    code1 = jnp.sum(jnp.where(hit & (e == last), code, 0), axis=1, keepdims=True)
    code0 = jnp.where(first < EB, code0, -1)
    code1 = jnp.where(last > first, code1, -1)
    lane = lax.broadcasted_iota(jnp.int32, (NC * 4, 128), 1)
    idx_v[...] = jnp.where(lane == 0, jnp.minimum(first, EB - 1), jnp.maximum(last, 0))
    codes = jnp.where(lane == 0, code0, code1)
    meta[...] = jnp.full(meta.shape, -1, jnp.int32)
    for i in range(NC):
        meta[i, 0:4, :] = codes[i * 4 : i * 4 + 4]
    to_scalars = pltpu.make_async_copy(idx_v, idx, e_sems.at[6])
    to_scalars.start()
    to_scalars.wait()
    load_tiles.wait()

    def put(ci):
        def one(s, carry):
            packed[ci, s] = tiles_v[idx[ci * 4 + s // 2, s % 2]]
            return carry

        lax.fori_loop(0, SLOTS, one, 0)

    x_copies = {}
    for h in range(2):
        ref = xp.at[z, x, pl.ds(h * 32, 32)]
        for i, q in enumerate(xs):
            x_copies[h, i] = send(ref, ref, x_send.at[h, i], x_recv.at[h, i], *q)

    def x_phase():
        @pl.when(is_self)
        def _():
            pltpu.make_async_copy(piece, xp.at[z, x], own_sems.at[0]).wait()

        for h in range(2):

            @pl.when(jnp.logical_not(is_self))
            def _():
                dst = xp.at[z, x, pl.ds(h * 32, 32)]
                send(pieces[h], dst, v_send.at[h], v_recv.at[h], *target).wait()

            for i in range(3):
                x_copies[h, i].start()

    tile_copies = []
    for i, q in enumerate(peers):
        if i == 3:
            x_phase()
        cq = q[2] * 2 + q[3]
        put(cq)
        a = send(packed.at[cq], tiles_o.at[c], t_send.at[i], t_recv.at[i], *q)
        b = send(meta.at[cq], meta_o.at[c], m_send.at[i], m_recv.at[i], *q)
        a.start()
        b.start()
        tile_copies += [a, b]
    put(c)
    own_copies = [
        pltpu.make_async_copy(packed.at[c], tiles_o.at[c], own_sems.at[1]),
        pltpu.make_async_copy(meta.at[c], meta_o.at[c], own_sems.at[2]),
    ]
    for a in own_copies:
        a.start()
    own_copies.append(own_w)

    zeros[...] = jnp.zeros_like(zeros)

    wx_copies = []
    wc_copies = []
    z_copies = {}
    for s in range(4):
        for i, h in ((i, h) for i in range(NX) for h in range(2)):
            xi = (x + i) % NX
            if s == 0 and i > 0:
                x_copies[h, 3 - i].wait_recv()
            for d, q in ((0, up), (1, down)):
                if s > 0 and (d, s - 1, i, h) in z_copies:
                    z_copies[d, s - 1, i, h].wait_recv()
                if s < 3 or (i < 2) == (d == 0):
                    zs = (z - s + NZ) % NZ if d == 0 else (z + s) % NZ
                    ref = xp.at[zs, xi, pl.ds(h * 32, 32)]
                    a = send(ref, ref, z_send.at[d, s, i, h], z_recv.at[d, s, i, h], *q)
                    a.start()
                    z_copies[d, s, i, h] = a
        if s == 0:
            for i, yi in enumerate(((y + 3) % NY, (y + 1) % NY, (y + 2) % NY)):
                wy_copies[i].wait_recv()
                for j, q in enumerate(xs):
                    ref = full.at[:, rows(yi, x)]
                    a = send(ref, ref, wx_send.at[i, j], wx_recv.at[i, j], *q)
                    a.start()
                    wx_copies.append(a)
        if s == 2:
            for i, yi in enumerate(((y + 3) % NY, (y + 1) % NY, (y + 2) % NY)):
                for j in range(3):
                    wx_copies[i * 3 + j].wait_recv()
                ref = full.at[:, pl.ds(pl.multiple_of(yi * 128 + p * 64, 64), 64)]
                a = send(ref, ref, wc_send.at[i], wc_recv.at[i], *core)
                a.start()
                wc_copies.append(a)
    for (d, s, i, h), a in z_copies.items():
        if s == 3:
            a.wait_recv()
    for a in list(x_copies.values()) + list(z_copies.values()) + wy_copies + wx_copies:
        a.wait_send()
    for a in own_copies + wc_copies + tile_copies:
        a.wait()


def deal(owner, source, target, relation, count, tiles, states, weights):
    return pl.pallas_call(
        deal_kernel,
        out_shape=(
            jax.ShapeDtypeStruct((NC, SLOTS, TILE, TILE), BF),
            jax.ShapeDtypeStruct((NC, 8, 128), jnp.int32),
            jax.ShapeDtypeStruct((NZ, NX, ROWS, D), BF),
            jax.ShapeDtypeStruct((REL + 1, D, D), BF),
            jax.ShapeDtypeStruct((NY * REL * TILE, 16 * TILE), BF),
        ),
        in_specs=[IN_HBM] * 8,
        out_specs=(ANY,) * 4 + (VM,),
        scratch_shapes=[
            pltpu.VMEM((4, NZ * NX, EB), jnp.int32),
            pltpu.VMEM((1, NZ * NX), jnp.int32),
            pltpu.VMEM((EB, TILE, TILE), BF),
            pltpu.VMEM((NC * 4, 128), jnp.int32),
            pltpu.SMEM((NC * 4, 128), jnp.int32),
            pltpu.VMEM((NC, 8, 128), jnp.int32),
            pltpu.VMEM((NC, SLOTS, TILE, TILE), BF),
            DMA((7,)), DMA((4,)), DMA((7,)), DMA((7,)), DMA((7,)), DMA((7,)), DMA((2,)), DMA((2,)),
            DMA((2, 3)), DMA((2, 3)), DMA((2, 4, 4, 2)), DMA((2, 4, 4, 2)),
            DMA((3,)), DMA((3,)), DMA((3, 3)), DMA((3, 3)), DMA((3,)), DMA((3,)),
        ],
        compiler_params=params(8, 0),
    )(owner, source, target, relation, count, tiles, states, weights)


def adjacency_kernel(meta, tiles, zeros, adj):
    del zeros

    def slots(c, carry):
        for s in range(SLOTS):
            code = meta[c, s // 2, s % 2]

            @pl.when(code >= 0)
            def _():
                row = pl.ds(pl.multiple_of((code >> 2) * TILE, TILE), TILE)
                column = pl.ds(pl.multiple_of(((s // 2) * 4 + (code & 3)) * TILE, TILE), TILE)
                adj[row, column] += tiles[c, s]

        return carry

    lax.fori_loop(0, NC, slots, 0)


def adjacency(meta, tiles, zeros):
    return pl.pallas_call(
        adjacency_kernel,
        out_shape=jax.ShapeDtypeStruct((NY * REL * TILE, 16 * TILE), BF),
        in_specs=[SM, VM, VM],
        out_specs=VM,
        input_output_aliases={2: 0},
        compiler_params=params(6),
    )(meta, tiles, zeros)


def main_kernel(
    adj, xp, weights, states, cotangent,
    layer_o, g_o, wa, wb,
    tq, tc_buf, ty_src, ty_buf, tg, m_own, m_src, m_buf, my_src, my_buf, slope_s, zs,
    gw_a, xw_src_a, xw_buf_a, zw_src_a, zw_buf_a, aw_buf_a,
    gw_b, xw_src_b, xw_buf_b, zw_src_b, zw_buf_b, aw_buf_b, wb_src, g_in, g_src, g_buf, gx_src, gx_buf,
    bx_buf, gb_src, gb_buf, v_src, v_buf,
    tc_s, tc_r, ty_s, ty_r, mc_s, mc_r, my_s, my_r, s_s, s_r, f_s, f_r,
    xw_s, xw_r, zw_s, zw_r, aw_s, aw_r, wa_s, wa_r, wb_s, wb_r, g_s, g_r, gx_s, gx_r, bx_s, bx_r, gb_s, gb_r, v_s, v_r,
):
    over_rows = (((0,), (0,)), ((), ()))
    over_columns = (((1,), (1,)), ((), ()))
    gw, xw_src, xw_buf = (gw_a, gw_b), (xw_src_a, xw_src_b), (xw_buf_a, xw_buf_b)
    zw_src, zw_buf, aw_buf = (zw_src_a, zw_src_b), (zw_buf_a, zw_buf_b), (aw_buf_a, aw_buf_b)
    z, x, y, p = place()
    core = (z, x, y, 1 - p)
    shifts = (2, 1, 3)
    ys = [(z, x, (y + i) % NY, p) for i in shifts]
    senders = [(y + NY - i) % NY for i in shifts]
    xs = x_peers(z, x, y, p)
    xo = [(q[0], q[1], q[2], 1 - p) for q in xs]
    around = z_peers(z, x, y, p, (4, 3, 5, 2, 6, 1, 7))
    up, down = around[5], around[6]
    target, is_self = swap_of(z, x, y, p)
    arrived = greet([core] + ys + xs + xo + around, (target, is_self))
    c = y * 2 + p
    share = pl.ds(pl.multiple_of(c * ROWS, ROWS), ROWS)

    def half(v, mine):
        low, high = v[:ROWS], v[ROWS:]
        return jnp.where(p == (0 if mine else 1), low, high)

    order = [q[2] for q in ys] + [y]
    m_copies, t_copies, my_copies = [], [], []

    def messages_on(n):
        m_copies[n].wait_recv()
        t = order[n]
        my_src[n] = (m_own[t] + m_buf[t].astype(F32)).astype(BF)
        a = send(my_src.at[n], my_buf.at[n], my_s.at[n], my_r.at[n], *ys[n])
        a.start()
        my_copies.append(a)

    ty_copies = {}

    def transforms_on(n, send_now=True):
        t = order[n]
        t_copies[n].wait_recv()
        for j, q in enumerate(ys):
            yi = q[2]
            ty_src[j, t] = (tq[p, t, yi].astype(F32) + tc_buf[t, yi].astype(F32)).astype(BF)
            if send_now:
                a = send(ty_src.at[j, t], ty_buf.at[j, t], ty_s.at[j, n, 0], ty_r.at[j, n, 0], *q)
                a.start()
                ty_copies[j, n, 0] = a

    def transforms_part(n, r):
        t = order[n]
        for j, q in enumerate(ys):
            a = send(
                ty_src.at[j, t, r], ty_buf.at[j, t, r], ty_s.at[j, n, r], ty_r.at[j, n, r], *q
            )
            a.start()
            ty_copies[j, n, r] = a

    for n, t in enumerate(order):
        rows = pl.ds(pl.multiple_of(t * D, D), D)
        tt = jnp.dot(adj[rows, :], xp[...], preferred_element_type=F32).astype(BF)
        m = jnp.zeros((TILE, D), F32)
        for r in range(REL):
            part = tt[r * TILE : (r + 1) * TILE]
            m = m + jnp.dot(part, weights[r], preferred_element_type=F32)
            for q in range(NY):
                tq[r // 2, t, q, r % 2] = part[:, q * TILE : (q + 1) * TILE]
        m_own[t] = half(m, True)
        m_src[t] = half(m, False).astype(BF)
        if n == 0:
            arrived()
        a = send(m_src.at[t], m_buf.at[t], mc_s.at[n], mc_r.at[n], *core)
        a.start()
        m_copies.append(a)
        if n > 0:
            messages_on(n - 1)
        a = send(tq.at[1 - p, t], tc_buf.at[t], tc_s.at[n], tc_r.at[n], *core)
        a.start()
        t_copies.append(a)


    w_self = weights[REL]
    pre = jnp.dot(states[share, :], w_self, preferred_element_type=F32)
    m_copies[3].wait_recv()
    pre = pre + m_own[y] + m_buf[y].astype(F32)
    for n, a in enumerate(my_copies):
        a.wait_recv()
        pre = pre + my_buf[n].astype(F32)
    sigma = jax.nn.sigmoid(pre)
    slope = (cotangent[share, :].astype(F32) * (sigma * (1.0 + pre * (1.0 - sigma)))).astype(BF)
    slope_s[c] = slope
    mine = slope_s.at[c]
    s_copies = []
    for i, q in enumerate(ys + [core]):
        a = send(mine, mine, s_s.at[i], s_r.at[i], *q)
        a.start()
        s_copies.append(a)
    for n in (0, 1, 2, 3):
        transforms_on(n, False)
        transforms_part(n, 0)
    for n in (0, 1, 2, 3):
        transforms_part(n, 1)
    layer_o[...] = pre * sigma
    g_o[...] = lax.dot_general(slope, w_self, over_columns, preferred_element_type=F32)
    f_copies = []
    for i in (1, 2, 0):
        s_copies[i].wait_recv()
        ref = slope_s.at[senders[i] * 2 + p]
        a = send(ref, ref, f_s.at[i], f_r.at[i], *core)
        a.start()
        f_copies.append(a)
    def transposed(core_of):
        rows = jnp.concatenate([slope_s[t * 2 + core_of] for t in range(NY)], axis=0)
        for r in range(REL):
            part = lax.dot_general(rows, weights[r], over_columns, preferred_element_type=F32)
            part = part.astype(BF)
            for t in range(NY):
                at = pl.multiple_of(t * D + r * TILE + core_of * ROWS, ROWS)
                zs[pl.ds(at, ROWS), :] = part[t * ROWS : (t + 1) * ROWS]

    transposed(p)
    s_copies[3].wait_recv()
    for a in f_copies:
        a.wait_recv()
    transposed(1 - p)
    whole = slope_s[...].reshape(D, D)

    def gradients(k):
        columns = pl.ds(pl.multiple_of(k * D, D), D)
        part = lax.dot_general(adj[:, columns], zs[...], over_rows, preferred_element_type=F32)
        part = part.astype(BF)
        for b in range(4):
            for h in range(2):
                row = b * TILE + h * ROWS
                g_in[2 * k + h, b] = part[row : row + ROWS]

    g_copies = {}
    hops = {(d, i): 4 if (i < 2) == (d == 0) else 3 for d in range(2) for i in range(NX)}

    def chain(s, only=(3, 4)):
        for i in range(NX):
            xi = (x + i) % NX
            for d, q in ((0, up), (1, down)):
                left = hops[d, i] - s
                if left <= 0 or hops[d, i] not in only:
                    continue
                zd = (z + left) % NZ if d == 0 else (z - left + NZ) % NZ
                if s == 0:
                    src = g_in.at[zd, xi, pl.ds(0, HA)]
                else:
                    g_copies[d, s - 1, i].wait_recv()
                    g_src[d, s - 1, i] = (
                        g_in[zd, xi, :HA].astype(F32) + g_buf[d, s - 1, i].astype(F32)
                    ).astype(BF)
                    src = g_src.at[d, s - 1, i]
                a = send(src, g_buf.at[d, s, i], g_s.at[d, s, i], g_r.at[d, s, i], *q)
                a.start()
                g_copies[d, s, i] = a

    bx_copies = {}

    def across(n):
        k = near[n]
        two = pl.ds(2 * k, 2)
        for j, q in enumerate(xs):
            a = send(
                g_in.at[two, q[1], pl.ds(HA, HB)], bx_buf.at[j, two], bx_s.at[j, n], bx_r.at[j, n], *q
            )
            a.start()
            bx_copies[j, n] = a

    def across_wait(n):
        for j in range(3):
            bx_copies[j, n].wait_recv()

    gb_copies = {}

    def x_sum(zd):
        total = g_in[zd, x, HA:].astype(F32)
        for j in range(3):
            total = total + bx_buf[j, zd].astype(F32)
        return total

    def second(i):
        zd = (z + i) % NZ
        gb_src[i] = x_sum(zd).astype(BF)
        a = send(gb_src.at[i], gb_buf.at[i], gb_s.at[i], gb_r.at[i], zd, x, y, p)
        a.start()
        gb_copies[i] = a

    pair = z // 2
    odd = 2 * (z % 2)
    near = ((pair + 2) % 4, (pair + 1 + odd) % 4, (pair + 3 + odd) % 4, pair)
    columns = pl.ds(pl.multiple_of(y * TILE, TILE), TILE)
    xw_copies, zw_copies, aw_copies, w_copies = [[], []], [[], []], [[], []], []

    def weight_part(r):
        for (j, n, q), a in ty_copies.items():
            if q == r:
                a.wait_recv()
        for t in range(NY):
            total = tq[p, t, y, r].astype(F32) + tc_buf[t, y, r].astype(F32)
            for j in range(3):
                total = total + ty_buf[j, t, r].astype(F32)
            tg[r, t * TILE : (t + 1) * TILE, :] = total.astype(BF)
        part = lax.dot_general(tg[r], whole, over_rows, preferred_element_type=F32)
        rows_of = [half(part, True), half(part, False)]
        if r == 1:
            part = lax.dot_general(states[:, columns], whole, over_rows, preferred_element_type=F32)
            rows_of.insert(1, half(part, True))
        for m, v in enumerate(rows_of):
            for q in range(NX):
                gw[r][q, m * ROWS : (m + 1) * ROWS, :] = v[:, q * WC : (q + 1) * WC]
        for i in range(3):
            xw_src[r][i] = gw[r][xs[i][1]].astype(BF)
            a = send(xw_src[r].at[i], xw_buf[r].at[i], xw_s.at[r, i], xw_r.at[r, i], *xs[i])
            a.start()
            xw_copies[r].append(a)

    def weight_x(r):
        total = gw[r][x]
        for i, a in enumerate(xw_copies[r]):
            a.wait_recv()
            total = total + xw_buf[r][i].astype(F32)
        total = total.reshape(NZ, PART[r] // NZ, WC)
        if EIGHTH[r] > PART[r] // NZ:
            padding = jnp.zeros((NZ, EIGHTH[r] - PART[r] // NZ, WC), F32)
            total = jnp.concatenate([total, padding], axis=1)
        zw_src[r][...] = total.astype(BF)
        for i, q in enumerate(around):
            a = send(zw_src[r].at[q[0]], zw_buf[r].at[i], zw_s.at[r, i], zw_r.at[r, i], *q)
            a.start()
            zw_copies[r].append(a)

    def weight_z(r):
        total = zw_src[r][z].astype(F32)
        for i, a in enumerate(zw_copies[r]):
            a.wait_recv()
            total = total + zw_buf[r][i].astype(F32)
        aw_buf[r][z] = total.astype(BF)
        for i, q in enumerate(around):
            a = send(aw_buf[r].at[z], aw_buf[r].at[z], aw_s.at[r, i], aw_r.at[r, i], *q)
            a.start()
            aw_copies[r].append(a)

    def weight_out(r):
        for a in aw_copies[r]:
            a.wait_recv()
        done = aw_buf[r][...].astype(F32)[:, : PART[r] // NZ].reshape(PART[r], WC).astype(BF)
        mine, other = pl.ds(r * ROWS, (r + 1) * ROWS), pl.ds(r * ROWS, ROWS)
        wa[x, mine, :] = done[: (r + 1) * ROWS]
        wb_src[other, :] = done[(r + 1) * ROWS :]
        for i, q in enumerate(xs):
            ref = wa.at[x, mine]
            w_copies.append(send(ref, ref, wa_s.at[r, i], wa_r.at[r, i], *q))
        for i, q in enumerate(xo + [core]):
            w_copies.append(
                send(wb_src.at[other], wb.at[x, other], wb_s.at[r, i], wb_r.at[r, i], *q)
            )
        for a in w_copies[-7:]:
            a.start()

    gradients(near[0])
    across(0)
    chain(0, (4,))
    gradients(near[1])
    across(1)
    chain(0, (3,))
    weight_part(0)
    gradients(near[2])
    across(2)
    chain(1)
    weight_part(1)
    gradients(near[3])
    across(3)
    weight_x(0)
    chain(2)
    across_wait(0)
    across_wait(1)
    for i in (4, 3, 5):
        second(i)
    weight_z(0)
    weight_x(1)
    chain(3)
    across_wait(2)
    for i in (2, 6):
        second(i)
    weight_out(0)
    weight_z(1)
    across_wait(3)
    for i in (1, 7):
        second(i)

    gx_copies = []
    own = None
    for i in (1, 2, 3, 0):
        xi = (x + i) % NX
        part = g_in[z, xi, :HA].astype(F32)
        for d in range(2):
            last = hops[d, i] - 1
            g_copies[d, last, i].wait_recv()
            part = part + g_buf[d, last, i].astype(F32)
        if i:
            gx_src[i - 1] = part.astype(BF)
            a = send(gx_src.at[i - 1], gx_buf.at[i - 1], gx_s.at[i - 1], gx_r.at[i - 1], *xs[i - 1])
            a.start()
            gx_copies.append(a)
        else:
            own = part

    weight_out(1)
    total = x_sum(z)
    for i, a in gb_copies.items():
        a.wait_recv()
        total = total + gb_buf[i].astype(F32)
    v_src[HA:] = total.astype(BF)
    for i, a in enumerate(gx_copies):
        a.wait_recv()
        own = own + gx_buf[i].astype(F32)
    v_src[:HA] = own.astype(BF)

    @pl.when(jnp.logical_not(is_self))
    def _():
        a = send(v_src, v_buf, v_s, v_r, *target)
        a.start()
        a.wait()

    @pl.when(is_self)
    def _():
        v_buf[...] = v_src[...]

    g_o[...] = g_o[...] + v_buf[...].astype(F32)
    for a in w_copies:
        a.wait()
    for a in m_copies + t_copies + my_copies + s_copies + f_copies:
        a.wait_send()
    for copies in xw_copies + zw_copies + aw_copies + [gx_copies]:
        for a in copies:
            a.wait_send()
    for some in (ty_copies, g_copies, bx_copies, gb_copies):
        for a in some.values():
            a.wait_send()


def main(adj, xp, weights, states, cotangent):
    return pl.pallas_call(
        main_kernel,
        out_shape=(
            jax.ShapeDtypeStruct((ROWS, D), F32),
            jax.ShapeDtypeStruct((ROWS, D), F32),
            jax.ShapeDtypeStruct((NX, 3 * ROWS, WC), BF),
            jax.ShapeDtypeStruct((NX, 2 * ROWS, WC), BF),
        ),
        in_specs=[VM] * 5,
        out_specs=(VM,) * 4,
        scratch_shapes=[
            pltpu.VMEM((2, NY, NY, 2, TILE, TILE), BF),
            pltpu.VMEM((NY, NY, 2, TILE, TILE), BF),
            pltpu.VMEM((3, NY, 2, TILE, TILE), BF),
            pltpu.VMEM((3, NY, 2, TILE, TILE), BF),
            pltpu.VMEM((2, D, TILE), BF),
            pltpu.VMEM((NY, ROWS, D), F32),
            pltpu.VMEM((NY, ROWS, D), BF),
            pltpu.VMEM((NY, ROWS, D), BF),
            pltpu.VMEM((3, ROWS, D), BF),
            pltpu.VMEM((3, ROWS, D), BF),
            pltpu.VMEM((NC, ROWS, D), BF),
            pltpu.VMEM((NY * D, D), BF),
            *(
                v
                for r in range(2)
                for v in (
                    pltpu.VMEM((NX, PART[r], WC), F32),
                    pltpu.VMEM((3, PART[r], WC), BF),
                    pltpu.VMEM((3, PART[r], WC), BF),
                    pltpu.VMEM((NZ, EIGHTH[r], WC), BF),
                    pltpu.VMEM((7, EIGHTH[r], WC), BF),
                    pltpu.VMEM((NZ, EIGHTH[r], WC), BF),
                )
            ),
            pltpu.VMEM((2 * ROWS, WC), BF),
            pltpu.VMEM((NZ, NX, ROWS, D), BF),
            pltpu.VMEM((2, 3, NX, HA, D), BF),
            pltpu.VMEM((2, 4, NX, HA, D), BF),
            pltpu.VMEM((3, HA, D), BF),
            pltpu.VMEM((3, HA, D), BF),
            pltpu.VMEM((3, NZ, HB, D), BF),
            pltpu.VMEM((NZ, HB, D), BF),
            pltpu.VMEM((NZ, HB, D), BF),
            pltpu.VMEM((ROWS, D), BF),
            pltpu.VMEM((ROWS, D), BF),
            DMA((4,)), DMA((4,)), DMA((3, 4, 2)), DMA((3, 4, 2)), DMA((4,)), DMA((4,)), DMA((3,)), DMA((3,)),
            DMA((4,)), DMA((4,)), DMA((3,)), DMA((3,)),
            DMA((2, 3)), DMA((2, 3)), DMA((2, 7)), DMA((2, 7)), DMA((2, 7)), DMA((2, 7)),
            DMA((2, 3)), DMA((2, 3)), DMA((2, 4)), DMA((2, 4)), DMA((2, 4, 4)), DMA((2, 4, 4)), DMA((3,)), DMA((3,)),
            DMA((3, 4)), DMA((3, 4)), DMA((8,)), DMA((8,)), DMA(()), DMA(()),
        ],
        compiler_params=params(32, 1),
    )(adj, xp, weights, states, cotangent)


def close_kernel(layer, g, wa, wb, layer_o, g_o, w_o):
    p = lax.axis_index("replica")
    layer_o[...] = layer[...]
    g_o[...] = g[...]
    for q in range(NX):
        columns = slice(q * WC, (q + 1) * WC)
        for m in range(2):
            a = wa[q, m * ROWS : (m + 1) * ROWS, :].astype(F32)
            b = wb[q, m * ROWS : (m + 1) * ROWS, :].astype(F32)
            w_o[m, :, columns] = jnp.where(p == 0, a, b)
            w_o[2 + m, :, columns] = jnp.where(p == 0, b, a)
        w_o[REL, :, columns] = wa[q, 2 * ROWS :, :].astype(F32)


def close(layer, g, wa, wb):
    return pl.pallas_call(
        close_kernel,
        out_shape=(
            jax.ShapeDtypeStruct((ROWS, D), F32),
            jax.ShapeDtypeStruct((ROWS, D), F32),
            jax.ShapeDtypeStruct((REL + 1, ROWS, D), F32),
        ),
        in_specs=[VM] * 4,
        out_specs=(VM, VM, VM),
        compiler_params=params(8),
    )(layer, g, wa, wb)


def shards(
    states,
    weights,
    edge_tiles,
    edge_owner,
    edge_source,
    edge_target,
    edge_relation,
    edge_count,
    cotangent,
):
    groups = edge_owner.shape[0]
    owner = edge_owner.reshape(groups, EB)
    source = edge_source.reshape(groups, EB)
    target = edge_target.reshape(groups, EB)
    relation = edge_relation.reshape(groups, EB)
    count = edge_count.reshape(1, groups)
    tiles = edge_tiles.reshape(EB, TILE, TILE)
    given = (owner, source, target, relation, count, tiles, states, weights)
    given = (pltpu.with_memory_space_constraint(v, pltpu.HBM) for v in given)
    tiles, meta, xp, full, zeros = deal(*given)
    adj = adjacency(meta, tiles, zeros)
    layer, g, wa, wb = main(adj, xp.reshape(-1, D), full, states, cotangent)
    return close(layer, g, wa, wb)


def solution(mesh):
    return jax.shard_map(
        shards,
        mesh=mesh,
        in_specs=(
            P("graph", None),
            P(None, "fsdp", None),
            P("graph", "fsdp", "replica", None, None, None),
            P(None, "fsdp", "replica", None),
            P(None, "fsdp", "replica", None),
            P(None, "fsdp", "replica", None),
            P(None, "fsdp", "replica", None),
            P(None, "fsdp", "replica"),
            P("graph", None),
        ),
        out_specs=(
            P(("graph", "fsdp", "replica"), None),
            P(("graph", "fsdp", "replica"), None),
            P(None, ("fsdp", "replica"), None),
        ),
        check_vma=False,
    )
```
